256 devices in a mesh: blk: 64 (over y, x_lo, z), rep: 4 (over x_hi, core).
Axes of the slice: x: 4 (x_hi: 2, x_lo: 2; x = x_hi * 2 + x_lo), y: 4, z: 8, core: 2. Of those that a mesh axis runs over, the one named last changes fastest.
Arguments:
- image_feats: bfloat16 [131072, 1152], P(('blk', 'rep')), may hold values from -16 to 16, as said below
- text_feats: bfloat16 [131072, 1152], P(('blk', 'rep')), may hold values from -16 to 16, as said below
- head: bfloat16 [1152, 1152], replicated, may hold values from -0.1875 to 0.1875
- image_ids: int32 [131072], P(('blk', 'rep')), may hold values from 0 to 2047
- text_ids: int32 [131072], P(('blk', 'rep')), may hold values from 0 to 2047
- log_scale: float32 [1], replicated, may hold values from 3 to 3.7
- bias: float32 [1], replicated, may hold values from -3 to -1
Outputs:
- grad_image_feats: bfloat16 [131072, 1152], P(('blk', 'rep'))
- grad_text_feats: bfloat16 [131072, 1152], P(('blk', 'rep'))
- grad_head: float32 [1152, 1152], P('blk')
The draws below stay inside these ranges and needn't reach their ends.
Inputs may be any that keep to these rules, and one draw needn't show every extreme that they name: `image_feats`: row magnitudes differ from row to row. `text_feats`: row magnitudes differ from row to row.
All inputs are finite; a program needn't handle non-finite values.
Results may differ from the reference program's by a relative error of at most 0.0072.
Values may be sent and summed in bfloat16 or wider, within the bound.
No kernel may reach another device: no remote copies, remote signals or barrier semaphores. Data moves between devices by JAX's collectives and lax.ppermute only.
A program may use at most 128 MiB of HBM per device.

```python
import jax
import jax.numpy as jnp
from jax import lax

D = 1152
TOK_DEV = 512
HOPS = 4
NIMG = 131072
ID_RANGE = 2048
N_BLK = 64
N_REP = 4


def rough_rows(key):
    noise_key, scale_key = jax.random.split(key, 2)
    row_scale = jnp.exp(jax.random.uniform(scale_key, (NIMG, 1), jnp.float32, jnp.log(0.3), jnp.log(3.0)))
    values = jnp.clip(jax.random.normal(noise_key, (NIMG, D), jnp.float32), -4.0, 4.0)
    return (values * row_scale).astype(jnp.bfloat16)


def draw_image_feats(key, part):
    key = jax.random.fold_in(key, 11)
    return rough_rows(key)


def draw_text_feats(key, part):
    key = jax.random.fold_in(key, 23)
    return rough_rows(key)


def touch_ends(entries, rng, least, largest):
    extent = entries.shape
    index_at = [jax.random.randint(jax.random.fold_in(rng, axis), (), 0, extent[axis]) for axis in range(len(extent))]
    entries = entries.at[tuple(index_at)].set(least)
    longest = extent.index(max(extent))
    index_at[longest] = (index_at[longest] + 1) % extent[longest]
    return entries.at[tuple(index_at)].set(largest)


def noise(rng, dims, scale, reach, held_as=jnp.bfloat16):
    values = scale * jax.random.normal(rng, dims, jnp.float32)
    return jnp.clip(values, min=-reach, max=reach).astype(held_as)


def setup_inputs(seed: int = 0) -> dict:
    splits = jax.random.split(jax.random.key(seed), 8)
    return {
        "image_feats": draw_image_feats(jax.random.fold_in(splits[7], 71), 0),
        "text_feats": draw_text_feats(jax.random.fold_in(splits[7], 71), 0),
        "head": noise(splits[2], (D, D), D ** -0.5, 0.1875),
        "image_ids": touch_ends(jax.random.randint(splits[3], (NIMG,), 0, ID_RANGE), jax.random.fold_in(splits[3], 1), 0, ID_RANGE - 1).astype(jnp.int32),
        "text_ids": touch_ends(jax.random.randint(splits[4], (NIMG,), 0, ID_RANGE), jax.random.fold_in(splits[4], 1), 0, ID_RANGE - 1).astype(jnp.int32),
        "log_scale": jnp.clip(jax.random.uniform(splits[5], (1,), jnp.float32, 3.0, 3.7), 3.0, 3.7),
        "bias": jnp.clip(jax.random.uniform(splits[6], (1,), jnp.float32, -3.0, -1.0), -3.0, -1.0),
    }


def unit_rows(values):
    inverse = lax.rsqrt(lax.optimization_barrier(jnp.sum(values * values, axis=-1, keepdims=True)) + 1e-06)
    return (values * inverse, inverse)

def reference(image_feats, text_feats, head, image_ids, text_ids, log_scale, bias):
    u_full = jnp.dot(image_feats, head, preferred_element_type=jnp.float32)
    x_full, inv_u = unit_rows(u_full)
    x_half = x_full.astype(jnp.bfloat16)
    y_full, inv_t = unit_rows(text_feats.astype(jnp.float32))
    y_half = y_full.astype(jnp.bfloat16)
    scale = jnp.exp(log_scale[0])
    shape4 = (N_BLK, N_REP, TOK_DEV, D)
    xb = x_half.reshape(shape4).astype(jnp.float32)
    yb = y_half.reshape(shape4)
    img_ids = image_ids.reshape(N_BLK, N_REP, TOK_DEV)
    txt_ids = text_ids.reshape(N_BLK, N_REP, TOK_DEV)
    grad_x = jnp.zeros(shape4, jnp.float32)
    grad_y = jnp.zeros(shape4, jnp.float32)
    for step in range(HOPS + 1):
        cycle_text = jnp.roll(yb, step, axis=0).astype(jnp.float32)
        cycle_ids = jnp.roll(txt_ids, step, axis=0)
        logits = scale * jnp.einsum('brid,brjd->brij', xb, cycle_text) + bias[0]
        positive = (img_ids[:, :, :, None] == cycle_ids[:, :, None, :]).astype(jnp.float32)
        coef = (scale * (jax.nn.sigmoid(logits) - positive)).astype(jnp.bfloat16).astype(jnp.float32)
        grad_x = grad_x + jnp.einsum('brij,brjd->brid', coef, cycle_text)
        part_y = jnp.einsum('brij,brid->brjd', coef, xb)
        grad_y = grad_y + jnp.roll(part_y, -step, axis=0)
    grad_x = grad_x.reshape(NIMG, D)
    grad_y = grad_y.reshape(NIMG, D)
    grad_u = (inv_u * (grad_x - x_full * lax.optimization_barrier(jnp.sum(x_full * grad_x, axis=1, keepdims=True)))).astype(jnp.bfloat16)
    grad_image = jnp.dot(grad_u, head.T, preferred_element_type=jnp.float32).astype(jnp.bfloat16)
    grad_head = jnp.dot(image_feats.T, grad_u, preferred_element_type=jnp.float32) / (N_BLK * N_REP)
    grad_text = (inv_t * (grad_y - y_full * lax.optimization_barrier(jnp.sum(y_full * grad_y, axis=1, keepdims=True)))).astype(jnp.bfloat16)
    return (grad_image, grad_text, grad_head)
```

```python
import jax
import jax.numpy as jnp
from jax import lax
from jax.sharding import Mesh, PartitionSpec as P

HOPS = 4
AXES = ("y", "xl", "z", "xh", "c")
CYCLE = ("y", "xl", "z")
F32 = jnp.float32
BF16 = jnp.bfloat16


def shifted(value, steps):
    count = lax.axis_size(CYCLE)
    return lax.ppermute(value, CYCLE, [(i, (i + steps) % count) for i in range(count)])


def unit_rows(values):
    inverse = lax.rsqrt(jnp.sum(values * values, axis=-1, keepdims=True) + 1e-06)
    return values * inverse, inverse


def tn(a, b):
    return lax.dot_general(a, b, (((0,), (0,)), ((), ())), preferred_element_type=F32)


def nt(a, b):
    return lax.dot_general(a, b, (((1,), (1,)), ((), ())), preferred_element_type=F32)


def nn(a, b):
    return jnp.dot(a, b, preferred_element_type=F32)


def head_sum(images, grads):
    core = lax.axis_index("c")
    width, part = 640, 384

    def half(which):
        start = 512 * which
        total = 0.0
        for a, g in zip(images, grads):
            total = total + tn(a, lax.dynamic_slice_in_dim(g, start, width, 1))
        return total

    away = half(1 - core).astype(BF16)
    away = lax.ppermute(away, "c", [(0, 1), (1, 0)])
    mine = half(core) + away.astype(F32)
    rows = mine.astype(BF16).reshape(4, 2, 144, width)
    sends = jnp.stack(
        [
            rows[:, i, :, 256 * j : 256 * j + part].reshape(576, part)
            for i in range(2)
            for j in range(2)
        ]
    )
    got = lax.all_to_all(sends, ("xl", "xh"), 0, 0)
    total = jnp.sum(got.astype(F32), axis=0).reshape(4, 144, part)
    total = jnp.sum(lax.all_to_all(total, "y", 0, 0), axis=0)
    total = jnp.sum(lax.all_to_all(total.reshape(8, 18, part), "z", 0, 0), axis=0)
    parts = lax.all_gather(total * (1.0 / 256.0), ("xh", "c"))
    return jnp.concatenate(
        [parts[0], parts[2][:, 128:], parts[1][:, 128:], parts[3][:, 128:]], axis=1
    )


def per_device(image_feats, text_feats, head, image_ids, text_ids, log_scale, bias):
    scale = jnp.exp(log_scale[0])
    offset = bias[0]

    def coefficients(images, image_labels, texts, text_labels):
        logits = scale * nt(images, texts) + offset
        positive = (image_labels[:, None] == text_labels[None, :]).astype(F32)
        return (scale * (jax.nn.sigmoid(logits) - positive)).astype(BF16)

    def images_of(feats):
        full, inverse = unit_rows(nn(feats, head))
        return full, inverse, full.astype(BF16)

    def project(inverse, grad, full):
        return (inverse * (grad - full * jnp.sum(full * grad, axis=1, keepdims=True))).astype(BF16)

    a = [image_feats]
    ai = [image_ids]
    y_full, inv_t = unit_rows(text_feats.astype(F32))
    y = [y_full.astype(BF16)]
    yi = [text_ids]
    for hop in range(HOPS):
        a.append(shifted(a[hop], -1))
        ai.append(shifted(ai[hop], -1))
        y.append(shifted(y[hop], 1))
        yi.append(shifted(yi[hop], 1))
    x_full, inv_u, x_half = images_of(a[0])
    coef = coefficients(x_half, ai[0], y[0], yi[0])
    grad_x = nn(coef, y[0])
    grad_y = tn(coef, x_half)
    images = {}
    grads = []
    for hop in range(1, HOPS + 1):
        coef = coefficients(x_half, ai[0], y[hop], yi[hop])
        grad_x = grad_x + nn(coef, y[hop])
        images[hop] = images_of(a[hop])
        coef = coefficients(images[hop][2], ai[hop], y[0], yi[0])
        grad_y = grad_y + tn(coef, images[hop][2])
        if hop == 2:
            grads.append(project(inv_u, grad_x, x_full))
            for near in (1, 2):
                full, inverse, half = images[near]
                coef = coefficients(half, ai[near], y[2], yi[2])
                grads.append(project(inverse, nn(coef, y[2]), full))
            grad_head = head_sum(a[:3], grads)
    grad_u = project(inv_u, grad_x, x_full)
    grad_image = nt(grad_u, head).astype(BF16)
    grad_text = (
        inv_t * (grad_y - y_full * jnp.sum(y_full * grad_y, axis=1, keepdims=True))
    ).astype(BF16)
    return grad_image, grad_text, grad_head


def solution(mesh):
    fine = Mesh(mesh.devices.reshape(4, 2, 8, 2, 2), AXES)
    placed = (P(AXES, None), P(AXES, None), P(), P(AXES), P(AXES), P(), P())
    return jax.shard_map(
        per_device,
        mesh=fine,
        in_specs=placed,
        out_specs=(P(AXES, None), P(AXES, None), P(CYCLE, None)),
        check_vma=False,
    )
```

```python
import jax
import jax.numpy as jnp
from jax import lax
from jax.experimental import pallas as pl
from jax.experimental.pallas import tpu as pltpu
from jax.sharding import Mesh, PartitionSpec as P

AXES = ("y", "xl", "z", "xh", "c")
CYCLE = ("y", "xl", "z")
F32 = jnp.float32
BF16 = jnp.bfloat16
D = 1152
ROWS = 512
SENT = 528
STEP = 256
WIDE = 640
PART = 384


def shifted(value, steps):
    count = lax.axis_size(CYCLE)
    return lax.ppermute(value, CYCLE, [(i, (i + steps) % count) for i in range(count)])


def after(value, *others):
    return lax.optimization_barrier((value,) + others)[0]


def nn(a, b):
    return jnp.dot(a, b, preferred_element_type=F32)


def nt(a, b):
    return lax.dot_general(a, b, (((1,), (1,)), ((), ())), preferred_element_type=F32)


def run(kernel, outs, *args, scalars=1, aliases=None, vmem=40):
    specs = [pl.BlockSpec(memory_space=pltpu.SMEM)] * scalars
    specs += [pl.BlockSpec(memory_space=pltpu.VMEM)] * (len(args) - scalars)
    return pl.pallas_call(
        kernel,
        out_shape=[jax.ShapeDtypeStruct(s, t) for s, t in outs],
        in_specs=specs,
        out_specs=[pl.BlockSpec(memory_space=pltpu.VMEM)] * len(outs),
        input_output_aliases=aliases or {},
        compiler_params=pltpu.CompilerParams(vmem_limit_bytes=vmem * 2**20),
        cost_estimate=pl.CostEstimate(flops=0, bytes_accessed=0, transcendentals=0),
    )(*args)


def steps(body):
    @pl.loop(0, ROWS // STEP)
    def _(i):
        body(pl.ds(pl.multiple_of(i * STEP, STEP), STEP))


def inverse_norm(values):
    return lax.rsqrt(jnp.sum(values * values, axis=-1, keepdims=True) + 1e-06)


def lane_ids(block):
    pair = block[pl.ds(ROWS, 16), pl.ds(0, ROWS)].astype(F32)
    return pair[0:1] * 256.0 + pair[1:2]


def coef_of(par, rows, row_ids, columns, column_ids):
    scale, offset = par[0], par[1]
    logits = scale * nt(rows, columns) + offset
    positive = (row_ids == column_ids).astype(F32)
    return (scale * (jax.nn.sigmoid(logits) - positive)).astype(BF16)


def unit_images(feats, head, full, inverse, half, feats_t):
    def body(r):
        u = nn(feats[r, :], head[...])
        inv = inverse_norm(u)
        x = u * inv
        half[r, :] = x.astype(BF16)
        if full is not None:
            full[r, :] = x
            inverse[r, :] = inv

    steps(body)
    if feats_t is not None:

        @pl.loop(0, D // 128)
        def _(k):
            cols = pl.ds(pl.multiple_of(k * 128, 128), 128)
            feats_t[cols, :] = feats[pl.ds(0, ROWS), cols].T


def project(inv, grad, x):
    return inv * (grad - x * jnp.sum(x * grad, axis=1, keepdims=True))


def prepare(text, image, text_lane, image_lane, text_out, image_out):
    def body(r):
        t = text[r, :].astype(F32)
        text_out[r, :] = (t * inverse_norm(t)).astype(BF16)
        image_out[r, :] = image[r, :]

    steps(body)
    for lane, out in ((text_lane, text_out), (image_lane, image_out)):
        out[pl.ds(ROWS, 16), :] = jnp.zeros((16, D), BF16)
        row = lax.broadcasted_iota(jnp.int32, (16, ROWS), 0)
        ids = lane[...]
        high, low = (ids >> 8).astype(F32), (ids & 255).astype(F32)
        pair = jnp.where(row == 0, high, jnp.where(row == 1, low, 0.0))
        out[pl.ds(ROWS, 16), pl.ds(0, ROWS)] = pair.astype(BF16)


def first(par, head, a0, y0, iid, tid, full, inv, half, a_t, gx, gy):
    unit_images(a0, head, full, inv, half, a_t)
    t_lane, i_lane = lane_ids(y0), lane_ids(a0)
    text = y0[pl.ds(0, ROWS), :]

    def body(r):
        gx[r, :] = nn(coef_of(par, half[r, :], iid[r, :], text, t_lane), text)
        gy[r, :] = nn(coef_of(par, y0[r, :], tid[r, :], half[...], i_lane), half[...])

    steps(body)


def second(par, head, a1, y1, x0, y0, iid, tid, gx0, gy0, full, inv, half, a_t, gx, gy):
    unit_images(a1, head, full, inv, half, a_t)
    t_lane, i_lane = lane_ids(y1), lane_ids(a1)
    text = y1[pl.ds(0, ROWS), :]

    def body(r):
        gx[r, :] = gx0[r, :] + nn(coef_of(par, x0[r, :], iid[r, :], text, t_lane), text)
        gy[r, :] = gy0[r, :] + nn(
            coef_of(par, y0[r, :], tid[r, :], half[...], i_lane), half[...]
        )

    steps(body)


def third(par, head, a2, y2, x0, f0, v0, x1, f1, v1, iid, ids1, ids2, gx0,
          half, a_t, u0, u1, u2, gx, full, inv):
    unit_images(a2, head, full, inv, half, a_t)
    t_lane = lane_ids(y2)
    text = y2[pl.ds(0, ROWS), :]

    def body(r):
        grad = gx0[r, :] + nn(coef_of(par, x0[r, :], iid[r, :], text, t_lane), text)
        gx[r, :] = grad
        u0[r, :] = project(v0[r, :], grad, f0[r, :]).astype(BF16)
        grad = nn(coef_of(par, x1[r, :], ids1[r, :], text, t_lane), text)
        u1[r, :] = project(v1[r, :], grad, f1[r, :]).astype(BF16)
        grad = nn(coef_of(par, half[r, :], ids2[r, :], text, t_lane), text)
        u2[r, :] = project(inv[r, :], grad, full[r, :]).astype(BF16)

    steps(body)


def head_part(start, a0, a1, a2, u0, u1, u2, out):
    cols = pl.ds(pl.multiple_of(start[0], 128), WIDE)

    @pl.loop(0, D // 384)
    def _(k):
        r = pl.ds(pl.multiple_of(k * 384, 384), 384)
        total = nn(a0[r, :], u0[:, cols])
        total = total + nn(a1[r, :], u1[:, cols])
        total = total + nn(a2[r, :], u2[:, cols])
        out[r, :] = total.astype(out.dtype)


def text_only(par, y0, a2, x2, tid, gy0, gy):
    i_lane = lane_ids(a2)

    def body(r):
        gy[r, :] = gy0[r, :] + nn(coef_of(par, y0[r, :], tid[r, :], x2[...], i_lane), x2[...])

    steps(body)


def to_pieces(mine, away, out):
    @pl.loop(0, 8)
    def _(k):
        r = pl.ds(pl.multiple_of(k * 144, 144), 144)
        total = (mine[r, :] + away[r, :].astype(F32)).astype(BF16)
        out[2 * k] = total[:, :PART]
        out[2 * k + 1] = total[:, 256 : 256 + PART]


def add_pieces(got, out):
    total = got[0].astype(F32)
    for k in range(1, 16):
        total = total + got[k].astype(F32)
    for k in range(8):
        out[k] = total[18 * k : 18 * k + 18]


def add_last(got, out):
    total = got[0]
    for k in range(1, 8):
        total = total + got[k]
    out[...] = total * (1.0 / 256.0)


def fourth(par, head, a3, y3, x0, y0, iid, tid, gx0, gy0, gx, gy, half):
    unit_images(a3, head, None, None, half, None)
    t_lane, i_lane = lane_ids(y3), lane_ids(a3)
    text = y3[pl.ds(0, ROWS), :]

    def body(r):
        gx[r, :] = gx0[r, :] + nn(coef_of(par, x0[r, :], iid[r, :], text, t_lane), text)
        gy[r, :] = gy0[r, :] + nn(
            coef_of(par, y0[r, :], tid[r, :], half[...], i_lane), half[...]
        )

    steps(body)


def last(par, head, a4, y4, x0, y0, iid, tid, gx0, gy0, f0, v0, text_in, g_image, g_text, half):
    unit_images(a4, head, None, None, half, None)
    t_lane, i_lane = lane_ids(y4), lane_ids(a4)
    text = y4[pl.ds(0, ROWS), :]

    def body(r):
        grad = gx0[r, :] + nn(coef_of(par, x0[r, :], iid[r, :], text, t_lane), text)
        grad_u = project(v0[r, :], grad, f0[r, :]).astype(BF16)
        g_image[r, :] = nt(grad_u, head[...]).astype(BF16)
        grad = gy0[r, :] + nn(coef_of(par, y0[r, :], tid[r, :], half[...], i_lane), half[...])
        t = text_in[r, :].astype(F32)
        inv = inverse_norm(t)
        g_text[r, :] = project(inv, grad, t * inv).astype(BF16)

    steps(body)


BLOCK = ((ROWS, D), BF16)
WIDEBLOCK = ((ROWS, D), F32)
COLUMN = ((ROWS, 1), F32)
TURNED = ((D, ROWS), BF16)


def per_device(image_feats, text_feats, head, image_ids, text_ids, log_scale, bias):
    core = lax.axis_index("c")
    par = jnp.stack([jnp.exp(log_scale[0]), bias[0]])
    iid = image_ids.astype(F32).reshape(ROWS, 1)
    tid = text_ids.astype(F32).reshape(ROWS, 1)
    travel = ((SENT, D), BF16)
    y0, a0 = run(
        prepare, [travel, travel], text_feats, image_feats,
        text_ids.reshape(1, ROWS), image_ids.reshape(1, ROWS), scalars=0,
    )
    y1, a1 = shifted(y0, 1), shifted(a0, -1)
    f0, v0, x0, at0, gx, gy = run(
        first, [WIDEBLOCK, COLUMN, BLOCK, TURNED, WIDEBLOCK, WIDEBLOCK],
        par, head, a0, y0, iid, tid,
    )
    y2, a2 = shifted(after(y1, gx), 1), shifted(after(a1, gx), -1)
    f1, v1, x1, at1, gx, gy = run(
        second, [WIDEBLOCK, COLUMN, BLOCK, TURNED, WIDEBLOCK, WIDEBLOCK],
        par, head, a1, y1, x0, y0, iid, tid, gx, gy,
    )
    y3, a3 = shifted(after(y2, gx), 1), shifted(after(a2, gx), -1)

    def column_ids(block):
        pair = block[ROWS : ROWS + 2, :ROWS].astype(F32)
        return (pair[0] * 256.0 + pair[1]).reshape(ROWS, 1)

    x2, at2, u0, u1, u2, gx, _, _ = run(
        third, [BLOCK, TURNED, BLOCK, BLOCK, BLOCK, WIDEBLOCK, WIDEBLOCK, COLUMN],
        par, head, a2, y2, x0, f0, v0, x1, f1, v1, iid, column_ids(a1), column_ids(a2), gx,
    )
    half = ((D, WIDE), BF16)
    (away,) = run(head_part, [half], (512 * (1 - core)).reshape(1), at0, at1, at2, u0, u1, u2)
    got = lax.ppermute(away, "c", [(0, 1), (1, 0)])
    (mine,) = run(
        head_part, [((D, WIDE), F32)],
        after((512 * core).reshape(1), away), at0, at1, at2, u0, u1, u2,
    )
    (gy,) = run(text_only, [WIDEBLOCK], par, y0, a2, x2, tid, after(gy, mine))
    (pieces,) = run(to_pieces, [((16, 144, PART), BF16)], after(mine, gy), got, scalars=0)
    spread = lax.all_to_all(pieces, ("y", "xl", "xh"), 0, 0)
    gx, gy, _ = run(
        fourth, [WIDEBLOCK, WIDEBLOCK, BLOCK],
        par, head, a3, y3, x0, y0, iid, tid, gx, after(gy, pieces),
    )
    y4, a4 = shifted(after(y3, mine), 1), shifted(after(a3, mine), -1)
    (total,) = run(add_pieces, [((8, 18, PART), F32)], after(spread, gx), scalars=0)
    spread = lax.all_to_all(total, "z", 0, 0)
    (total,) = run(add_last, [((18, PART), F32)], spread, scalars=0)
    parts = lax.all_gather(total, ("xh", "c"))
    grad_head = jnp.concatenate(
        [parts[0], parts[2][:, 128:], parts[1][:, 128:], parts[3][:, 128:]], axis=1
    )
    grad_image, grad_text, _ = run(
        last, [BLOCK, BLOCK, BLOCK],
        par, head, a4, y4, x0, y0, iid, tid, gx, after(gy, total), f0, v0, text_feats,
    )
    return grad_image, grad_text, grad_head


def solution(mesh):
    fine = Mesh(mesh.devices.reshape(4, 2, 8, 2, 2), AXES)
    placed = (P(AXES, None), P(AXES, None), P(), P(AXES), P(AXES), P(), P())
    return jax.shard_map(
        per_device,
        mesh=fine,
        in_specs=placed,
        out_specs=(P(AXES, None), P(AXES, None), P(CYCLE, None)),
        check_vma=False,
    )
```

```python
import jax
import jax.numpy as jnp
from jax import lax
from jax.experimental import pallas as pl
from jax.experimental.pallas import tpu as pltpu
from jax.sharding import Mesh, PartitionSpec as P

AXES = ("y", "xl", "z", "xh", "c")
CYCLE = ("y", "xl", "z")
F32 = jnp.float32
BF16 = jnp.bfloat16
D = 1152
ROWS = 512
SENT = 528
STEP = 256
WIDE = 640
PART = 384


def shifted(value, steps):
    count = lax.axis_size(CYCLE)
    return lax.ppermute(value, CYCLE, [(i, (i + steps) % count) for i in range(count)])


def after(value, *others):
    return lax.optimization_barrier((value,) + others)[0]


def nn(a, b):
    return jnp.dot(a, b, preferred_element_type=F32)


def nt(a, b):
    return lax.dot_general(a, b, (((1,), (1,)), ((), ())), preferred_element_type=F32)


def run(kernel, outs, *args, scalars=1, aliases=None, vmem=14, flops=0):
    specs = [pl.BlockSpec(memory_space=pltpu.SMEM)] * scalars
    specs += [pl.BlockSpec(memory_space=pltpu.VMEM)] * (len(args) - scalars)
    return pl.pallas_call(
        kernel,
        out_shape=[jax.ShapeDtypeStruct(s, t) for s, t in outs],
        in_specs=specs,
        out_specs=[pl.BlockSpec(memory_space=pltpu.VMEM)] * len(outs),
        input_output_aliases=aliases or {},
        compiler_params=pltpu.CompilerParams(vmem_limit_bytes=vmem * 2**20),
        cost_estimate=pl.CostEstimate(flops=flops, bytes_accessed=0, transcendentals=0),
    )(*args)


def steps(body):
    @pl.loop(0, ROWS // STEP)
    def _(i):
        body(pl.ds(pl.multiple_of(i * STEP, STEP), STEP))


def inverse_norm(values):
    return lax.rsqrt(jnp.sum(values * values, axis=-1, keepdims=True) + 1e-06)


def lane_ids(block):
    pair = block[pl.ds(ROWS, 16), pl.ds(0, ROWS)].astype(F32)
    return pair[0:1] * 256.0 + pair[1:2]


def coef_of(par, rows, row_ids, columns, column_ids):
    scale, offset = par[0], par[1]
    logits = scale * nt(rows, columns) + offset
    positive = (row_ids == column_ids).astype(F32)
    return (scale * (jax.nn.sigmoid(logits) - positive)).astype(BF16)


def unit_images(feats, head, full, inverse, half, feats_t):
    def body(r):
        u = nn(feats[r, :], head[...])
        inv = inverse_norm(u)
        x = u * inv
        half[r, :] = x.astype(BF16)
        if full is not None:
            full[r, :] = x
            inverse[r, :] = inv

    steps(body)
    if feats_t is not None:

        @pl.loop(0, D // 128)
        def _(k):
            cols = pl.ds(pl.multiple_of(k * 128, 128), 128)
            feats_t[cols, :] = feats[pl.ds(0, ROWS), cols].T


def project(inv, grad, x):
    return inv * (grad - x * jnp.sum(x * grad, axis=1, keepdims=True))


def prepare(text, image, text_lane, image_lane, text_out, image_out):
    def body(r):
        t = text[r, :].astype(F32)
        text_out[r, :] = (t * inverse_norm(t)).astype(BF16)
        image_out[r, :] = image[r, :]

    steps(body)
    for lane, out in ((text_lane, text_out), (image_lane, image_out)):
        out[pl.ds(ROWS, 16), :] = jnp.zeros((16, D), BF16)
        row = lax.broadcasted_iota(jnp.int32, (16, ROWS), 0)
        ids = lane[...]
        high, low = (ids >> 8).astype(F32), (ids & 255).astype(F32)
        pair = jnp.where(row == 0, high, jnp.where(row == 1, low, 0.0))
        out[pl.ds(ROWS, 16), pl.ds(0, ROWS)] = pair.astype(BF16)


def first(par, head, a0, y0, iid, tid, full, inv, half, a_t, gx, gy):
    unit_images(a0, head, full, inv, half, a_t)
    t_lane, i_lane = lane_ids(y0), lane_ids(a0)
    text = y0[pl.ds(0, ROWS), :]

    def body(r):
        gx[r, :] = nn(coef_of(par, half[r, :], iid[r, :], text, t_lane), text)
        gy[r, :] = nn(coef_of(par, y0[r, :], tid[r, :], half[...], i_lane), half[...])

    steps(body)


def second(par, head, a1, y1, x0, y0, iid, tid, gx0, gy0, full, inv, half, a_t, gx, gy):
    unit_images(a1, head, full, inv, half, a_t)
    t_lane, i_lane = lane_ids(y1), lane_ids(a1)
    text = y1[pl.ds(0, ROWS), :]

    def body(r):
        gx[r, :] = gx0[r, :] + nn(coef_of(par, x0[r, :], iid[r, :], text, t_lane), text)
        gy[r, :] = gy0[r, :] + nn(
            coef_of(par, y0[r, :], tid[r, :], half[...], i_lane), half[...]
        )

    steps(body)


def third(par, head, a2, y2, x0, f0, v0, x1, f1, v1, iid, ids1, ids2, gx0,
          half, a_t, u0, u1, u2, gx, full, inv):
    unit_images(a2, head, full, inv, half, a_t)
    t_lane = lane_ids(y2)
    text = y2[pl.ds(0, ROWS), :]

    def body(r):
        grad = gx0[r, :] + nn(coef_of(par, x0[r, :], iid[r, :], text, t_lane), text)
        gx[r, :] = grad
        u0[r, :] = project(v0[r, :], grad, f0[r, :]).astype(BF16)
        grad = nn(coef_of(par, x1[r, :], ids1[r, :], text, t_lane), text)
        u1[r, :] = project(v1[r, :], grad, f1[r, :]).astype(BF16)
        grad = nn(coef_of(par, half[r, :], ids2[r, :], text, t_lane), text)
        u2[r, :] = project(inv[r, :], grad, full[r, :]).astype(BF16)

    steps(body)


def head_part(start, a0, a1, a2, u0, u1, u2, *outs):
    cols = pl.ds(pl.multiple_of(start[0], 128), WIDE)

    for i, out in enumerate(outs):

        @pl.loop(0, D // 288 // len(outs))
        def _(k):
            at = pl.multiple_of(k * 288, 288)
            s = pl.ds(at, 288)
            r = pl.ds(at + D // len(outs) * i, 288)
            total = nn(a0[r, :], u0[:, cols])
            total = total + nn(a1[r, :], u1[:, cols])
            total = total + nn(a2[r, :], u2[:, cols])
            out[s, :] = total.astype(out.dtype)


def text_only(par, y0, a2, x2, tid, gy0, gy):
    i_lane = lane_ids(a2)

    def body(r):
        gy[r, :] = gy0[r, :] + nn(coef_of(par, y0[r, :], tid[r, :], x2[...], i_lane), x2[...])

    steps(body)


def to_pieces(mine, low, high, out):
    @pl.loop(0, 4)
    def _(k):
        r = pl.ds(pl.multiple_of(k * 144, 144), 144)
        total = (mine[r, :] + low[r, :].astype(F32)).astype(BF16)
        out[2 * k] = total[:, :PART]
        out[2 * k + 1] = total[:, 256 : 256 + PART]

    @pl.loop(4, 8)
    def _(k):
        r = pl.ds(pl.multiple_of(k * 144, 144), 144)
        s = pl.ds(pl.multiple_of((k - 4) * 144, 144), 144)
        total = (mine[r, :] + high[s, :].astype(F32)).astype(BF16)
        out[2 * k] = total[:, :PART]
        out[2 * k + 1] = total[:, 256 : 256 + PART]


def add_pieces(got, out):
    total = got[0].astype(F32)
    for k in range(1, 16):
        total = total + got[k].astype(F32)
    for k in range(8):
        out[k] = total[18 * k : 18 * k + 18]


def add_last(got, out):
    total = got[0]
    for k in range(1, 8):
        total = total + got[k]
    out[...] = total * (1.0 / 256.0)


def fourth(par, head, a3, y3, x0, y0, iid, tid, gx0, gy0, gx, gy, half):
    unit_images(a3, head, None, None, half, None)
    t_lane, i_lane = lane_ids(y3), lane_ids(a3)
    text = y3[pl.ds(0, ROWS), :]

    def body(r):
        gx[r, :] = gx0[r, :] + nn(coef_of(par, x0[r, :], iid[r, :], text, t_lane), text)
        gy[r, :] = gy0[r, :] + nn(
            coef_of(par, y0[r, :], tid[r, :], half[...], i_lane), half[...]
        )

    steps(body)


def last(par, head, a4, y4, x0, y0, iid, tid, gx0, gy0, f0, v0, text_in, g_image, g_text, half):
    unit_images(a4, head, None, None, half, None)
    t_lane, i_lane = lane_ids(y4), lane_ids(a4)
    text = y4[pl.ds(0, ROWS), :]

    def body(r):
        grad = gx0[r, :] + nn(coef_of(par, x0[r, :], iid[r, :], text, t_lane), text)
        grad_u = project(v0[r, :], grad, f0[r, :]).astype(BF16)
        g_image[r, :] = nt(grad_u, head[...]).astype(BF16)
        grad = gy0[r, :] + nn(coef_of(par, y0[r, :], tid[r, :], half[...], i_lane), half[...])
        t = text_in[r, :].astype(F32)
        inv = inverse_norm(t)
        g_text[r, :] = project(inv, grad, t * inv).astype(BF16)

    steps(body)


BLOCK = ((ROWS, D), BF16)
WIDEBLOCK = ((ROWS, D), F32)
COLUMN = ((ROWS, 1), F32)
TURNED = ((D, ROWS), BF16)


def per_device(image_feats, text_feats, head, image_ids, text_ids, log_scale, bias):
    core = lax.axis_index("c")
    par = jnp.stack([jnp.exp(log_scale[0]), bias[0]])
    iid = image_ids.astype(F32).reshape(ROWS, 1)
    tid = text_ids.astype(F32).reshape(ROWS, 1)
    travel = ((SENT, D), BF16)
    y0, a0 = run(
        prepare, [travel, travel], text_feats, image_feats,
        text_ids.reshape(1, ROWS), image_ids.reshape(1, ROWS), scalars=0,
    )
    y1, a1 = shifted(y0, 1), shifted(a0, -1)
    f0, v0, x0, at0, gx, gy = run(
        first, [WIDEBLOCK, COLUMN, BLOCK, TURNED, WIDEBLOCK, WIDEBLOCK],
        par, head, a0, y0, iid, tid,
    )
    y2, a2 = shifted(after(y1, gx), 1), shifted(after(a1, gx), -1)
    f1, v1, x1, at1, gx, gy = run(
        second, [WIDEBLOCK, COLUMN, BLOCK, TURNED, WIDEBLOCK, WIDEBLOCK],
        par, head, a1, y1, x0, y0, iid, tid, gx, gy,
    )
    y3, a3 = shifted(after(y2, gx), 1), shifted(after(a2, gx), -1)

    def column_ids(block):
        pair = block[ROWS : ROWS + 2, :ROWS].astype(F32)
        return (pair[0] * 256.0 + pair[1]).reshape(ROWS, 1)

    x2, at2, u0, u1, u2, gx, _, _ = run(
        third, [BLOCK, TURNED, BLOCK, BLOCK, BLOCK, WIDEBLOCK, WIDEBLOCK, COLUMN],
        par, head, a2, y2, x0, f0, v0, x1, f1, v1, iid, column_ids(a1), column_ids(a2), gx,
    )
    half = ((D // 2, WIDE), BF16)
    away = run(head_part, [half, half], (512 * (1 - core)).reshape(1), at0, at1, at2, u0, u1, u2)
    got = [lax.ppermute(part, "c", [(0, 1), (1, 0)]) for part in away]
    (mine,) = run(
        head_part, [((D, WIDE), F32)],
        after((512 * core).reshape(1), *away), at0, at1, at2, u0, u1, u2,
    )
    (gy,) = run(text_only, [WIDEBLOCK], par, y0, a2, x2, tid, after(gy, mine))
    (pieces,) = run(to_pieces, [((16, 144, PART), BF16)], after(mine, gy), *got, scalars=0)
    spread = lax.all_to_all(pieces, ("y", "xl", "xh"), 0, 0)
    gx, gy, _ = run(
        fourth, [WIDEBLOCK, WIDEBLOCK, BLOCK],
        par, head, a3, y3, x0, y0, iid, tid, gx, after(gy, pieces), flops=10**11,
    )
    y4, a4 = shifted(after(y3, mine), 1), shifted(after(a3, mine), -1)
    (total,) = run(add_pieces, [((8, 18, PART), F32)], after(spread, gx), scalars=0)
    spread = lax.all_to_all(total, "z", 0, 0)
    (total,) = run(add_last, [((18, PART), F32)], spread, scalars=0)
    parts = lax.all_gather(total, ("xh", "c"))
    grad_head = jnp.concatenate(
        [parts[0], parts[2][:, 128:], parts[1][:, 128:], parts[3][:, 128:]], axis=1
    )
    grad_image, grad_text, _ = run(
        last, [BLOCK, BLOCK, BLOCK],
        par, head, a4, y4, x0, y0, iid, tid, gx, after(gy, total), f0, v0, text_feats,
    )
    return grad_image, grad_text, grad_head


def solution(mesh):
    fine = Mesh(mesh.devices.reshape(4, 2, 8, 2, 2), AXES)
    placed = (P(AXES, None), P(AXES, None), P(), P(AXES), P(AXES), P(), P())
    return jax.shard_map(
        per_device,
        mesh=fine,
        in_specs=placed,
        out_specs=(P(AXES, None), P(AXES, None), P(CYCLE, None)),
        check_vma=False,
    )
```

```python
import jax
import jax.numpy as jnp
from jax import lax
from jax.experimental import pallas as pl
from jax.experimental.pallas import tpu as pltpu
from jax.sharding import Mesh, PartitionSpec as P

AXES = ("y", "xl", "z", "xh", "c")
CYCLE = ("y", "xl", "z")
F32 = jnp.float32
BF16 = jnp.bfloat16
D = 1152
ROWS = 512
SENT = 528
STEP = 256
WIDE = 640
PART = 384


def shifted(value, steps):
    count = lax.axis_size(CYCLE)
    return lax.ppermute(value, CYCLE, [(i, (i + steps) % count) for i in range(count)])


def after(value, *others):
    return lax.optimization_barrier((value,) + others)[0]


def nn(a, b):
    return jnp.dot(a, b, preferred_element_type=F32)


def nt(a, b):
    return lax.dot_general(a, b, (((1,), (1,)), ((), ())), preferred_element_type=F32)


class Load:
    def __init__(self, copy, buf):
        self.copy, self.buf, self.here = copy, buf, False

    def __call__(self):
        if not self.here:
            self.copy.wait()
            self.here = True
        return self.buf


class Store:
    def __init__(self, out, buf, sems):
        self.out, self.buf, self.sems, self.sent = out, buf, sems, []

    def send(self, half=None):
        if half is None:
            copy = pltpu.make_async_copy(self.buf, self.out, self.sems.at[0])
        else:
            size = self.buf.shape[0] // 2
            rows = pl.ds(half * size, size)
            copy = pltpu.make_async_copy(self.buf.at[rows], self.out.at[rows], self.sems.at[half])
        copy.start()
        self.sent.append(copy)


def run(body, outs, ins, scalars=(), scratch=(), flops=0, vmem=56):
    ins = [i if isinstance(i, tuple) else (i, None, None) for i in ins]
    n_s, n_i, n_o = len(scalars), len(ins), len(outs)

    def kernel(*refs):
        pars, refs = refs[:n_s], refs[n_s:]
        sources, refs = refs[:n_i], refs[n_i:]
        results, refs = refs[:n_o], refs[n_o:]
        in_bufs, refs = refs[:n_i], refs[n_i:]
        out_bufs, refs = refs[:n_o], refs[n_o:]
        in_sems, out_sems, extra = refs[0], refs[1], refs[2:]
        loads = []
        for k, (_, first, rows) in enumerate(ins):
            source = sources[k] if first is None else sources[k].at[pl.ds(first, rows)]
            copy = pltpu.make_async_copy(source, in_bufs[k], in_sems.at[k])
            copy.start()
            loads.append(Load(copy, in_bufs[k]))
        stores = [Store(results[k], out_bufs[k], out_sems.at[k]) for k in range(n_o)]
        body(pars, loads, stores, extra)
        for load in loads:
            load()
        for store in stores:
            for copy in store.sent:
                copy.wait()

    shapes = []
    for array, _, rows in ins:
        shape = array.shape if rows is None else (rows,) + array.shape[1:]
        shapes.append(pltpu.VMEM(shape, array.dtype))
    shapes += [pltpu.VMEM(s, t) for s, t in outs]
    shapes += [pltpu.SemaphoreType.DMA((max(n_i, 1),)), pltpu.SemaphoreType.DMA((n_o, 2))]
    shapes += [pltpu.VMEM(s, t) for s, t in scratch]
    return pl.pallas_call(
        kernel,
        out_shape=[jax.ShapeDtypeStruct(s, t) for s, t in outs],
        in_specs=[pl.BlockSpec(memory_space=pltpu.SMEM)] * n_s
        + [pl.BlockSpec(memory_space=pl.ANY)] * n_i,
        out_specs=[pl.BlockSpec(memory_space=pl.ANY)] * n_o,
        scratch_shapes=shapes,
        compiler_params=pltpu.CompilerParams(vmem_limit_bytes=vmem * 2**20),
        cost_estimate=pl.CostEstimate(flops=flops, bytes_accessed=0, transcendentals=0),
    )(*scalars, *[i[0] for i in ins])


HALVES = [pl.ds(i * STEP, STEP) for i in range(ROWS // STEP)]


def inverse_norm(values):
    return lax.rsqrt(jnp.sum(values * values, axis=-1, keepdims=True) + 1e-06)


def lane_ids(pair):
    pair = pair[:, pl.ds(0, ROWS)].astype(F32)
    return pair[0:1] * 256.0 + pair[1:2]


def carried(block):
    return lane_ids(block.at[pl.ds(ROWS, 16)])


def column(lane):
    return jnp.broadcast_to(lane, (8, ROWS)).T[:, 0:1]


def coef_of(par, rows, row_ids, columns, column_ids):
    scale, offset = par[0], par[1]
    logits = scale * nt(rows, columns) + offset
    positive = (row_ids == column_ids).astype(F32)
    return (scale * (jax.nn.sigmoid(logits) - positive)).astype(BF16)


def unit_images(feats, head, half, u_out=None):
    for r in HALVES:
        u = nn(feats[r, :], head[...])
        half[r, :] = (u * inverse_norm(u)).astype(BF16)
        if u_out is not None:
            u_out[r, :] = u


def turn(feats, out):
    for k in range(D // 128):
        cols = pl.ds(k * 128, 128)
        out[cols, :] = feats[pl.ds(0, ROWS), cols].T


def project(inv, grad, x):
    return inv * (grad - x * jnp.sum(x * grad, axis=1, keepdims=True))


def project_u(grad, u):
    inv = inverse_norm(u)
    return project(inv, grad, u * inv).astype(BF16)


def prepare(_, loads, stores, __):
    text, image, text_lane, image_lane = loads
    text_out, image_out = stores
    image()
    text()
    for r in HALVES:
        image_out.buf[r, :] = image()[r, :]
    for load, out in ((image_lane, image_out), (text_lane, text_out)):
        if out is text_out:
            for r in HALVES:
                t = text()[r, :].astype(F32)
                out.buf[r, :] = (t * inverse_norm(t)).astype(BF16)
        out.buf[pl.ds(ROWS, 16), :] = jnp.zeros((16, D), BF16)
        row = lax.broadcasted_iota(jnp.int32, (16, ROWS), 0)
        ids = load()[...]
        high, low = (ids >> 8).astype(F32), (ids & 255).astype(F32)
        pair = jnp.where(row == 0, high, jnp.where(row == 1, low, 0.0))
        out.buf[pl.ds(ROWS, 16), pl.ds(0, ROWS)] = pair.astype(BF16)
        out.send()


def first(pars, loads, stores, _):
    (par,) = pars
    a0, head, y0 = loads
    u_out, half, a_t, gx, gy = stores
    unit_images(a0(), head(), half.buf, u_out.buf)
    u_out.send()
    half.send()
    t_lane, i_lane = carried(y0()), carried(a0())
    iid, tid = column(i_lane), column(t_lane)
    text, x = y0()[pl.ds(0, ROWS), :], half.buf
    for k, r in enumerate(HALVES):
        ids = slice(k * STEP, k * STEP + STEP)
        gx.buf[r, :] = nn(coef_of(par, x[r, :], iid[ids], text, t_lane), text)
        gy.buf[r, :] = nn(coef_of(par, y0()[r, :], tid[ids], x[...], i_lane), x[...])
        gx.send(k)
        gy.send(k)
    turn(a0(), a_t.buf)
    a_t.send()


def second(pars, loads, stores, _):
    (par,) = pars
    a1, head, y1, x0, y0, i_own, t_own, gx0, gy0 = loads
    u_out, half, a_t, gx, gy = stores
    unit_images(a1(), head(), half.buf, u_out.buf)
    u_out.send()
    half.send()
    tiles(par, y1, a1, half.buf, x0, y0, i_own, t_own, gx0, gy0, gx, gy)
    turn(a1(), a_t.buf)
    a_t.send()


def tiles(par, y, a, x, x0, y0, i_own, t_own, gx0, gy0, gx, gy):
    t_lane, i_lane = carried(y()), carried(a())
    iid, tid = column(lane_ids(i_own())), column(lane_ids(t_own()))
    text = y()[pl.ds(0, ROWS), :]
    x0(), y0(), gx0(), gy0()
    for k, r in enumerate(HALVES):
        ids = slice(k * STEP, k * STEP + STEP)
        gx.buf[r, :] = gx0()[r, :] + nn(coef_of(par, x0()[r, :], iid[ids], text, t_lane), text)
        gy.buf[r, :] = gy0()[r, :] + nn(coef_of(par, y0()[r, :], tid[ids], x[...], i_lane), x[...])
        gx.send(k)
        gy.send(k)


def third(pars, loads, stores, scratch):
    (par,) = pars
    a2, head, y2, x0, i_own, gx0, u0, x1, i_near, u1 = loads
    half, a_t, g0, g1, g2, gx = stores
    (u2,) = scratch
    unit_images(a2(), head(), half.buf, u2)
    half.send()
    t_lane = carried(y2())
    iid = column(lane_ids(i_own()))
    ids1 = column(lane_ids(i_near()))
    ids2 = column(carried(a2()))
    text = y2()[pl.ds(0, ROWS), :]
    x0(), gx0(), u0(), x1(), u1()
    for k, r in enumerate(HALVES):
        ids = slice(k * STEP, k * STEP + STEP)
        grad = gx0()[r, :] + nn(coef_of(par, x0()[r, :], iid[ids], text, t_lane), text)
        gx.buf[r, :] = grad
        g0.buf[r, :] = project_u(grad, u0()[r, :])
        grad = nn(coef_of(par, x1()[r, :], ids1[ids], text, t_lane), text)
        g1.buf[r, :] = project_u(grad, u1()[r, :])
        grad = nn(coef_of(par, half.buf[r, :], ids2[ids], text, t_lane), text)
        g2.buf[r, :] = project_u(grad, u2[r, :])
        for store in (gx, g0, g1, g2):
            store.send(k)
    turn(a2(), a_t.buf)
    a_t.send()


def head_part(pars, loads, stores, _):
    (start,) = pars
    cols = pl.ds(pl.multiple_of(start[0], 128), WIDE)
    for load in loads:
        load()
    a0, a1, a2, u0, u1, u2 = [load() for load in loads]
    for i, store in enumerate(stores):
        out = store.buf

        @pl.loop(0, D // 288 // len(stores))
        def _(k):
            at = pl.multiple_of(k * 288, 288)
            r = pl.ds(at + D // len(stores) * i, 288)
            total = nn(a0[r, :], u0[:, cols])
            total = total + nn(a1[r, :], u1[:, cols])
            total = total + nn(a2[r, :], u2[:, cols])
            out[pl.ds(at, 288), :] = total.astype(out.dtype)

        store.send()


def text_only(pars, loads, stores, _):
    (par,) = pars
    y0, x2, i_far, t_own, gy0 = loads
    (gy,) = stores
    i_lane, tid = lane_ids(i_far()), column(lane_ids(t_own()))
    y0(), x2(), gy0()
    for k, r in enumerate(HALVES):
        ids = slice(k * STEP, k * STEP + STEP)
        gy.buf[r, :] = gy0()[r, :] + nn(
            coef_of(par, y0()[r, :], tid[ids], x2()[...], i_lane), x2()[...]
        )
        gy.send(k)


def to_pieces(_, loads, stores, __):
    mine, low, high = [load() for load in loads]
    out = stores[0].buf
    for k in range(8):
        other = (low, high)[k // 4]
        s = pl.ds(144 * (k % 4), 144)
        total = (mine[pl.ds(144 * k, 144), :] + other[s, :].astype(F32)).astype(BF16)
        out[2 * k] = total[:, :PART]
        out[2 * k + 1] = total[:, 256 : 256 + PART]
        if k % 4 == 3:
            stores[0].send(k // 4)


def add_pieces(_, loads, stores, __):
    got, out = loads[0](), stores[0].buf
    total = got[0].astype(F32)
    for k in range(1, 16):
        total = total + got[k].astype(F32)
    for k in range(8):
        out[k] = total[18 * k : 18 * k + 18]
    stores[0].send()


def add_last(_, loads, stores, __):
    got = loads[0]()
    total = got[0]
    for k in range(1, 8):
        total = total + got[k]
    stores[0].buf[...] = total * (1.0 / 256.0)
    stores[0].send()


def fourth(pars, loads, stores, scratch):
    (par,) = pars
    a3, head, y3, x0, y0, i_own, t_own, gx0, gy0 = loads
    gx, gy = stores
    (half,) = scratch
    unit_images(a3(), head(), half)
    tiles(par, y3, a3, half, x0, y0, i_own, t_own, gx0, gy0, gx, gy)


def last(pars, loads, stores, scratch):
    (par,) = pars
    y4, x0, i_own, head, gx0, u0, a4, y0, t_own, gy0, text_in = loads
    g_image, g_text = stores
    (half,) = scratch
    t_lane = carried(y4())
    iid = column(lane_ids(i_own()))
    text = y4()[pl.ds(0, ROWS), :]
    x0(), gx0(), u0(), head()
    for k, r in enumerate(HALVES):
        ids = slice(k * STEP, k * STEP + STEP)
        grad = gx0()[r, :] + nn(coef_of(par, x0()[r, :], iid[ids], text, t_lane), text)
        g_image.buf[r, :] = nt(project_u(grad, u0()[r, :]), head()[...]).astype(BF16)
        g_image.send(k)
    unit_images(a4(), head(), half)
    i_lane, tid = carried(a4()), column(lane_ids(t_own()))
    y0(), gy0(), text_in()
    for k, r in enumerate(HALVES):
        ids = slice(k * STEP, k * STEP + STEP)
        grad = gy0()[r, :] + nn(coef_of(par, y0()[r, :], tid[ids], half[...], i_lane), half[...])
        t = text_in()[r, :].astype(F32)
        inv = inverse_norm(t)
        g_text.buf[r, :] = project(inv, grad, t * inv).astype(BF16)
        g_text.send(k)


BLOCK = ((ROWS, D), BF16)
SUMS = ((ROWS, D), F32)
TURNED = ((D, ROWS), BF16)
TRAVEL = ((SENT, D), BF16)


def per_device(image_feats, text_feats, head, image_ids, text_ids, log_scale, bias):
    core = lax.axis_index("c")
    par = jnp.stack([jnp.exp(log_scale[0]), bias[0]])
    ids_of = lambda block: (block, ROWS, 16)
    y0, a0 = run(
        prepare, [TRAVEL, TRAVEL],
        [text_feats, image_feats, text_ids.reshape(1, ROWS), image_ids.reshape(1, ROWS)],
    )
    y1, a1 = shifted(y0, 1), shifted(a0, -1)
    u0, x0, at0, gx, gy = run(first, [SUMS, BLOCK, TURNED, SUMS, SUMS], [a0, head, y0], [par])
    y2, a2 = shifted(after(y1, gx), 1), shifted(after(a1, gx), -1)
    own_y = (y0, 0, ROWS)
    u1, x1, at1, gx, gy = run(
        second, [SUMS, BLOCK, TURNED, SUMS, SUMS],
        [a1, head, y1, x0, own_y, ids_of(a0), ids_of(y0), gx, gy], [par],
    )
    y3, a3 = shifted(after(y2, gx), 1), shifted(after(a2, gx), -1)
    x2, at2, g0, g1, g2, gx = run(
        third, [BLOCK, TURNED, BLOCK, BLOCK, BLOCK, SUMS],
        [a2, head, y2, x0, ids_of(a0), gx, u0, x1, ids_of(a1), u1], [par], [SUMS],
    )
    part = ((D // 2, WIDE), BF16)
    terms = [at0, at1, at2, g0, g1, g2]
    away = run(head_part, [part, part], terms, [(512 * (1 - core)).reshape(1)])
    got = [lax.ppermute(half, "c", [(0, 1), (1, 0)]) for half in away]
    (mine,) = run(
        head_part, [((D, WIDE), F32)], terms, [after((512 * core).reshape(1), *away)]
    )
    (gy,) = run(
        text_only, [SUMS], [own_y, x2, ids_of(a2), ids_of(y0), after(gy, mine)], [par]
    )
    (pieces,) = run(to_pieces, [((16, 144, PART), BF16)], [after(mine, gy), *got])
    spread = lax.all_to_all(pieces, ("y", "xl", "xh"), 0, 0)
    gx, gy = run(
        fourth, [SUMS, SUMS],
        [a3, head, y3, x0, own_y, ids_of(a0), ids_of(y0), gx, after(gy, pieces)],
        [par], [BLOCK], flops=10**11,
    )
    y4, a4 = shifted(after(y3, mine), 1), shifted(after(a3, mine), -1)
    (total,) = run(add_pieces, [((8, 18, PART), F32)], [after(spread, gx)])
    spread = lax.all_to_all(total, "z", 0, 0)
    (total,) = run(add_last, [((18, PART), F32)], [spread])
    parts = lax.all_gather(total, ("xh", "c"))
    grad_head = jnp.concatenate(
        [parts[0], parts[2][:, 128:], parts[1][:, 128:], parts[3][:, 128:]], axis=1
    )
    grad_image, grad_text = run(
        last, [BLOCK, BLOCK],
        [y4, x0, ids_of(a0), head, gx, u0, a4, own_y, ids_of(y0), after(gy, total), text_feats],
        [par], [BLOCK],
    )
    return grad_image, grad_text, grad_head


def solution(mesh):
    fine = Mesh(mesh.devices.reshape(4, 2, 8, 2, 2), AXES)
    placed = (P(AXES, None), P(AXES, None), P(), P(AXES), P(AXES), P(), P())
    return jax.shard_map(
        per_device,
        mesh=fine,
        in_specs=placed,
        out_specs=(P(AXES, None), P(AXES, None), P(CYCLE, None)),
        check_vma=False,
    )
```

```python
import jax
import jax.numpy as jnp
from jax import lax
from jax.experimental import pallas as pl
from jax.experimental.pallas import tpu as pltpu
from jax.sharding import Mesh, PartitionSpec as P

AXES = ("y", "xl", "z", "xh", "c")
CYCLE = ("y", "xl", "z")
F32 = jnp.float32
BF16 = jnp.bfloat16
D = 1152
ROWS = 512
SENT = 528
STEP = 256
WIDE = 640
PART = 384


def shifted(value, steps):
    count = lax.axis_size(CYCLE)
    return lax.ppermute(value, CYCLE, [(i, (i + steps) % count) for i in range(count)])


def after(value, *others):
    return lax.optimization_barrier((value,) + others)[0]


def nn(a, b):
    return jnp.dot(a, b, preferred_element_type=F32)


def nt(a, b):
    return lax.dot_general(a, b, (((1,), (1,)), ((), ())), preferred_element_type=F32)


class Load:
    def __init__(self, copy, buf):
        self.copy, self.buf, self.here = copy, buf, False

    def __call__(self):
        if not self.here:
            self.copy.wait()
            self.here = True
        return self.buf


class Store:
    def __init__(self, out, buf, sems):
        self.out, self.buf, self.sems, self.sent = out, buf, sems, []

    def send(self, half=None):
        if half is None:
            copy = pltpu.make_async_copy(self.buf, self.out, self.sems.at[0])
        else:
            size = self.buf.shape[0] // 2
            rows = pl.ds(half * size, size)
            copy = pltpu.make_async_copy(self.buf.at[rows], self.out.at[rows], self.sems.at[half])
        copy.start()
        self.sent.append(copy)


def run(body, outs, ins, scalars=(), scratch=(), flops=0, vmem=56, direct=()):
    ins = [i if isinstance(i, tuple) else (i, None, None) for i in ins]
    n_d, n_i, n_o = len(direct), len(ins), len(outs)
    n_s = len(scalars) + n_d

    def kernel(*refs):
        pars, refs = refs[:n_s], refs[n_s:]
        sources, refs = refs[:n_i], refs[n_i:]
        results, refs = refs[:n_o], refs[n_o:]
        in_bufs, refs = refs[:n_i], refs[n_i:]
        out_bufs, refs = refs[:n_o], refs[n_o:]
        in_sems, out_sems, extra = refs[0], refs[1], refs[2:]
        loads = []
        for k, (_, first, rows) in enumerate(ins):
            source = sources[k] if first is None else sources[k].at[pl.ds(first, rows)]
            copy = pltpu.make_async_copy(source, in_bufs[k], in_sems.at[k])
            copy.start()
            loads.append(Load(copy, in_bufs[k]))
        stores = [Store(results[k], out_bufs[k], out_sems.at[k]) for k in range(n_o)]
        body(pars, loads, stores, extra)
        for load in loads:
            load()
        for store in stores:
            for copy in store.sent:
                copy.wait()

    shapes = []
    for array, _, rows in ins:
        shape = array.shape if rows is None else (rows,) + array.shape[1:]
        shapes.append(pltpu.VMEM(shape, array.dtype))
    shapes += [pltpu.VMEM(s, t) for s, t in outs]
    shapes += [pltpu.SemaphoreType.DMA((max(n_i, 1),)), pltpu.SemaphoreType.DMA((n_o, 2))]
    shapes += [pltpu.VMEM(s, t) for s, t in scratch]
    return pl.pallas_call(
        kernel,
        out_shape=[jax.ShapeDtypeStruct(s, t) for s, t in outs],
        in_specs=[pl.BlockSpec(memory_space=pltpu.SMEM)] * len(scalars)
        + [pl.BlockSpec(memory_space=pltpu.VMEM)] * n_d
        + [pl.BlockSpec(memory_space=pl.ANY)] * n_i,
        out_specs=[pl.BlockSpec(memory_space=pl.ANY)] * n_o,
        scratch_shapes=shapes,
        compiler_params=pltpu.CompilerParams(vmem_limit_bytes=vmem * 2**20),
        cost_estimate=pl.CostEstimate(flops=flops, bytes_accessed=0, transcendentals=0),
    )(*scalars, *direct, *[i[0] for i in ins])


HALVES = [pl.ds(i * STEP, STEP) for i in range(ROWS // STEP)]


def inverse_norm(values):
    return lax.rsqrt(jnp.sum(values * values, axis=-1, keepdims=True) + 1e-06)


def lane_ids(pair):
    pair = pair[:, pl.ds(0, ROWS)].astype(F32)
    return pair[0:1] * 256.0 + pair[1:2]


def carried(block):
    return lane_ids(block.at[pl.ds(ROWS, 16)])


def column(lane):
    return jnp.broadcast_to(lane, (8, ROWS)).T[:, 0:1]


def coef_of(par, rows, row_ids, columns, column_ids):
    scale, offset = par[0], par[1]
    logits = scale * nt(rows, columns) + offset
    positive = (row_ids == column_ids).astype(F32)
    return (scale * (jax.nn.sigmoid(logits) - positive)).astype(BF16)


def unit_images(feats, head, half, u_out=None):
    for r in HALVES:
        u = nn(feats[r, :], head[...])
        half[r, :] = (u * inverse_norm(u)).astype(BF16)
        if u_out is not None:
            u_out[r, :] = u


def turn(feats, out):
    for k in range(D // 128):
        cols = pl.ds(k * 128, 128)
        out[cols, :] = feats[pl.ds(0, ROWS), cols].T


def project(inv, grad, x):
    return inv * (grad - x * jnp.sum(x * grad, axis=1, keepdims=True))


def project_u(grad, u):
    inv = inverse_norm(u)
    return project(inv, grad, u * inv).astype(BF16)


def prepare(_, loads, stores, __):
    text, image, text_lane, image_lane = loads
    text_out, image_out = stores
    image()
    text()
    for r in HALVES:
        image_out.buf[r, :] = image()[r, :]
    for load, out in ((image_lane, image_out), (text_lane, text_out)):
        if out is text_out:
            for r in HALVES:
                t = text()[r, :].astype(F32)
                out.buf[r, :] = (t * inverse_norm(t)).astype(BF16)
        out.buf[pl.ds(ROWS, 16), :] = jnp.zeros((16, D), BF16)
        row = lax.broadcasted_iota(jnp.int32, (16, ROWS), 0)
        ids = load()[...]
        high, low = (ids >> 8).astype(F32), (ids & 255).astype(F32)
        pair = jnp.where(row == 0, high, jnp.where(row == 1, low, 0.0))
        out.buf[pl.ds(ROWS, 16), pl.ds(0, ROWS)] = pair.astype(BF16)
        out.send()


def first(pars, loads, stores, _):
    (par,) = pars
    a0, head, y0 = loads
    u_out, half, a_t, gx, gy = stores
    unit_images(a0(), head(), half.buf, u_out.buf)
    u_out.send()
    half.send()
    t_lane, i_lane = carried(y0()), carried(a0())
    iid, tid = column(i_lane), column(t_lane)
    text, x = y0()[pl.ds(0, ROWS), :], half.buf
    for k, r in enumerate(HALVES):
        ids = slice(k * STEP, k * STEP + STEP)
        gx.buf[r, :] = nn(coef_of(par, x[r, :], iid[ids], text, t_lane), text)
        gy.buf[r, :] = nn(coef_of(par, y0()[r, :], tid[ids], x[...], i_lane), x[...])
        gx.send(k)
        gy.send(k)
    turn(a0(), a_t.buf)
    a_t.send()


def second(pars, loads, stores, scratch):
    par, starts = pars
    a1, head, y1, x0, y0, i_own, t_own, gx0, gy0, u0, at0 = loads
    u_out, half, a_t, gx, gy, near, away, mine = stores
    (g0,) = scratch
    unit_images(a1(), head(), half.buf, u_out.buf)
    u_out.send()
    half.send()
    tiles(par, y1, a1, half.buf, x0, y0, i_own, t_own, gx0, gy0, gx, gy)
    t_lane, ids1 = carried(y1()), column(carried(a1()))
    text = y1()[pl.ds(0, ROWS), :]
    u0()
    for k, r in enumerate(HALVES):
        ids = slice(k * STEP, k * STEP + STEP)
        near.buf[r, :] = nn(coef_of(par, half.buf[r, :], ids1[ids], text, t_lane), text)
        near.send(k)
        g0[r, :] = project_u(gx.buf[r, :], u0()[r, :])
    turn(a1(), a_t.buf)
    a_t.send()
    at0()
    for start, store in ((starts[0], away), (starts[1], mine)):
        cols = pl.ds(pl.multiple_of(start, 128), WIDE)
        for k in range(2):

            @pl.loop(2 * k, 2 * k + 2)
            def _(j):
                r = pl.ds(pl.multiple_of(j * 288, 288), 288)
                store.buf[r, :] = nn(at0()[r, :], g0[:, cols])

            store.send(k)


def tiles(par, y, a, x, x0, y0, i_own, t_own, gx0, gy0, gx, gy):
    t_lane, i_lane = carried(y()), carried(a())
    iid, tid = column(lane_ids(i_own())), column(lane_ids(t_own()))
    text = y()[pl.ds(0, ROWS), :]
    x0(), y0(), gx0(), gy0()
    for k, r in enumerate(HALVES):
        ids = slice(k * STEP, k * STEP + STEP)
        gx.buf[r, :] = gx0()[r, :] + nn(coef_of(par, x0()[r, :], iid[ids], text, t_lane), text)
        gy.buf[r, :] = gy0()[r, :] + nn(coef_of(par, y0()[r, :], tid[ids], x[...], i_lane), x[...])
        gx.send(k)
        gy.send(k)


def third(pars, loads, stores, scratch):
    par, starts = pars
    a2, head, y2, x1, i_near, near, u1, at1, away0, mine0 = loads
    half, low, high, mine = stores
    u2, at2, g1, g2 = scratch
    unit_images(a2(), head(), half.buf, u2)
    half.send()
    t_lane = carried(y2())
    ids1 = column(lane_ids(i_near()))
    ids2 = column(carried(a2()))
    text = y2()[pl.ds(0, ROWS), :]
    x1(), u1(), near()
    for k, r in enumerate(HALVES):
        ids = slice(k * STEP, k * STEP + STEP)
        grad = nn(coef_of(par, x1()[r, :], ids1[ids], text, t_lane), text)
        g1[r, :] = project_u(grad + near()[r, :], u1()[r, :])
        grad = nn(coef_of(par, half.buf[r, :], ids2[ids], text, t_lane), text)
        g2[r, :] = project_u(grad, u2[r, :])
    turn(a2(), at2)
    at1(), away0(), mine0()

    def summed(start, before, r):
        cols = pl.ds(pl.multiple_of(start, 128), WIDE)
        total = before()[r, :] + nn(at1()[r, :], g1[:, cols])
        return total + nn(at2[r, :], g2[:, cols])

    for i, store in enumerate((low, high)):

        @pl.loop(0, 2)
        def _(k):
            at = pl.multiple_of(k * 288, 288)
            rows = summed(starts[0], away0, pl.ds(at + 576 * i, 288))
            store.buf[pl.ds(at, 288), :] = rows.astype(BF16)

        store.send()
    for k in range(2):

        @pl.loop(2 * k, 2 * k + 2)
        def _(j):
            r = pl.ds(pl.multiple_of(j * 288, 288), 288)
            mine.buf[r, :] = summed(starts[1], mine0, r)

        mine.send(k)


def to_pieces(direct, loads, stores, __):
    mine, (low, high) = loads[0](), direct
    out = stores[0].buf
    for k in range(8):
        other = (low, high)[k // 4]
        s = pl.ds(144 * (k % 4), 144)
        total = (mine[pl.ds(144 * k, 144), :] + other[s, :].astype(F32)).astype(BF16)
        out[2 * k] = total[:, :PART]
        out[2 * k + 1] = total[:, 256 : 256 + PART]
        if k % 4 == 3:
            stores[0].send(k // 4)


def add_pieces(direct, _, stores, __):
    got, out = direct[0], stores[0].buf
    total = got[0].astype(F32)
    for k in range(1, 16):
        total = total + got[k].astype(F32)
    for k in range(8):
        out[k] = total[18 * k : 18 * k + 18]
    stores[0].send()


def add_last(direct, _, stores, __):
    got = direct[0]
    total = got[0]
    for k in range(1, 8):
        total = total + got[k]
    stores[0].buf[...] = total * (1.0 / 256.0)
    stores[0].send()


def fourth(pars, loads, stores, scratch):
    (par,) = pars
    a3, head, y3, x0, y0, i_own, t_own, gx0, x2, i_far, y2, gy0 = loads
    gx, gy = stores
    (half,) = scratch
    unit_images(a3(), head(), half)
    t_lane, i_lane, far = carried(y3()), carried(a3()), lane_ids(i_far())
    iid, tid = column(lane_ids(i_own())), column(lane_ids(t_own()))
    text = y3()[pl.ds(0, ROWS), :]
    x0(), y0(), gx0(), gy0(), x2()
    text2, t_lane2 = y2()[pl.ds(0, ROWS), :], carried(y2())
    for k, r in enumerate(HALVES):
        ids = slice(k * STEP, k * STEP + STEP)
        total = gx0()[r, :] + nn(coef_of(par, x0()[r, :], iid[ids], text2, t_lane2), text2)
        total = total + nn(coef_of(par, x0()[r, :], iid[ids], text, t_lane), text)
        gx.buf[r, :] = total
        gx.send(k)
        total = gy0()[r, :] + nn(coef_of(par, y0()[r, :], tid[ids], x2()[...], far), x2()[...])
        total = total + nn(coef_of(par, y0()[r, :], tid[ids], half[...], i_lane), half[...])
        gy.buf[r, :] = total
        gy.send(k)


def last(pars, loads, stores, scratch):
    (par,) = pars
    y4, x0, i_own, head, gx0, u0, a4, y0, t_own, gy0, text_in = loads
    g_image, g_text = stores
    (half,) = scratch
    t_lane = carried(y4())
    iid = column(lane_ids(i_own()))
    text = y4()[pl.ds(0, ROWS), :]
    x0(), gx0(), u0(), head()
    for k, r in enumerate(HALVES):
        ids = slice(k * STEP, k * STEP + STEP)
        grad = gx0()[r, :] + nn(coef_of(par, x0()[r, :], iid[ids], text, t_lane), text)
        g_image.buf[r, :] = nt(project_u(grad, u0()[r, :]), head()[...]).astype(BF16)
        g_image.send(k)
    unit_images(a4(), head(), half)
    i_lane, tid = carried(a4()), column(lane_ids(t_own()))
    y0(), gy0(), text_in()
    for k, r in enumerate(HALVES):
        ids = slice(k * STEP, k * STEP + STEP)
        grad = gy0()[r, :] + nn(coef_of(par, y0()[r, :], tid[ids], half[...], i_lane), half[...])
        t = text_in()[r, :].astype(F32)
        inv = inverse_norm(t)
        g_text.buf[r, :] = project(inv, grad, t * inv).astype(BF16)
        g_text.send(k)


BLOCK = ((ROWS, D), BF16)
SUMS = ((ROWS, D), F32)
TURNED = ((D, ROWS), BF16)
TRAVEL = ((SENT, D), BF16)


def per_device(image_feats, text_feats, head, image_ids, text_ids, log_scale, bias):
    core = lax.axis_index("c")
    par = jnp.stack([jnp.exp(log_scale[0]), bias[0]])
    ids_of = lambda block: (block, ROWS, 16)
    y0, a0 = run(
        prepare, [TRAVEL, TRAVEL],
        [text_feats, image_feats, text_ids.reshape(1, ROWS), image_ids.reshape(1, ROWS)],
    )
    y1, a1 = shifted(y0, 1), shifted(a0, -1)
    u0, x0, at0, gx, gy = run(first, [SUMS, BLOCK, TURNED, SUMS, SUMS], [a0, head, y0], [par])
    y2, a2 = shifted(after(y1, gx), 1), shifted(after(a1, gx), -1)
    own_y = (y0, 0, ROWS)
    starts = jnp.stack([512 * (1 - core), 512 * core])
    piece = ((D, WIDE), F32)
    u1, x1, at1, gx, gy, near, away, mine = run(
        second, [SUMS, BLOCK, TURNED, SUMS, SUMS, SUMS, piece, piece],
        [a1, head, y1, x0, own_y, ids_of(a0), ids_of(y0), gx, gy, u0, at0],
        [par, starts], [BLOCK],
    )
    y3, a3 = shifted(after(y2, gx), 1), shifted(after(a2, gx), -1)
    part = ((D // 2, WIDE), BF16)
    x2, low, high, mine = run(
        third, [BLOCK, part, part, piece],
        [a2, head, y2, x1, ids_of(a1), near, u1, at1, away, mine],
        [par, starts], [SUMS, TURNED, BLOCK, BLOCK],
    )
    got = [lax.ppermute(half, "c", [(0, 1), (1, 0)]) for half in (low, high)]
    (pieces,) = run(to_pieces, [((16, 144, PART), BF16)], [mine], direct=got)
    spread = lax.all_to_all(pieces, ("y", "xl", "xh"), 0, 0)
    gx, gy = run(
        fourth, [SUMS, SUMS],
        [a3, head, y3, x0, own_y, ids_of(a0), ids_of(y0), gx, x2, ids_of(a2), y2,
         after(gy, pieces)],
        [par], [BLOCK], flops=10**11,
    )
    y4, a4 = shifted(after(y3, mine), 1), shifted(after(a3, mine), -1)
    (total,) = run(add_pieces, [((8, 18, PART), F32)], [], direct=[after(spread, gx)])
    spread = lax.all_to_all(total, "z", 0, 0)
    grad_image, grad_text = run(
        last, [BLOCK, BLOCK],
        [y4, x0, ids_of(a0), head, gx, u0, a4, own_y, ids_of(y0), after(gy, total), text_feats],
        [par], [BLOCK], flops=10**11,
    )
    (total,) = run(add_last, [((18, PART), F32)], [], direct=[after(spread, grad_text)])
    parts = lax.all_gather(total, ("xh", "c"))
    grad_head = jnp.concatenate(
        [parts[0], parts[2][:, 128:], parts[1][:, 128:], parts[3][:, 128:]], axis=1
    )
    return grad_image, grad_text, grad_head


def solution(mesh):
    fine = Mesh(mesh.devices.reshape(4, 2, 8, 2, 2), AXES)
    placed = (P(AXES, None), P(AXES, None), P(), P(AXES), P(AXES), P(), P())
    return jax.shard_map(
        per_device,
        mesh=fine,
        in_specs=placed,
        out_specs=(P(AXES, None), P(AXES, None), P(CYCLE, None)),
        check_vma=False,
    )
```

```python
import jax
import jax.numpy as jnp
from jax import lax
from jax.experimental import pallas as pl
from jax.experimental.pallas import tpu as pltpu
from jax.sharding import Mesh, PartitionSpec as P

AXES = ("y", "xl", "z", "xh", "c")
CYCLE = ("y", "xl", "z")
F32 = jnp.float32
BF16 = jnp.bfloat16
D = 1152
ROWS = 512
SENT = 528
STEP = 256
WIDE = 640
PART = 384


def shifted(value, steps):
    count = lax.axis_size(CYCLE)
    return lax.ppermute(value, CYCLE, [(i, (i + steps) % count) for i in range(count)])


def after(value, *others):
    return lax.optimization_barrier((value,) + others)[0]


def nn(a, b):
    return jnp.dot(a, b, preferred_element_type=F32)


def nt(a, b):
    return lax.dot_general(a, b, (((1,), (1,)), ((), ())), preferred_element_type=F32)


class Load:
    def __init__(self, copy, buf):
        self.copy, self.buf, self.here, self.then = copy, buf, False, []

    def __call__(self):
        if not self.here:
            self.copy.wait()
            self.here = True
            for copy in self.then:
                copy.start()
        return self.buf


class Store:
    def __init__(self, out, buf, sems):
        self.out, self.buf, self.sems, self.sent = out, buf, sems, []

    def send(self, half=None):
        if half is None:
            copy = pltpu.make_async_copy(self.buf, self.out, self.sems.at[0])
        else:
            size = self.buf.shape[0] // 2
            rows = pl.ds(half * size, size)
            copy = pltpu.make_async_copy(self.buf.at[rows], self.out.at[rows], self.sems.at[half])
        copy.start()
        self.sent.append(copy)


def run(body, outs, ins, scalars=(), scratch=(), flops=0, vmem=56, direct=(), eager=99):
    ins = [i if isinstance(i, tuple) else (i, None, None) for i in ins]
    n_d, n_i, n_o = len(direct), len(ins), len(outs)
    n_s = len(scalars) + n_d

    def kernel(*refs):
        pars, refs = refs[:n_s], refs[n_s:]
        sources, refs = refs[:n_i], refs[n_i:]
        results, refs = refs[:n_o], refs[n_o:]
        in_bufs, refs = refs[:n_i], refs[n_i:]
        out_bufs, refs = refs[:n_o], refs[n_o:]
        in_sems, out_sems, extra = refs[0], refs[1], refs[2:]
        loads = []
        for k, (_, first, rows) in enumerate(ins):
            source = sources[k] if first is None else sources[k].at[pl.ds(first, rows)]
            copy = pltpu.make_async_copy(source, in_bufs[k], in_sems.at[k])
            loads.append(Load(copy, in_bufs[k]))
            if k < eager:
                copy.start()
            else:
                loads[eager - 1].then.append(copy)
        stores = [Store(results[k], out_bufs[k], out_sems.at[k]) for k in range(n_o)]
        body(pars, loads, stores, extra)
        for load in loads:
            load()
        for store in stores:
            for copy in store.sent:
                copy.wait()

    shapes = []
    for array, _, rows in ins:
        shape = array.shape if rows is None else (rows,) + array.shape[1:]
        shapes.append(pltpu.VMEM(shape, array.dtype))
    shapes += [pltpu.VMEM(s, t) for s, t in outs]
    shapes += [pltpu.SemaphoreType.DMA((max(n_i, 1),)), pltpu.SemaphoreType.DMA((n_o, 2))]
    shapes += [pltpu.VMEM(s, t) for s, t in scratch]
    return pl.pallas_call(
        kernel,
        out_shape=[jax.ShapeDtypeStruct(s, t) for s, t in outs],
        in_specs=[pl.BlockSpec(memory_space=pltpu.SMEM)] * len(scalars)
        + [pl.BlockSpec(memory_space=pltpu.VMEM)] * n_d
        + [pl.BlockSpec(memory_space=pl.ANY)] * n_i,
        out_specs=[pl.BlockSpec(memory_space=pl.ANY)] * n_o,
        scratch_shapes=shapes,
        compiler_params=pltpu.CompilerParams(vmem_limit_bytes=vmem * 2**20),
        cost_estimate=pl.CostEstimate(flops=flops, bytes_accessed=0, transcendentals=0),
    )(*scalars, *direct, *[i[0] for i in ins])


HALVES = [pl.ds(i * STEP, STEP) for i in range(ROWS // STEP)]


def inverse_norm(values):
    return lax.rsqrt(jnp.sum(values * values, axis=-1, keepdims=True) + 1e-06)


def lane_ids(pair):
    pair = pair[:, pl.ds(0, ROWS)].astype(F32)
    return pair[0:1] * 256.0 + pair[1:2]


def carried(block):
    return lane_ids(block.at[pl.ds(ROWS, 16)])


def column(lane):
    return jnp.broadcast_to(lane, (8, ROWS)).T[:, 0:1]


def coef_of(par, rows, row_ids, columns, column_ids):
    scale, offset = par[0], par[1]
    logits = scale * nt(rows, columns) + offset
    positive = (row_ids == column_ids).astype(F32)
    return (scale * (jax.nn.sigmoid(logits) - positive)).astype(BF16)


def unit_images(feats, head, half, u_out=None):
    for r in HALVES:
        u = nn(feats[r, :], head[...])
        half[r, :] = (u * inverse_norm(u)).astype(BF16)
        if u_out is not None:
            u_out[r, :] = u


def turn(feats, out):
    for k in range(D // 128):
        cols = pl.ds(k * 128, 128)
        out[cols, :] = feats[pl.ds(0, ROWS), cols].T


def project(inv, grad, x):
    return inv * (grad - x * jnp.sum(x * grad, axis=1, keepdims=True))


def project_u(grad, u):
    inv = inverse_norm(u)
    return project(inv, grad, u * inv).astype(BF16)


def prepare(_, loads, stores, __):
    text, image, text_lane, image_lane = loads
    text_out, image_out = stores
    image()
    text()
    for r in HALVES:
        image_out.buf[r, :] = image()[r, :]
    for load, out in ((image_lane, image_out), (text_lane, text_out)):
        if out is text_out:
            for r in HALVES:
                t = text()[r, :].astype(F32)
                out.buf[r, :] = (t * inverse_norm(t)).astype(BF16)
        out.buf[pl.ds(ROWS, 16), :] = jnp.zeros((16, D), BF16)
        row = lax.broadcasted_iota(jnp.int32, (16, ROWS), 0)
        ids = load()[...]
        high, low = (ids >> 8).astype(F32), (ids & 255).astype(F32)
        pair = jnp.where(row == 0, high, jnp.where(row == 1, low, 0.0))
        out.buf[pl.ds(ROWS, 16), pl.ds(0, ROWS)] = pair.astype(BF16)
        out.send()


def first(pars, loads, stores, _):
    (par,) = pars
    a0, head, y0 = loads
    u_out, half, a_t, gx, gy = stores
    unit_images(a0(), head(), half.buf, u_out.buf)
    u_out.send()
    half.send()
    t_lane, i_lane = carried(y0()), carried(a0())
    iid, tid = column(i_lane), column(t_lane)
    text, x = y0()[pl.ds(0, ROWS), :], half.buf
    for k, r in enumerate(HALVES):
        ids = slice(k * STEP, k * STEP + STEP)
        gx.buf[r, :] = nn(coef_of(par, x[r, :], iid[ids], text, t_lane), text)
        gy.buf[r, :] = nn(coef_of(par, y0()[r, :], tid[ids], x[...], i_lane), x[...])
        gx.send(k)
        gy.send(k)
    turn(a0(), a_t.buf)
    a_t.send()


def second(pars, loads, stores, scratch):
    par, starts = pars
    a1, head, y1, x0, y0, i_own, t_own, gx0, gy0, u0, at0 = loads
    u_out, half, a_t, gx, gy, near, away, mine = stores
    (g0,) = scratch
    unit_images(a1(), head(), half.buf, u_out.buf)
    u_out.send()
    half.send()
    tiles(par, y1, a1, half.buf, x0, y0, i_own, t_own, gx0, gy0, gx, gy)
    t_lane, ids1 = carried(y1()), column(carried(a1()))
    text = y1()[pl.ds(0, ROWS), :]
    u0()
    for k, r in enumerate(HALVES):
        ids = slice(k * STEP, k * STEP + STEP)
        near.buf[r, :] = nn(coef_of(par, half.buf[r, :], ids1[ids], text, t_lane), text)
        near.send(k)
        g0[r, :] = project_u(gx.buf[r, :], u0()[r, :])
    turn(a1(), a_t.buf)
    a_t.send()
    at0()
    for start, store in ((starts[0], away), (starts[1], mine)):
        cols = pl.ds(pl.multiple_of(start, 128), WIDE)
        for k in range(2):

            @pl.loop(2 * k, 2 * k + 2)
            def _(j):
                r = pl.ds(pl.multiple_of(j * 288, 288), 288)
                store.buf[r, :] = nn(at0()[r, :], g0[:, cols])

            store.send(k)


def tiles(par, y, a, x, x0, y0, i_own, t_own, gx0, gy0, gx, gy):
    t_lane, i_lane = carried(y()), carried(a())
    iid, tid = column(lane_ids(i_own())), column(lane_ids(t_own()))
    text = y()[pl.ds(0, ROWS), :]
    x0(), y0(), gx0(), gy0()
    for k, r in enumerate(HALVES):
        ids = slice(k * STEP, k * STEP + STEP)
        gx.buf[r, :] = gx0()[r, :] + nn(coef_of(par, x0()[r, :], iid[ids], text, t_lane), text)
        gy.buf[r, :] = gy0()[r, :] + nn(coef_of(par, y0()[r, :], tid[ids], x[...], i_lane), x[...])
        gx.send(k)
        gy.send(k)


def third(pars, loads, stores, scratch):
    par, starts = pars
    a2, head, y2, x1, i_near, near, u1, at1, away0, mine0 = loads
    half, low, high, mine = stores
    u2, at2, g1, g2 = scratch
    unit_images(a2(), head(), half.buf, u2)
    half.send()
    t_lane = carried(y2())
    ids1 = column(lane_ids(i_near()))
    ids2 = column(carried(a2()))
    text = y2()[pl.ds(0, ROWS), :]
    x1(), u1(), near()
    for k, r in enumerate(HALVES):
        ids = slice(k * STEP, k * STEP + STEP)
        grad = nn(coef_of(par, x1()[r, :], ids1[ids], text, t_lane), text)
        g1[r, :] = project_u(grad + near()[r, :], u1()[r, :])
        grad = nn(coef_of(par, half.buf[r, :], ids2[ids], text, t_lane), text)
        g2[r, :] = project_u(grad, u2[r, :])
    turn(a2(), at2)
    at1(), away0(), mine0()

    def summed(start, before, r):
        cols = pl.ds(pl.multiple_of(start, 128), WIDE)
        total = before()[r, :] + nn(at1()[r, :], g1[:, cols])
        return total + nn(at2[r, :], g2[:, cols])

    for i, store in enumerate((low, high)):

        @pl.loop(0, 2)
        def _(k):
            at = pl.multiple_of(k * 288, 288)
            rows = summed(starts[0], away0, pl.ds(at + 576 * i, 288))
            store.buf[pl.ds(at, 288), :] = rows.astype(BF16)

        store.send()
    for k in range(2):

        @pl.loop(2 * k, 2 * k + 2)
        def _(j):
            r = pl.ds(pl.multiple_of(j * 288, 288), 288)
            mine.buf[r, :] = summed(starts[1], mine0, r)

        mine.send(k)


def to_pieces(direct, loads, stores, __):
    mine, (low, high) = loads[0](), direct
    out = stores[0].buf
    for k in range(8):
        other = (low, high)[k // 4]
        s = pl.ds(144 * (k % 4), 144)
        total = (mine[pl.ds(144 * k, 144), :] + other[s, :].astype(F32)).astype(BF16)
        out[2 * k] = total[:, :PART]
        out[2 * k + 1] = total[:, 256 : 256 + PART]
        if k % 4 == 3:
            stores[0].send(k // 4)


def add_pieces(direct, _, stores, __):
    got, out = direct[0], stores[0].buf
    total = got[0].astype(F32)
    for k in range(1, 16):
        total = total + got[k].astype(F32)
    for k in range(8):
        out[k] = total[18 * k : 18 * k + 18]
    stores[0].send()


def add_last(direct, _, stores, __):
    got = direct[0]
    total = got[0]
    for k in range(1, 8):
        total = total + got[k]
    stores[0].buf[...] = total * (1.0 / 256.0)
    stores[0].send()


def middle(pars, loads, stores, _):
    (par,) = pars
    y2, x0, i_own, gx0, x2, y0, t_own, i_far, gy0 = loads
    gx, gy = stores
    x0()
    t_lane, iid = carried(y2()), column(lane_ids(i_own()))
    text = y2()[pl.ds(0, ROWS), :]
    gx0()
    for k, r in enumerate(HALVES):
        ids = slice(k * STEP, k * STEP + STEP)
        gx.buf[r, :] = gx0()[r, :] + nn(coef_of(par, x0()[r, :], iid[ids], text, t_lane), text)
        gx.send(k)
    x2(), y0()
    far, tid = lane_ids(i_far()), column(lane_ids(t_own()))
    gy0()
    for k, r in enumerate(HALVES):
        ids = slice(k * STEP, k * STEP + STEP)
        gy.buf[r, :] = gy0()[r, :] + nn(
            coef_of(par, y0()[r, :], tid[ids], x2()[...], far), x2()[...]
        )
        gy.send(k)


def fourth(pars, loads, stores, scratch):
    (par,) = pars
    a3, head, y3, x0, y0, i_own, t_own, gx0, gy0 = loads
    gx, gy = stores
    (half,) = scratch
    unit_images(a3(), head(), half)
    tiles(par, y3, a3, half, x0, y0, i_own, t_own, gx0, gy0, gx, gy)


def last_image(pars, loads, stores, _):
    (par,) = pars
    y4, x0, i_own, gx0, u0, head = loads
    (g_image,) = stores
    x0()
    t_lane, iid = carried(y4()), column(lane_ids(i_own()))
    text = y4()[pl.ds(0, ROWS), :]
    for k, r in enumerate(HALVES):
        ids = slice(k * STEP, k * STEP + STEP)
        grad = gx0()[r, :] + nn(coef_of(par, x0()[r, :], iid[ids], text, t_lane), text)
        g_image.buf[r, :] = nt(project_u(grad, u0()[r, :]), head()[...]).astype(BF16)
        g_image.send(k)


def last_text(pars, loads, stores, scratch):
    (par,) = pars
    a4, head, y0, t_own, gy0, text_in = loads
    (g_text,) = stores
    (half,) = scratch
    unit_images(a4(), head(), half)
    i_lane, tid = carried(a4()), column(lane_ids(t_own()))
    for k, r in enumerate(HALVES):
        ids = slice(k * STEP, k * STEP + STEP)
        grad = gy0()[r, :] + nn(coef_of(par, y0()[r, :], tid[ids], half[...], i_lane), half[...])
        t = text_in()[r, :].astype(F32)
        inv = inverse_norm(t)
        g_text.buf[r, :] = project(inv, grad, t * inv).astype(BF16)
        g_text.send(k)


BLOCK = ((ROWS, D), BF16)
SUMS = ((ROWS, D), F32)
TURNED = ((D, ROWS), BF16)
TRAVEL = ((SENT, D), BF16)


def per_device(image_feats, text_feats, head, image_ids, text_ids, log_scale, bias):
    core = lax.axis_index("c")
    par = jnp.stack([jnp.exp(log_scale[0]), bias[0]])
    ids_of = lambda block: (block, ROWS, 16)
    y0, a0 = run(
        prepare, [TRAVEL, TRAVEL],
        [text_feats, image_feats, text_ids.reshape(1, ROWS), image_ids.reshape(1, ROWS)],
    )
    y1, a1 = shifted(y0, 1), shifted(a0, -1)
    u0, x0, at0, gx, gy = run(first, [SUMS, BLOCK, TURNED, SUMS, SUMS], [a0, head, y0], [par], eager=2)
    y2, a2 = shifted(after(y1, gx), 1), shifted(after(a1, gx), -1)
    own_y = (y0, 0, ROWS)
    starts = jnp.stack([512 * (1 - core), 512 * core])
    piece = ((D, WIDE), F32)
    u1, x1, at1, gx, gy, near, away, mine = run(
        second, [SUMS, BLOCK, TURNED, SUMS, SUMS, SUMS, piece, piece],
        [a1, head, y1, x0, own_y, ids_of(a0), ids_of(y0), gx, gy, u0, at0],
        [par, starts], [BLOCK], eager=2,
    )
    y3, a3 = shifted(after(y2, gx), 1), shifted(after(a2, gx), -1)
    part = ((D // 2, WIDE), BF16)
    x2, low, high, mine = run(
        third, [BLOCK, part, part, piece],
        [a2, head, y2, x1, ids_of(a1), near, u1, at1, away, mine],
        [par, starts], [SUMS, TURNED, BLOCK, BLOCK], eager=2,
    )
    got = [lax.ppermute(half, "c", [(0, 1), (1, 0)]) for half in (low, high)]
    (pieces,) = run(to_pieces, [((16, 144, PART), BF16)], [mine], direct=got)
    spread = lax.all_to_all(pieces, ("y", "xl", "xh"), 0, 0)
    gx, gy = run(
        middle, [SUMS, SUMS],
        [y2, x0, ids_of(a0), gx, x2, own_y, ids_of(y0), ids_of(a2), after(gy, pieces, y3, a3)],
        [par], flops=10**11, eager=4,
    )
    y4, a4 = shifted(after(y3, mine), 1), shifted(after(a3, mine), -1)
    (total,) = run(add_pieces, [((8, 18, PART), F32)], [], direct=[after(spread, gx)])
    spread = lax.all_to_all(total, "z", 0, 0)
    gx, gy = run(
        fourth, [SUMS, SUMS],
        [a3, head, y3, x0, own_y, ids_of(a0), ids_of(y0), gx, after(gy, total)],
        [par], [BLOCK], flops=10**11, eager=2,
    )
    (grad_image,) = run(
        last_image, [BLOCK], [y4, x0, ids_of(a0), gx, u0, head], [par], flops=10**11, eager=3
    )
    (total,) = run(add_last, [((18, PART), F32)], [], direct=[after(spread, grad_image)])
    swap = [(0, 1), (1, 0)]
    other = lax.ppermute(total, "xh", swap)
    (grad_text,) = run(
        last_text, [BLOCK], [a4, head, own_y, ids_of(y0), after(gy, total), text_feats],
        [par], [BLOCK], flops=10**11, eager=2,
    )
    other = after(other, grad_text)
    even = lax.axis_index("xh") == 0
    low, high = jnp.where(even, total, other), jnp.where(even, other, total)
    wide = jnp.concatenate([low, high[:, 128:]], axis=1)
    other = lax.ppermute(wide, "c", swap)
    low, high = jnp.where(core == 0, wide, other), jnp.where(core == 0, other, wide)
    grad_head = jnp.concatenate([low, high[:, 128:]], axis=1)
    return grad_image, grad_text, grad_head


def solution(mesh):
    fine = Mesh(mesh.devices.reshape(4, 2, 8, 2, 2), AXES)
    placed = (P(AXES, None), P(AXES, None), P(), P(AXES), P(AXES), P(), P())
    return jax.shard_map(
        per_device,
        mesh=fine,
        in_specs=placed,
        out_specs=(P(AXES, None), P(AXES, None), P(CYCLE, None)),
        check_vma=False,
    )
```

```python
import jax
import jax.numpy as jnp
from jax import lax
from jax.experimental import pallas as pl
from jax.experimental.pallas import tpu as pltpu
from jax.sharding import Mesh, PartitionSpec as P

AXES = ("y", "xl", "z", "xh", "c")
CYCLE = ("y", "xl", "z")
F32 = jnp.float32
BF16 = jnp.bfloat16
D = 1152
ROWS = 512
SENT = 528
STEP = 256
WIDE = 640
PART = 384


def shifted(value, steps):
    count = lax.axis_size(CYCLE)
    return lax.ppermute(value, CYCLE, [(i, (i + steps) % count) for i in range(count)])


def after(value, *others):
    return lax.optimization_barrier((value,) + others)[0]


def nn(a, b):
    return jnp.dot(a, b, preferred_element_type=F32)


def nt(a, b):
    return lax.dot_general(a, b, (((1,), (1,)), ((), ())), preferred_element_type=F32)


class Load:
    def __init__(self, copy, buf):
        self.copy, self.buf, self.here, self.then = copy, buf, False, []

    def __call__(self):
        if not self.here:
            self.copy.wait()
            self.here = True
            for copy in self.then:
                copy.start()
        return self.buf


class Store:
    def __init__(self, out, buf, sems):
        self.out, self.buf, self.sems, self.sent = out, buf, sems, []

    def send(self, half=None):
        if half is None:
            copy = pltpu.make_async_copy(self.buf, self.out, self.sems.at[0])
        else:
            size = self.buf.shape[0] // 2
            rows = pl.ds(half * size, size)
            copy = pltpu.make_async_copy(self.buf.at[rows], self.out.at[rows], self.sems.at[half])
        copy.start()
        self.sent.append(copy)


def run(body, outs, ins, scalars=(), scratch=(), flops=0, vmem=56, direct=(), eager=99):
    ins = [i if isinstance(i, tuple) else (i, None, None) for i in ins]
    n_d, n_i, n_o = len(direct), len(ins), len(outs)
    n_s = len(scalars) + n_d

    def kernel(*refs):
        pars, refs = refs[:n_s], refs[n_s:]
        sources, refs = refs[:n_i], refs[n_i:]
        results, refs = refs[:n_o], refs[n_o:]
        in_bufs, refs = refs[:n_i], refs[n_i:]
        out_bufs, refs = refs[:n_o], refs[n_o:]
        in_sems, out_sems, extra = refs[0], refs[1], refs[2:]
        loads = []
        for k, (_, first, rows) in enumerate(ins):
            source = sources[k] if first is None else sources[k].at[pl.ds(first, rows)]
            copy = pltpu.make_async_copy(source, in_bufs[k], in_sems.at[k])
            loads.append(Load(copy, in_bufs[k]))
            if k < eager:
                copy.start()
            else:
                loads[eager - 1].then.append(copy)
        stores = [Store(results[k], out_bufs[k], out_sems.at[k]) for k in range(n_o)]
        body(pars, loads, stores, extra)
        for load in loads:
            load()
        for store in stores:
            for copy in store.sent:
                copy.wait()

    shapes = []
    for array, _, rows in ins:
        shape = array.shape if rows is None else (rows,) + array.shape[1:]
        shapes.append(pltpu.VMEM(shape, array.dtype))
    shapes += [pltpu.VMEM(s, t) for s, t in outs]
    shapes += [pltpu.SemaphoreType.DMA((max(n_i, 1),)), pltpu.SemaphoreType.DMA((n_o, 2))]
    shapes += [pltpu.VMEM(s, t) for s, t in scratch]
    return pl.pallas_call(
        kernel,
        out_shape=[jax.ShapeDtypeStruct(s, t) for s, t in outs],
        in_specs=[pl.BlockSpec(memory_space=pltpu.SMEM)] * len(scalars)
        + [pl.BlockSpec(memory_space=pltpu.VMEM)] * n_d
        + [pl.BlockSpec(memory_space=pl.ANY)] * n_i,
        out_specs=[pl.BlockSpec(memory_space=pl.ANY)] * n_o,
        scratch_shapes=shapes,
        compiler_params=pltpu.CompilerParams(vmem_limit_bytes=vmem * 2**20),
        cost_estimate=pl.CostEstimate(flops=flops, bytes_accessed=0, transcendentals=0),
    )(*scalars, *direct, *[i[0] for i in ins])


HALVES = [pl.ds(i * STEP, STEP) for i in range(ROWS // STEP)]


def inverse_norm(values):
    return lax.rsqrt(jnp.sum(values * values, axis=-1, keepdims=True) + 1e-06)


def lane_ids(pair):
    pair = pair[:, pl.ds(0, ROWS)].astype(F32)
    return pair[0:1] * 256.0 + pair[1:2]


def carried(block):
    return lane_ids(block.at[pl.ds(ROWS, 16)])


def column(lane):
    return jnp.broadcast_to(lane, (8, ROWS)).T[:, 0:1]


def coef_of(par, rows, row_ids, columns, column_ids):
    scale, offset = par[0], par[1]
    logits = scale * nt(rows, columns) + offset
    positive = (row_ids == column_ids).astype(F32)
    return (scale * (jax.nn.sigmoid(logits) - positive)).astype(BF16)


def unit_images(feats, head, half, u_out=None):
    for r in HALVES:
        u = nn(feats[r, :], head[...])
        half[r, :] = (u * inverse_norm(u)).astype(BF16)
        if u_out is not None:
            u_out[r, :] = u


def turn(feats, out):
    for k in range(D // 128):
        cols = pl.ds(k * 128, 128)
        out[cols, :] = feats[pl.ds(0, ROWS), cols].T


def project(inv, grad, x):
    return inv * (grad - x * jnp.sum(x * grad, axis=1, keepdims=True))


def project_u(grad, u):
    inv = inverse_norm(u)
    return project(inv, grad, u * inv).astype(BF16)


def prepare(_, loads, stores, __):
    text, image, text_lane, image_lane = loads
    text_out, image_out = stores
    image()
    text()
    for r in HALVES:
        image_out.buf[r, :] = image()[r, :]
    for load, out in ((image_lane, image_out), (text_lane, text_out)):
        if out is text_out:
            for r in HALVES:
                t = text()[r, :].astype(F32)
                out.buf[r, :] = (t * inverse_norm(t)).astype(BF16)
        out.buf[pl.ds(ROWS, 16), :] = jnp.zeros((16, D), BF16)
        row = lax.broadcasted_iota(jnp.int32, (16, ROWS), 0)
        ids = load()[...]
        high, low = (ids >> 8).astype(F32), (ids & 255).astype(F32)
        pair = jnp.where(row == 0, high, jnp.where(row == 1, low, 0.0))
        out.buf[pl.ds(ROWS, 16), pl.ds(0, ROWS)] = pair.astype(BF16)
        out.send()


def first(pars, loads, stores, _):
    (par,) = pars
    a0, head, y0 = loads
    u_out, half, a_t, gx, gy = stores
    unit_images(a0(), head(), half.buf, u_out.buf)
    u_out.send()
    half.send()
    t_lane, i_lane = carried(y0()), carried(a0())
    iid, tid = column(i_lane), column(t_lane)
    text, x = y0()[pl.ds(0, ROWS), :], half.buf
    for k, r in enumerate(HALVES):
        ids = slice(k * STEP, k * STEP + STEP)
        gx.buf[r, :] = nn(coef_of(par, x[r, :], iid[ids], text, t_lane), text)
        gy.buf[r, :] = nn(coef_of(par, y0()[r, :], tid[ids], x[...], i_lane), x[...])
        gx.send(k)
        gy.send(k)
    turn(a0(), a_t.buf)
    a_t.send()


def second(pars, loads, stores, scratch):
    par, starts = pars
    a1, head, y1, x0, y0, i_own, t_own, gx0, gy0, u0, at0 = loads
    u_out, half, a_t, gx, gy, near, away, mine = stores
    (g0,) = scratch
    unit_images(a1(), head(), half.buf, u_out.buf)
    u_out.send()
    half.send()
    tiles(par, y1, a1, half.buf, x0, y0, i_own, t_own, gx0, gy0, gx, gy)
    t_lane, ids1 = carried(y1()), column(carried(a1()))
    text = y1()[pl.ds(0, ROWS), :]
    u0()
    for k, r in enumerate(HALVES):
        ids = slice(k * STEP, k * STEP + STEP)
        near.buf[r, :] = nn(coef_of(par, half.buf[r, :], ids1[ids], text, t_lane), text)
        near.send(k)
        g0[r, :] = project_u(gx.buf[r, :], u0()[r, :])
    turn(a1(), a_t.buf)
    a_t.send()
    at0()
    for start, store in ((starts[0], away), (starts[1], mine)):
        cols = pl.ds(pl.multiple_of(start, 128), WIDE)
        for k in range(2):

            @pl.loop(2 * k, 2 * k + 2)
            def _(j):
                r = pl.ds(pl.multiple_of(j * 288, 288), 288)
                store.buf[r, :] = nn(at0()[r, :], g0[:, cols])

            store.send(k)


def tiles(par, y, a, x, x0, y0, i_own, t_own, gx0, gy0, gx, gy):
    t_lane, i_lane = carried(y()), carried(a())
    iid, tid = column(lane_ids(i_own())), column(lane_ids(t_own()))
    text = y()[pl.ds(0, ROWS), :]
    x0(), y0(), gx0(), gy0()
    for k, r in enumerate(HALVES):
        ids = slice(k * STEP, k * STEP + STEP)
        gx.buf[r, :] = gx0()[r, :] + nn(coef_of(par, x0()[r, :], iid[ids], text, t_lane), text)
        gy.buf[r, :] = gy0()[r, :] + nn(coef_of(par, y0()[r, :], tid[ids], x[...], i_lane), x[...])
        gx.send(k)
        gy.send(k)


def third(pars, loads, stores, scratch):
    par, starts = pars
    a2, head, y2, x1, i_near, near, u1, at1, away0, mine0 = loads
    half, low, high, mine = stores
    u2, at2, g1, g2 = scratch
    unit_images(a2(), head(), half.buf, u2)
    half.send()
    t_lane = carried(y2())
    ids1 = column(lane_ids(i_near()))
    ids2 = column(carried(a2()))
    text = y2()[pl.ds(0, ROWS), :]
    x1(), u1(), near()
    for k, r in enumerate(HALVES):
        ids = slice(k * STEP, k * STEP + STEP)
        grad = nn(coef_of(par, x1()[r, :], ids1[ids], text, t_lane), text)
        g1[r, :] = project_u(grad + near()[r, :], u1()[r, :])
        grad = nn(coef_of(par, half.buf[r, :], ids2[ids], text, t_lane), text)
        g2[r, :] = project_u(grad, u2[r, :])
    turn(a2(), at2)
    at1(), away0(), mine0()

    def summed(start, before, r):
        cols = pl.ds(pl.multiple_of(start, 128), WIDE)
        total = before()[r, :] + nn(at1()[r, :], g1[:, cols])
        return total + nn(at2[r, :], g2[:, cols])

    for i, store in enumerate((low, high)):

        @pl.loop(0, 2)
        def _(k):
            at = pl.multiple_of(k * 288, 288)
            rows = summed(starts[0], away0, pl.ds(at + 576 * i, 288))
            store.buf[pl.ds(at, 288), :] = rows.astype(BF16)

        store.send()
    for k in range(2):

        @pl.loop(2 * k, 2 * k + 2)
        def _(j):
            r = pl.ds(pl.multiple_of(j * 288, 288), 288)
            mine.buf[r, :] = summed(starts[1], mine0, r)

        mine.send(k)


def to_pieces(direct, loads, stores, __):
    mine, (low, high) = loads[0](), direct
    out = stores[0].buf
    for k in range(8):
        other = (low, high)[k // 4]
        s = pl.ds(144 * (k % 4), 144)
        total = (mine[pl.ds(144 * k, 144), :] + other[s, :].astype(F32)).astype(BF16)
        out[2 * k] = total[:, :PART]
        out[2 * k + 1] = total[:, 256 : 256 + PART]
        if k % 4 == 3:
            stores[0].send(k // 4)


def add_pieces(direct, _, stores, __):
    got, out = direct[0], stores[0].buf
    total = got[0].astype(F32)
    for k in range(1, 16):
        total = total + got[k].astype(F32)
    for k in range(8):
        out[k] = total[18 * k : 18 * k + 18]
    stores[0].send()


def add_last(direct, _, stores, __):
    got = direct[0]
    total = got[0]
    for k in range(1, 8):
        total = total + got[k]
    stores[0].buf[...] = total * (1.0 / 256.0)
    stores[0].send()


def middle(pars, loads, stores, _):
    (par,) = pars
    y2, x0, i_own, gx0, x2, y0, t_own, i_far, gy0 = loads
    gx, gy = stores
    x0()
    t_lane, iid = carried(y2()), column(lane_ids(i_own()))
    text = y2()[pl.ds(0, ROWS), :]
    gx0()
    for k, r in enumerate(HALVES):
        ids = slice(k * STEP, k * STEP + STEP)
        gx.buf[r, :] = gx0()[r, :] + nn(coef_of(par, x0()[r, :], iid[ids], text, t_lane), text)
        gx.send(k)
    x2(), y0()
    far, tid = lane_ids(i_far()), column(lane_ids(t_own()))
    gy0()
    for k, r in enumerate(HALVES):
        ids = slice(k * STEP, k * STEP + STEP)
        gy.buf[r, :] = gy0()[r, :] + nn(
            coef_of(par, y0()[r, :], tid[ids], x2()[...], far), x2()[...]
        )
        gy.send(k)


def fourth(pars, loads, stores, scratch):
    (par,) = pars
    a3, head, y3, x0, y0, i_own, t_own, gx0, gy0 = loads
    gx, gy = stores
    (half,) = scratch
    unit_images(a3(), head(), half)
    tiles(par, y3, a3, half, x0, y0, i_own, t_own, gx0, gy0, gx, gy)


def last(pars, loads, stores, scratch):
    (par,) = pars
    y4, x0, i_own, gx0, u0, head, a4, y0, t_own, gy0, text_in = loads
    g_image, g_text = stores
    (half,) = scratch
    x0()
    t_lane, iid = carried(y4()), column(lane_ids(i_own()))
    text = y4()[pl.ds(0, ROWS), :]
    for k, r in enumerate(HALVES):
        ids = slice(k * STEP, k * STEP + STEP)
        grad = gx0()[r, :] + nn(coef_of(par, x0()[r, :], iid[ids], text, t_lane), text)
        g_image.buf[r, :] = nt(project_u(grad, u0()[r, :]), head()[...]).astype(BF16)
        g_image.send(k)
    unit_images(a4(), head(), half)
    i_lane, tid = carried(a4()), column(lane_ids(t_own()))
    for k, r in enumerate(HALVES):
        ids = slice(k * STEP, k * STEP + STEP)
        grad = gy0()[r, :] + nn(coef_of(par, y0()[r, :], tid[ids], half[...], i_lane), half[...])
        t = text_in()[r, :].astype(F32)
        inv = inverse_norm(t)
        g_text.buf[r, :] = project(inv, grad, t * inv).astype(BF16)
        g_text.send(k)


BLOCK = ((ROWS, D), BF16)
SUMS = ((ROWS, D), F32)
TURNED = ((D, ROWS), BF16)
TRAVEL = ((SENT, D), BF16)


def per_device(image_feats, text_feats, head, image_ids, text_ids, log_scale, bias):
    core = lax.axis_index("c")
    par = jnp.stack([jnp.exp(log_scale[0]), bias[0]])
    ids_of = lambda block: (block, ROWS, 16)
    y0, a0 = run(
        prepare, [TRAVEL, TRAVEL],
        [text_feats, image_feats, text_ids.reshape(1, ROWS), image_ids.reshape(1, ROWS)],
    )
    y1, a1 = shifted(y0, 1), shifted(a0, -1)
    u0, x0, at0, gx, gy = run(first, [SUMS, BLOCK, TURNED, SUMS, SUMS], [a0, head, y0], [par], eager=2)
    y2, a2 = shifted(after(y1, gx), 1), shifted(after(a1, gx), -1)
    own_y = (y0, 0, ROWS)
    starts = jnp.stack([512 * (1 - core), 512 * core])
    piece = ((D, WIDE), F32)
    u1, x1, at1, gx, gy, near, away, mine = run(
        second, [SUMS, BLOCK, TURNED, SUMS, SUMS, SUMS, piece, piece],
        [a1, head, y1, x0, own_y, ids_of(a0), ids_of(y0), gx, gy, u0, at0],
        [par, starts], [BLOCK], eager=2,
    )
    y3, a3 = shifted(after(y2, gx), 1), shifted(after(a2, gx), -1)
    part = ((D // 2, WIDE), BF16)
    x2, low, high, mine = run(
        third, [BLOCK, part, part, piece],
        [a2, head, y2, x1, ids_of(a1), near, u1, at1, away, mine],
        [par, starts], [SUMS, TURNED, BLOCK, BLOCK], eager=2,
    )
    got = [lax.ppermute(half, "c", [(0, 1), (1, 0)]) for half in (low, high)]
    (pieces,) = run(to_pieces, [((16, 144, PART), BF16)], [mine], direct=got)
    spread = lax.all_to_all(pieces, ("y", "xl", "xh"), 0, 0)
    gx, gy = run(
        middle, [SUMS, SUMS],
        [y2, x0, ids_of(a0), gx, x2, own_y, ids_of(y0), ids_of(a2), after(gy, pieces, y3, a3)],
        [par], flops=10**11, eager=4,
    )
    y4, a4 = shifted(after(y3, spread), 1), shifted(after(a3, spread), -1)
    (total,) = run(add_pieces, [((8, 18, PART), F32)], [], direct=[after(spread, gx)])
    spread = lax.all_to_all(total, "z", 0, 0)
    gx, gy = run(
        fourth, [SUMS, SUMS],
        [a3, head, y3, x0, own_y, ids_of(a0), ids_of(y0), gx, after(gy, total)],
        [par], [BLOCK], flops=10**11, eager=2,
    )
    (total,) = run(add_last, [((18, PART), F32)], [], direct=[after(spread, gx)])
    swap = [(0, 1), (1, 0)]
    other = lax.ppermute(total, "xh", swap)
    grad_image, grad_text = run(
        last, [BLOCK, BLOCK],
        [y4, x0, ids_of(a0), gx, u0, head, a4, own_y, ids_of(y0), after(gy, total), text_feats],
        [par], [BLOCK], flops=10**11, eager=3,
    )
    other = after(other, grad_text)
    even = lax.axis_index("xh") == 0
    low, high = jnp.where(even, total, other), jnp.where(even, other, total)
    wide = jnp.concatenate([low, high[:, 128:]], axis=1)
    other = lax.ppermute(wide, "c", swap)
    low, high = jnp.where(core == 0, wide, other), jnp.where(core == 0, other, wide)
    grad_head = jnp.concatenate([low, high[:, 128:]], axis=1)
    return grad_image, grad_text, grad_head


def solution(mesh):
    fine = Mesh(mesh.devices.reshape(4, 2, 8, 2, 2), AXES)
    placed = (P(AXES, None), P(AXES, None), P(), P(AXES), P(AXES), P(), P())
    return jax.shard_map(
        per_device,
        mesh=fine,
        in_specs=placed,
        out_specs=(P(AXES, None), P(AXES, None), P(CYCLE, None)),
        check_vma=False,
    )
```

```python
import jax
import jax.numpy as jnp
from jax import lax
from jax.experimental import pallas as pl
from jax.experimental.pallas import tpu as pltpu
from jax.sharding import Mesh, PartitionSpec as P

AXES = ("y", "xl", "z", "xh", "c")
CYCLE = ("y", "xl", "z")
F32 = jnp.float32
BF16 = jnp.bfloat16
D = 1152
ROWS = 512
SENT = 528
STEP = 256
WIDE = 640
PART = 384


def shifted(value, steps):
    count = lax.axis_size(CYCLE)
    return lax.ppermute(value, CYCLE, [(i, (i + steps) % count) for i in range(count)])


def after(value, *others):
    return lax.optimization_barrier((value,) + others)[0]


def nn(a, b):
    return jnp.dot(a, b, preferred_element_type=F32)


def nt(a, b):
    return lax.dot_general(a, b, (((1,), (1,)), ((), ())), preferred_element_type=F32)


class Load:
    def __init__(self, copy, buf):
        self.copy, self.buf, self.here, self.then = copy, buf, False, []

    def __call__(self):
        if not self.here:
            self.copy.wait()
            self.here = True
            for copy in self.then:
                copy.start()
        return self.buf


class Store:
    def __init__(self, out, buf, sems):
        self.out, self.buf, self.sems, self.sent = out, buf, sems, []

    def send(self, half=None):
        if half is None:
            copy = pltpu.make_async_copy(self.buf, self.out, self.sems.at[0])
        else:
            size = self.buf.shape[0] // 2
            rows = pl.ds(half * size, size)
            copy = pltpu.make_async_copy(self.buf.at[rows], self.out.at[rows], self.sems.at[half])
        copy.start()
        self.sent.append(copy)


def run(body, outs, ins, scalars=(), scratch=(), flops=0, vmem=56, direct=(), eager=99):
    ins = [i if isinstance(i, tuple) else (i, None, None) for i in ins]
    n_d, n_i, n_o = len(direct), len(ins), len(outs)
    n_s = len(scalars) + n_d

    def kernel(*refs):
        pars, refs = refs[:n_s], refs[n_s:]
        sources, refs = refs[:n_i], refs[n_i:]
        results, refs = refs[:n_o], refs[n_o:]
        in_bufs, refs = refs[:n_i], refs[n_i:]
        out_bufs, refs = refs[:n_o], refs[n_o:]
        in_sems, out_sems, extra = refs[0], refs[1], refs[2:]
        loads = []
        for k, (_, first, rows) in enumerate(ins):
            source = sources[k] if first is None else sources[k].at[pl.ds(first, rows)]
            copy = pltpu.make_async_copy(source, in_bufs[k], in_sems.at[k])
            loads.append(Load(copy, in_bufs[k]))
            if k < eager:
                copy.start()
            else:
                loads[eager - 1].then.append(copy)
        stores = [Store(results[k], out_bufs[k], out_sems.at[k]) for k in range(n_o)]
        body(pars, loads, stores, extra)
        for load in loads:
            load()
        for store in stores:
            for copy in store.sent:
                copy.wait()

    shapes = []
    for array, _, rows in ins:
        shape = array.shape if rows is None else (rows,) + array.shape[1:]
        shapes.append(pltpu.VMEM(shape, array.dtype))
    shapes += [pltpu.VMEM(s, t) for s, t in outs]
    shapes += [pltpu.SemaphoreType.DMA((max(n_i, 1),)), pltpu.SemaphoreType.DMA((n_o, 2))]
    shapes += [pltpu.VMEM(s, t) for s, t in scratch]
    return pl.pallas_call(
        kernel,
        out_shape=[jax.ShapeDtypeStruct(s, t) for s, t in outs],
        in_specs=[pl.BlockSpec(memory_space=pltpu.SMEM)] * len(scalars)
        + [pl.BlockSpec(memory_space=pltpu.VMEM)] * n_d
        + [pl.BlockSpec(memory_space=pl.ANY)] * n_i,
        out_specs=[pl.BlockSpec(memory_space=pl.ANY)] * n_o,
        scratch_shapes=shapes,
        compiler_params=pltpu.CompilerParams(vmem_limit_bytes=vmem * 2**20),
        cost_estimate=pl.CostEstimate(flops=flops, bytes_accessed=0, transcendentals=0),
    )(*scalars, *direct, *[i[0] for i in ins])


HALVES = [pl.ds(i * STEP, STEP) for i in range(ROWS // STEP)]


def inverse_norm(values):
    return lax.rsqrt(jnp.sum(values * values, axis=-1, keepdims=True) + 1e-06)


def lane_ids(pair):
    pair = pair[:, pl.ds(0, ROWS)].astype(F32)
    return pair[0:1] * 256.0 + pair[1:2]


def carried(block):
    return lane_ids(block.at[pl.ds(ROWS, 16)])


def column(lane):
    return jnp.broadcast_to(lane, (8, ROWS)).T[:, 0:1]


def coef_of(par, rows, row_ids, columns, column_ids):
    scale, offset = par[0], par[1]
    logits = scale * nt(rows, columns) + offset
    positive = (row_ids == column_ids).astype(F32)
    return (scale * (jax.nn.sigmoid(logits) - positive)).astype(BF16)


def unit_images(feats, head, half, u_out=None):
    for r in HALVES:
        u = nn(feats[r, :], head[...])
        half[r, :] = (u * inverse_norm(u)).astype(BF16)
        if u_out is not None:
            u_out[r, :] = u


def turn(feats, out):
    for k in range(D // 128):
        cols = pl.ds(k * 128, 128)
        out[cols, :] = feats[pl.ds(0, ROWS), cols].T


def project(inv, grad, x):
    return inv * (grad - x * jnp.sum(x * grad, axis=1, keepdims=True))


def project_u(grad, u):
    inv = inverse_norm(u)
    return project(inv, grad, u * inv).astype(BF16)


def prepare(_, loads, stores, __):
    text, image, text_lane, image_lane = loads
    text_out, image_out = stores
    image()
    text()
    for r in HALVES:
        image_out.buf[r, :] = image()[r, :]
    for load, out in ((image_lane, image_out), (text_lane, text_out)):
        if out is text_out:
            for r in HALVES:
                t = text()[r, :].astype(F32)
                out.buf[r, :] = (t * inverse_norm(t)).astype(BF16)
        out.buf[pl.ds(ROWS, 16), :] = jnp.zeros((16, D), BF16)
        row = lax.broadcasted_iota(jnp.int32, (16, ROWS), 0)
        ids = load()[...]
        high, low = (ids >> 8).astype(F32), (ids & 255).astype(F32)
        pair = jnp.where(row == 0, high, jnp.where(row == 1, low, 0.0))
        out.buf[pl.ds(ROWS, 16), pl.ds(0, ROWS)] = pair.astype(BF16)
        out.send()


def first(pars, loads, stores, _):
    (par,) = pars
    a0, head, y0 = loads
    u_out, half, a_t, gx, gy = stores
    unit_images(a0(), head(), half.buf, u_out.buf)
    u_out.send()
    half.send()
    t_lane, i_lane = carried(y0()), carried(a0())
    iid, tid = column(i_lane), column(t_lane)
    text, x = y0()[pl.ds(0, ROWS), :], half.buf
    for k, r in enumerate(HALVES):
        ids = slice(k * STEP, k * STEP + STEP)
        gx.buf[r, :] = nn(coef_of(par, x[r, :], iid[ids], text, t_lane), text)
        gy.buf[r, :] = nn(coef_of(par, y0()[r, :], tid[ids], x[...], i_lane), x[...])
        gx.send(k)
        gy.send(k)
    turn(a0(), a_t.buf)
    a_t.send()


def second(pars, loads, stores, scratch):
    par, starts = pars
    a1, head, y1, x0, y0, i_own, t_own, gx0, gy0, u0, at0 = loads
    u_out, half, a_t, gx, gy, near, away, mine = stores
    (g0,) = scratch
    unit_images(a1(), head(), half.buf, u_out.buf)
    u_out.send()
    half.send()
    tiles(par, y1, a1, half.buf, x0, y0, i_own, t_own, gx0, gy0, gx, gy)
    t_lane, ids1 = carried(y1()), column(carried(a1()))
    text = y1()[pl.ds(0, ROWS), :]
    u0()
    for k, r in enumerate(HALVES):
        ids = slice(k * STEP, k * STEP + STEP)
        near.buf[r, :] = nn(coef_of(par, half.buf[r, :], ids1[ids], text, t_lane), text)
        near.send(k)
        g0[r, :] = project_u(gx.buf[r, :], u0()[r, :])
    turn(a1(), a_t.buf)
    a_t.send()
    at0()
    for start, store in ((starts[0], away), (starts[1], mine)):
        cols = pl.ds(pl.multiple_of(start, 128), WIDE)
        for k in range(2):

            @pl.loop(2 * k, 2 * k + 2)
            def _(j):
                r = pl.ds(pl.multiple_of(j * 288, 288), 288)
                store.buf[r, :] = nn(at0()[r, :], g0[:, cols])

            store.send(k)


def tiles(par, y, a, x, x0, y0, i_own, t_own, gx0, gy0, gx, gy):
    t_lane, i_lane = carried(y()), carried(a())
    iid, tid = column(lane_ids(i_own())), column(lane_ids(t_own()))
    text = y()[pl.ds(0, ROWS), :]
    x0(), y0(), gx0(), gy0()
    for k, r in enumerate(HALVES):
        ids = slice(k * STEP, k * STEP + STEP)
        gx.buf[r, :] = gx0()[r, :] + nn(coef_of(par, x0()[r, :], iid[ids], text, t_lane), text)
        gy.buf[r, :] = gy0()[r, :] + nn(coef_of(par, y0()[r, :], tid[ids], x[...], i_lane), x[...])
        gx.send(k)
        gy.send(k)


def third(pars, loads, stores, scratch):
    par, starts = pars
    a2, head, y2, x1, i_near, near, u1, at1, away0, mine0 = loads
    half, low, high, mine = stores
    u2, at2, g1, g2 = scratch
    unit_images(a2(), head(), half.buf, u2)
    half.send()
    t_lane = carried(y2())
    ids1 = column(lane_ids(i_near()))
    ids2 = column(carried(a2()))
    text = y2()[pl.ds(0, ROWS), :]
    x1(), u1(), near()
    for k, r in enumerate(HALVES):
        ids = slice(k * STEP, k * STEP + STEP)
        grad = nn(coef_of(par, x1()[r, :], ids1[ids], text, t_lane), text)
        g1[r, :] = project_u(grad + near()[r, :], u1()[r, :])
        grad = nn(coef_of(par, half.buf[r, :], ids2[ids], text, t_lane), text)
        g2[r, :] = project_u(grad, u2[r, :])
    turn(a2(), at2)
    at1(), away0(), mine0()

    def summed(start, before, r):
        cols = pl.ds(pl.multiple_of(start, 128), WIDE)
        total = before()[r, :] + nn(at1()[r, :], g1[:, cols])
        return total + nn(at2[r, :], g2[:, cols])

    for i, store in enumerate((low, high)):

        @pl.loop(0, 2)
        def _(k):
            at = pl.multiple_of(k * 288, 288)
            rows = summed(starts[0], away0, pl.ds(at + 576 * i, 288))
            store.buf[pl.ds(at, 288), :] = rows.astype(BF16)

        store.send()
    for k in range(2):

        @pl.loop(2 * k, 2 * k + 2)
        def _(j):
            r = pl.ds(pl.multiple_of(j * 288, 288), 288)
            mine.buf[r, :] = summed(starts[1], mine0, r).astype(BF16)

        mine.send(k)


def to_pieces(direct, loads, stores, __):
    mine, (low, high) = loads[0](), direct
    out = stores[0].buf
    for k in range(8):
        other = (low, high)[k // 4]
        s = pl.ds(144 * (k % 4), 144)
        total = mine[pl.ds(144 * k, 144), :].astype(F32) + other[s, :].astype(F32)
        total = total.astype(BF16)
        out[2 * k] = total[:, :PART]
        out[2 * k + 1] = total[:, 256 : 256 + PART]
        if k % 4 == 3:
            stores[0].send(k // 4)


def add_pieces(direct, _, stores, __):
    got, out = direct[0], stores[0].buf
    total = got[0].astype(F32)
    for k in range(1, 16):
        total = total + got[k].astype(F32)
    for k in range(8):
        out[k] = total[18 * k : 18 * k + 18]
    stores[0].send()


def add_last(direct, _, stores, __):
    got = direct[0]
    total = got[0]
    for k in range(1, 8):
        total = total + got[k]
    stores[0].buf[...] = total * (1.0 / 256.0)
    stores[0].send()


def middle(pars, loads, stores, _):
    (par,) = pars
    y2, x0, i_own, gx0 = loads
    (gx,) = stores
    x0()
    t_lane, iid = carried(y2()), column(lane_ids(i_own()))
    text = y2()[pl.ds(0, ROWS), :]
    gx0()
    for k, r in enumerate(HALVES):
        ids = slice(k * STEP, k * STEP + STEP)
        gx.buf[r, :] = gx0()[r, :] + nn(coef_of(par, x0()[r, :], iid[ids], text, t_lane), text)
        gx.send(k)


def fourth(pars, loads, stores, scratch):
    (par,) = pars
    a3, head, y3, x0, i_own, gx0, y0, t_own, x2, i_far, gy0 = loads
    gx, gy = stores
    (half,) = scratch
    unit_images(a3(), head(), half)
    t_lane, i_lane, far = carried(y3()), carried(a3()), lane_ids(i_far())
    iid, tid = column(lane_ids(i_own())), column(lane_ids(t_own()))
    text = y3()[pl.ds(0, ROWS), :]
    x0(), gx0()
    for k, r in enumerate(HALVES):
        ids = slice(k * STEP, k * STEP + STEP)
        gx.buf[r, :] = gx0()[r, :] + nn(coef_of(par, x0()[r, :], iid[ids], text, t_lane), text)
        gx.send(k)
    y0(), x2(), gy0()
    for k, r in enumerate(HALVES):
        ids = slice(k * STEP, k * STEP + STEP)
        total = gy0()[r, :] + nn(coef_of(par, y0()[r, :], tid[ids], x2()[...], far), x2()[...])
        total = total + nn(coef_of(par, y0()[r, :], tid[ids], half[...], i_lane), half[...])
        gy.buf[r, :] = total
        gy.send(k)


def last(pars, loads, stores, scratch):
    (par,) = pars
    y4, x0, i_own, gx0, u0, head, a4, y0, t_own, gy0, text_in = loads
    g_image, g_text = stores
    (half,) = scratch
    x0()
    t_lane, iid = carried(y4()), column(lane_ids(i_own()))
    text = y4()[pl.ds(0, ROWS), :]
    for k, r in enumerate(HALVES):
        ids = slice(k * STEP, k * STEP + STEP)
        grad = gx0()[r, :] + nn(coef_of(par, x0()[r, :], iid[ids], text, t_lane), text)
        g_image.buf[r, :] = nt(project_u(grad, u0()[r, :]), head()[...]).astype(BF16)
        g_image.send(k)
    unit_images(a4(), head(), half)
    i_lane, tid = carried(a4()), column(lane_ids(t_own()))
    for k, r in enumerate(HALVES):
        ids = slice(k * STEP, k * STEP + STEP)
        grad = gy0()[r, :] + nn(coef_of(par, y0()[r, :], tid[ids], half[...], i_lane), half[...])
        t = text_in()[r, :].astype(F32)
        inv = inverse_norm(t)
        g_text.buf[r, :] = project(inv, grad, t * inv).astype(BF16)
        g_text.send(k)


BLOCK = ((ROWS, D), BF16)
SUMS = ((ROWS, D), F32)
TURNED = ((D, ROWS), BF16)
TRAVEL = ((SENT, D), BF16)


def per_device(image_feats, text_feats, head, image_ids, text_ids, log_scale, bias):
    core = lax.axis_index("c")
    par = jnp.stack([jnp.exp(log_scale[0]), bias[0]])
    ids_of = lambda block: (block, ROWS, 16)
    y0, a0 = run(
        prepare, [TRAVEL, TRAVEL],
        [text_feats, image_feats, text_ids.reshape(1, ROWS), image_ids.reshape(1, ROWS)],
    )
    y1, a1 = shifted(y0, 1), shifted(a0, -1)
    u0, x0, at0, gx, gy = run(first, [SUMS, BLOCK, TURNED, SUMS, SUMS], [a0, head, y0], [par], eager=2)
    y2, a2 = shifted(after(y1, gx), 1), shifted(after(a1, gx), -1)
    own_y = (y0, 0, ROWS)
    starts = jnp.stack([512 * (1 - core), 512 * core])
    piece = ((D, WIDE), F32)
    u1, x1, at1, gx, gy, near, away, mine = run(
        second, [SUMS, BLOCK, TURNED, SUMS, SUMS, SUMS, piece, piece],
        [a1, head, y1, x0, own_y, ids_of(a0), ids_of(y0), gx, gy, u0, at0],
        [par, starts], [BLOCK], eager=2,
    )
    y3, a3 = shifted(after(y2, gx), 1), shifted(after(a2, gx), -1)
    part = ((D // 2, WIDE), BF16)
    x2, low, high, mine = run(
        third, [BLOCK, part, part, ((D, WIDE), BF16)],
        [a2, head, y2, x1, ids_of(a1), near, u1, at1, away, mine],
        [par, starts], [SUMS, TURNED, BLOCK, BLOCK], eager=2,
    )
    got = [lax.ppermute(half, "c", [(0, 1), (1, 0)]) for half in (low, high)]
    (pieces,) = run(to_pieces, [((16, 144, PART), BF16)], [mine], direct=got)
    spread = lax.all_to_all(pieces, ("y", "xl", "xh"), 0, 0)
    (gx,) = run(
        middle, [SUMS], [y2, x0, ids_of(a0), after(gx, pieces, y3, a3)],
        [par], flops=10**11, eager=2,
    )
    y4, a4 = shifted(after(y3, spread, gx), 1), shifted(after(a3, spread, gx), -1)
    (total,) = run(add_pieces, [((8, 18, PART), F32)], [], direct=[after(spread, gx)])
    spread = lax.all_to_all(total, "z", 0, 0)
    gx, gy = run(
        fourth, [SUMS, SUMS],
        [a3, head, y3, x0, ids_of(a0), gx, own_y, ids_of(y0), x2, ids_of(a2), after(gy, total)],
        [par], [BLOCK], flops=0, eager=2,
    )
    (total,) = run(add_last, [((18, PART), F32)], [], direct=[after(spread, gx)])
    swap = [(0, 1), (1, 0)]
    other = lax.ppermute(total, "xh", swap)
    grad_image, grad_text = run(
        last, [BLOCK, BLOCK],
        [y4, x0, ids_of(a0), gx, u0, head, a4, own_y, ids_of(y0), after(gy, total), text_feats],
        [par], [BLOCK], flops=10**11, eager=3,
    )
    other = after(other, grad_text)
    even = lax.axis_index("xh") == 0
    low, high = jnp.where(even, total, other), jnp.where(even, other, total)
    wide = jnp.concatenate([low, high[:, 128:]], axis=1)
    other = lax.ppermute(wide, "c", swap)
    low, high = jnp.where(core == 0, wide, other), jnp.where(core == 0, other, wide)
    grad_head = jnp.concatenate([low, high[:, 128:]], axis=1)
    return grad_image, grad_text, grad_head


def solution(mesh):
    fine = Mesh(mesh.devices.reshape(4, 2, 8, 2, 2), AXES)
    placed = (P(AXES, None), P(AXES, None), P(), P(AXES), P(AXES), P(), P())
    return jax.shard_map(
        per_device,
        mesh=fine,
        in_specs=placed,
        out_specs=(P(AXES, None), P(AXES, None), P(CYCLE, None)),
        check_vma=False,
    )
```

```python
import jax
import jax.numpy as jnp
from jax import lax
from jax.experimental import pallas as pl
from jax.experimental.pallas import tpu as pltpu
from jax.sharding import Mesh, PartitionSpec as P

AXES = ("y", "xl", "z", "xh", "c")
CYCLE = ("y", "xl", "z")
F32 = jnp.float32
BF16 = jnp.bfloat16
D = 1152
ROWS = 512
SENT = 528
STEP = 256
WIDE = 640
PART = 384


def shifted(value, steps):
    count = lax.axis_size(CYCLE)
    return lax.ppermute(value, CYCLE, [(i, (i + steps) % count) for i in range(count)])


def after(value, *others):
    return lax.optimization_barrier((value,) + others)[0]


def nn(a, b):
    return jnp.dot(a, b, preferred_element_type=F32)


def nt(a, b):
    return lax.dot_general(a, b, (((1,), (1,)), ((), ())), preferred_element_type=F32)


class Load:
    def __init__(self, copy, buf):
        self.copy, self.buf, self.here, self.then = copy, buf, False, []

    def __call__(self):
        if not self.here:
            self.copy.wait()
            self.here = True
            for copy in self.then:
                copy.start()
        return self.buf


class Store:
    def __init__(self, out, buf, sems):
        self.out, self.buf, self.sems, self.sent = out, buf, sems, []

    def send(self, half=None):
        if half is None:
            copy = pltpu.make_async_copy(self.buf, self.out, self.sems.at[0])
        else:
            size = self.buf.shape[0] // 2
            rows = pl.ds(half * size, size)
            copy = pltpu.make_async_copy(self.buf.at[rows], self.out.at[rows], self.sems.at[half])
        copy.start()
        self.sent.append(copy)


def run(body, outs, ins, scalars=(), scratch=(), flops=0, vmem=56, direct=(), eager=99):
    ins = [i if isinstance(i, tuple) else (i, None, None) for i in ins]
    n_d, n_i, n_o = len(direct), len(ins), len(outs)
    n_s = len(scalars) + n_d

    def kernel(*refs):
        pars, refs = refs[:n_s], refs[n_s:]
        sources, refs = refs[:n_i], refs[n_i:]
        results, refs = refs[:n_o], refs[n_o:]
        in_bufs, refs = refs[:n_i], refs[n_i:]
        out_bufs, refs = refs[:n_o], refs[n_o:]
        in_sems, out_sems, extra = refs[0], refs[1], refs[2:]
        loads = []
        for k, (_, first, rows) in enumerate(ins):
            source = sources[k] if first is None else sources[k].at[pl.ds(first, rows)]
            copy = pltpu.make_async_copy(source, in_bufs[k], in_sems.at[k])
            loads.append(Load(copy, in_bufs[k]))
            if k < eager:
                copy.start()
            else:
                loads[eager - 1].then.append(copy)
        stores = [Store(results[k], out_bufs[k], out_sems.at[k]) for k in range(n_o)]
        body(pars, loads, stores, extra)
        for load in loads:
            load()
        for store in stores:
            for copy in store.sent:
                copy.wait()

    shapes = []
    for array, _, rows in ins:
        shape = array.shape if rows is None else (rows,) + array.shape[1:]
        shapes.append(pltpu.VMEM(shape, array.dtype))
    shapes += [pltpu.VMEM(s, t) for s, t in outs]
    shapes += [pltpu.SemaphoreType.DMA((max(n_i, 1),)), pltpu.SemaphoreType.DMA((n_o, 2))]
    shapes += [pltpu.VMEM(s, t) for s, t in scratch]
    return pl.pallas_call(
        kernel,
        out_shape=[jax.ShapeDtypeStruct(s, t) for s, t in outs],
        in_specs=[pl.BlockSpec(memory_space=pltpu.SMEM)] * len(scalars)
        + [pl.BlockSpec(memory_space=pltpu.VMEM)] * n_d
        + [pl.BlockSpec(memory_space=pl.ANY)] * n_i,
        out_specs=[pl.BlockSpec(memory_space=pl.ANY)] * n_o,
        scratch_shapes=shapes,
        compiler_params=pltpu.CompilerParams(vmem_limit_bytes=vmem * 2**20),
        cost_estimate=pl.CostEstimate(flops=flops, bytes_accessed=0, transcendentals=0),
    )(*scalars, *direct, *[i[0] for i in ins])


HALVES = [pl.ds(i * STEP, STEP) for i in range(ROWS // STEP)]


def inverse_norm(values):
    return lax.rsqrt(jnp.sum(values * values, axis=-1, keepdims=True) + 1e-06)


def lane_ids(pair):
    pair = pair[:, pl.ds(0, ROWS)].astype(F32)
    return pair[0:1] * 256.0 + pair[1:2]


def carried(block):
    return lane_ids(block.at[pl.ds(ROWS, 16)])


def column(lane):
    return jnp.broadcast_to(lane, (8, ROWS)).T[:, 0:1]


def coef_of(par, rows, row_ids, columns, column_ids):
    scale, offset = par[0], par[1]
    logits = scale * nt(rows, columns) + offset
    positive = (row_ids == column_ids).astype(F32)
    return (scale * (jax.nn.sigmoid(logits) - positive)).astype(BF16)


def unit_images(feats, head, half, u_out=None):
    for r in HALVES:
        u = nn(feats[r, :], head[...])
        half[r, :] = (u * inverse_norm(u)).astype(BF16)
        if u_out is not None:
            u_out[r, :] = u


def turn(feats, out):
    for k in range(D // 128):
        cols = pl.ds(k * 128, 128)
        out[cols, :] = feats[pl.ds(0, ROWS), cols].T


def project(inv, grad, x):
    return inv * (grad - x * jnp.sum(x * grad, axis=1, keepdims=True))


def project_u(grad, u):
    inv = inverse_norm(u)
    return project(inv, grad, u * inv).astype(BF16)


def prepare(_, loads, stores, __):
    text, image, text_lane, image_lane = loads
    text_out, image_out = stores
    image()
    text()
    for r in HALVES:
        image_out.buf[r, :] = image()[r, :]
    for load, out in ((image_lane, image_out), (text_lane, text_out)):
        if out is text_out:
            for r in HALVES:
                t = text()[r, :].astype(F32)
                out.buf[r, :] = (t * inverse_norm(t)).astype(BF16)
        out.buf[pl.ds(ROWS, 16), :] = jnp.zeros((16, D), BF16)
        row = lax.broadcasted_iota(jnp.int32, (16, ROWS), 0)
        ids = load()[...]
        high, low = (ids >> 8).astype(F32), (ids & 255).astype(F32)
        pair = jnp.where(row == 0, high, jnp.where(row == 1, low, 0.0))
        out.buf[pl.ds(ROWS, 16), pl.ds(0, ROWS)] = pair.astype(BF16)
        out.send()


def first(pars, loads, stores, _):
    (par,) = pars
    a0, head, y0 = loads
    u_out, half, a_t, gx, gy = stores
    unit_images(a0(), head(), half.buf, u_out.buf)
    u_out.send()
    half.send()
    t_lane, i_lane = carried(y0()), carried(a0())
    iid, tid = column(i_lane), column(t_lane)
    text, x = y0()[pl.ds(0, ROWS), :], half.buf
    for k, r in enumerate(HALVES):
        ids = slice(k * STEP, k * STEP + STEP)
        gx.buf[r, :] = nn(coef_of(par, x[r, :], iid[ids], text, t_lane), text)
        gy.buf[r, :] = nn(coef_of(par, y0()[r, :], tid[ids], x[...], i_lane), x[...])
        gx.send(k)
        gy.send(k)
    turn(a0(), a_t.buf)
    a_t.send()


def second(pars, loads, stores, scratch):
    par, starts = pars
    a1, head, y1, x0, y0, i_own, t_own, gx0, gy0, u0, at0 = loads
    u_out, half, a_t, gx, gy, near, away, mine = stores
    (g0,) = scratch
    unit_images(a1(), head(), half.buf, u_out.buf)
    u_out.send()
    half.send()
    tiles(par, y1, a1, half.buf, x0, y0, i_own, t_own, gx0, gy0, gx, gy)
    t_lane, ids1 = carried(y1()), column(carried(a1()))
    text = y1()[pl.ds(0, ROWS), :]
    u0()
    for k, r in enumerate(HALVES):
        ids = slice(k * STEP, k * STEP + STEP)
        near.buf[r, :] = nn(coef_of(par, half.buf[r, :], ids1[ids], text, t_lane), text)
        near.send(k)
        g0[r, :] = project_u(gx.buf[r, :], u0()[r, :])
    turn(a1(), a_t.buf)
    a_t.send()
    at0()
    for start, store in ((starts[0], away), (starts[1], mine)):
        cols = pl.ds(pl.multiple_of(start, 128), WIDE)
        for k in range(2):

            @pl.loop(2 * k, 2 * k + 2)
            def _(j):
                r = pl.ds(pl.multiple_of(j * 288, 288), 288)
                store.buf[r, :] = nn(at0()[r, :], g0[:, cols])

            store.send(k)


def tiles(par, y, a, x, x0, y0, i_own, t_own, gx0, gy0, gx, gy):
    t_lane, i_lane = carried(y()), carried(a())
    iid, tid = column(lane_ids(i_own())), column(lane_ids(t_own()))
    text = y()[pl.ds(0, ROWS), :]
    x0(), y0(), gx0(), gy0()
    for k, r in enumerate(HALVES):
        ids = slice(k * STEP, k * STEP + STEP)
        gx.buf[r, :] = gx0()[r, :] + nn(coef_of(par, x0()[r, :], iid[ids], text, t_lane), text)
        gy.buf[r, :] = gy0()[r, :] + nn(coef_of(par, y0()[r, :], tid[ids], x[...], i_lane), x[...])
        gx.send(k)
        gy.send(k)


def third(pars, loads, stores, scratch):
    par, starts = pars
    a2, head, y2, x1, i_near, near, u1, at1, away0, mine0 = loads
    half, low, high, mine = stores
    u2, at2, g1, g2 = scratch
    unit_images(a2(), head(), half.buf, u2)
    half.send()
    t_lane = carried(y2())
    ids1 = column(lane_ids(i_near()))
    ids2 = column(carried(a2()))
    text = y2()[pl.ds(0, ROWS), :]
    x1(), u1(), near()
    for k, r in enumerate(HALVES):
        ids = slice(k * STEP, k * STEP + STEP)
        grad = nn(coef_of(par, x1()[r, :], ids1[ids], text, t_lane), text)
        g1[r, :] = project_u(grad + near()[r, :], u1()[r, :])
        grad = nn(coef_of(par, half.buf[r, :], ids2[ids], text, t_lane), text)
        g2[r, :] = project_u(grad, u2[r, :])
    turn(a2(), at2)
    at1(), away0(), mine0()

    def summed(start, before, r):
        cols = pl.ds(pl.multiple_of(start, 128), WIDE)
        total = before()[r, :] + nn(at1()[r, :], g1[:, cols])
        return total + nn(at2[r, :], g2[:, cols])

    for i, store in enumerate((low, high)):

        @pl.loop(0, 2)
        def _(k):
            at = pl.multiple_of(k * 288, 288)
            rows = summed(starts[0], away0, pl.ds(at + 576 * i, 288))
            store.buf[pl.ds(at, 288), :] = rows.astype(BF16)

        store.send()
    for k in range(2):

        @pl.loop(2 * k, 2 * k + 2)
        def _(j):
            r = pl.ds(pl.multiple_of(j * 288, 288), 288)
            mine.buf[r, :] = summed(starts[1], mine0, r).astype(BF16)

        mine.send(k)


def to_pieces(direct, loads, stores, __):
    mine, (low, high) = loads[0](), direct
    out = stores[0].buf
    for k in range(8):
        other = (low, high)[k // 4]
        s = pl.ds(144 * (k % 4), 144)
        total = mine[pl.ds(144 * k, 144), :].astype(F32) + other[s, :].astype(F32)
        total = total.astype(BF16)
        out[2 * k] = total[:, :PART]
        out[2 * k + 1] = total[:, 256 : 256 + PART]
        if k % 4 == 3:
            stores[0].send(k // 4)


def add_pieces(direct, _, stores, __):
    got, out = direct[0], stores[0].buf
    total = got[0].astype(F32)
    for k in range(1, 16):
        total = total + got[k].astype(F32)
    for k in range(8):
        out[k] = total[18 * k : 18 * k + 18]
    stores[0].send()


def add_last(direct, _, stores, __):
    got = direct[0]
    total = got[0]
    for k in range(1, 8):
        total = total + got[k]
    stores[0].buf[...] = total * (1.0 / 256.0)
    stores[0].send()


def fourth(pars, loads, stores, _):
    (par,) = pars
    a3, head, y0, t_own, x2, i_far, gy0, y2, x0, i_own, gx0, y3 = loads
    x3, gy, gx = stores
    unit_images(a3(), head(), x3.buf)
    x3.buf[pl.ds(ROWS, 16), :] = a3()[pl.ds(ROWS, 16), :]
    x3.send()
    i_lane, far, tid = carried(a3()), lane_ids(i_far()), column(lane_ids(t_own()))
    y0(), x2(), gy0()
    near = x3.buf[pl.ds(0, ROWS), :]
    for k, r in enumerate(HALVES):
        ids = slice(k * STEP, k * STEP + STEP)
        total = gy0()[r, :] + nn(coef_of(par, y0()[r, :], tid[ids], x2()[...], far), x2()[...])
        total = total + nn(coef_of(par, y0()[r, :], tid[ids], near, i_lane), near)
        gy.buf[r, :] = total
        gy.send(k)
    texts = [(y()[pl.ds(0, ROWS), :], carried(y())) for y in (y2, y3)]
    iid = column(lane_ids(i_own()))
    x0(), gx0()
    for k, r in enumerate(HALVES):
        ids = slice(k * STEP, k * STEP + STEP)
        total = gx0()[r, :]
        for text, lane in texts:
            total = total + nn(coef_of(par, x0()[r, :], iid[ids], text, lane), text)
        gx.buf[r, :] = total
        gx.send(k)


def last(pars, loads, stores, _):
    (par,) = pars
    y4, x0, i_own, gx0, u0, head, x4, y0, t_own, gy0, text_in = loads
    g_image, g_text = stores
    x0()
    t_lane, iid = carried(y4()), column(lane_ids(i_own()))
    text = y4()[pl.ds(0, ROWS), :]
    for k, r in enumerate(HALVES):
        ids = slice(k * STEP, k * STEP + STEP)
        grad = gx0()[r, :] + nn(coef_of(par, x0()[r, :], iid[ids], text, t_lane), text)
        g_image.buf[r, :] = nt(project_u(grad, u0()[r, :]), head()[...]).astype(BF16)
        g_image.send(k)
    i_lane, tid = carried(x4()), column(lane_ids(t_own()))
    image = x4()[pl.ds(0, ROWS), :]
    for k, r in enumerate(HALVES):
        ids = slice(k * STEP, k * STEP + STEP)
        grad = gy0()[r, :] + nn(coef_of(par, y0()[r, :], tid[ids], image, i_lane), image)
        t = text_in()[r, :].astype(F32)
        inv = inverse_norm(t)
        g_text.buf[r, :] = project(inv, grad, t * inv).astype(BF16)
        g_text.send(k)


BLOCK = ((ROWS, D), BF16)
SUMS = ((ROWS, D), F32)
TURNED = ((D, ROWS), BF16)
TRAVEL = ((SENT, D), BF16)


def per_device(image_feats, text_feats, head, image_ids, text_ids, log_scale, bias):
    core = lax.axis_index("c")
    par = jnp.stack([jnp.exp(log_scale[0]), bias[0]])
    ids_of = lambda block: (block, ROWS, 16)
    y0, a0 = run(
        prepare, [TRAVEL, TRAVEL],
        [text_feats, image_feats, text_ids.reshape(1, ROWS), image_ids.reshape(1, ROWS)],
    )
    y1, a1 = shifted(y0, 1), shifted(a0, -1)
    u0, x0, at0, gx, gy = run(first, [SUMS, BLOCK, TURNED, SUMS, SUMS], [a0, head, y0], [par], eager=2)
    y2, a2 = shifted(after(y1, gx), 1), shifted(after(a1, gx), -1)
    own_y = (y0, 0, ROWS)
    starts = jnp.stack([512 * (1 - core), 512 * core])
    piece = ((D, WIDE), F32)
    u1, x1, at1, gx, gy, near, away, mine = run(
        second, [SUMS, BLOCK, TURNED, SUMS, SUMS, SUMS, piece, piece],
        [a1, head, y1, x0, own_y, ids_of(a0), ids_of(y0), gx, gy, u0, at0],
        [par, starts], [BLOCK], eager=2,
    )
    y3, a3 = shifted(after(y2, gx), 1), shifted(after(a2, gx), -1)
    part = ((D // 2, WIDE), BF16)
    x2, low, high, mine = run(
        third, [BLOCK, part, part, ((D, WIDE), BF16)],
        [a2, head, y2, x1, ids_of(a1), near, u1, at1, away, mine],
        [par, starts], [SUMS, TURNED, BLOCK, BLOCK], eager=2,
    )
    got = [lax.ppermute(half, "c", [(0, 1), (1, 0)]) for half in (low, high)]
    (pieces,) = run(to_pieces, [((16, 144, PART), BF16)], [mine], direct=got)
    spread = lax.all_to_all(pieces, ("y", "xl", "xh"), 0, 0)
    x3, gy, gx = run(
        fourth, [TRAVEL, SUMS, SUMS],
        [a3, head, own_y, ids_of(y0), x2, ids_of(a2), gy, y2, x0, ids_of(a0),
         after(gx, pieces), y3],
        [par], flops=10**11, eager=2,
    )
    y4, x4 = shifted(after(y3, spread, gx), 1), shifted(after(x3, spread), -1)
    (total,) = run(add_pieces, [((8, 18, PART), F32)], [], direct=[after(spread, gx)])
    spread = lax.all_to_all(total, "z", 0, 0)
    grad_image, grad_text = run(
        last, [BLOCK, BLOCK],
        [y4, x0, ids_of(a0), gx, u0, head, x4, own_y, ids_of(y0), after(gy, total), text_feats],
        [par], flops=10**11, eager=4,
    )
    (total,) = run(add_last, [((18, PART), F32)], [], direct=[after(spread, grad_text)])
    parts = lax.all_gather(total, ("xh", "c"))
    grad_head = jnp.concatenate(
        [parts[0], parts[2][:, 128:], parts[1][:, 128:], parts[3][:, 128:]], axis=1
    )
    return grad_image, grad_text, grad_head


def solution(mesh):
    fine = Mesh(mesh.devices.reshape(4, 2, 8, 2, 2), AXES)
    placed = (P(AXES, None), P(AXES, None), P(), P(AXES), P(AXES), P(), P())
    return jax.shard_map(
        per_device,
        mesh=fine,
        in_specs=placed,
        out_specs=(P(AXES, None), P(AXES, None), P(CYCLE, None)),
        check_vma=False,
    )
```

```python
import jax
import jax.numpy as jnp
from jax import lax
from jax.experimental import pallas as pl
from jax.experimental.pallas import tpu as pltpu
from jax.sharding import Mesh, PartitionSpec as P

AXES = ("y", "xl", "z", "xh", "c")
CYCLE = ("y", "xl", "z")
F32 = jnp.float32
BF16 = jnp.bfloat16
D = 1152
ROWS = 512
SENT = 528
STEP = 256
WIDE = 640
PART = 384


def shifted(value, steps):
    count = lax.axis_size(CYCLE)
    return lax.ppermute(value, CYCLE, [(i, (i + steps) % count) for i in range(count)])


def after(value, *others):
    return lax.optimization_barrier((value,) + others)[0]


def nn(a, b):
    return jnp.dot(a, b, preferred_element_type=F32)


def nt(a, b):
    return lax.dot_general(a, b, (((1,), (1,)), ((), ())), preferred_element_type=F32)


class Load:
    def __init__(self, copy, buf):
        self.copy, self.buf, self.here, self.then = copy, buf, False, []

    def __call__(self):
        if not self.here:
            self.copy.wait()
            self.here = True
            for copy in self.then:
                copy.start()
        return self.buf


class Store:
    def __init__(self, out, buf, sems):
        self.out, self.buf, self.sems, self.sent = out, buf, sems, []

    def send(self, half=None):
        if half is None:
            copy = pltpu.make_async_copy(self.buf, self.out, self.sems.at[0])
        else:
            size = self.buf.shape[0] // 2
            rows = pl.ds(half * size, size)
            copy = pltpu.make_async_copy(self.buf.at[rows], self.out.at[rows], self.sems.at[half])
        copy.start()
        self.sent.append(copy)


def run(body, outs, ins, scalars=(), scratch=(), flops=0, vmem=56, direct=(), eager=99):
    ins = [i if isinstance(i, tuple) else (i, None, None) for i in ins]
    n_d, n_i, n_o = len(direct), len(ins), len(outs)
    n_s = len(scalars) + n_d

    def kernel(*refs):
        pars, refs = refs[:n_s], refs[n_s:]
        sources, refs = refs[:n_i], refs[n_i:]
        results, refs = refs[:n_o], refs[n_o:]
        in_bufs, refs = refs[:n_i], refs[n_i:]
        out_bufs, refs = refs[:n_o], refs[n_o:]
        in_sems, out_sems, extra = refs[0], refs[1], refs[2:]
        loads = []
        for k, (_, first, rows) in enumerate(ins):
            source = sources[k] if first is None else sources[k].at[pl.ds(first, rows)]
            copy = pltpu.make_async_copy(source, in_bufs[k], in_sems.at[k])
            loads.append(Load(copy, in_bufs[k]))
            if k < eager:
                copy.start()
            else:
                loads[eager - 1].then.append(copy)
        stores = [Store(results[k], out_bufs[k], out_sems.at[k]) for k in range(n_o)]
        body(pars, loads, stores, extra)
        for load in loads:
            load()
        for store in stores:
            for copy in store.sent:
                copy.wait()

    shapes = []
    for array, _, rows in ins:
        shape = array.shape if rows is None else (rows,) + array.shape[1:]
        shapes.append(pltpu.VMEM(shape, array.dtype))
    shapes += [pltpu.VMEM(s, t) for s, t in outs]
    shapes += [pltpu.SemaphoreType.DMA((max(n_i, 1),)), pltpu.SemaphoreType.DMA((n_o, 2))]
    shapes += [pltpu.VMEM(s, t) for s, t in scratch]
    return pl.pallas_call(
        kernel,
        out_shape=[jax.ShapeDtypeStruct(s, t) for s, t in outs],
        in_specs=[pl.BlockSpec(memory_space=pltpu.SMEM)] * len(scalars)
        + [pl.BlockSpec(memory_space=pltpu.VMEM)] * n_d
        + [pl.BlockSpec(memory_space=pl.ANY)] * n_i,
        out_specs=[pl.BlockSpec(memory_space=pl.ANY)] * n_o,
        scratch_shapes=shapes,
        compiler_params=pltpu.CompilerParams(vmem_limit_bytes=vmem * 2**20),
        cost_estimate=pl.CostEstimate(flops=flops, bytes_accessed=0, transcendentals=0),
    )(*scalars, *direct, *[i[0] for i in ins])


HALVES = [pl.ds(i * STEP, STEP) for i in range(ROWS // STEP)]


def inverse_norm(values):
    return lax.rsqrt(jnp.sum(values * values, axis=-1, keepdims=True) + 1e-06)


def lane_ids(pair):
    pair = pair[:, pl.ds(0, ROWS)].astype(F32)
    return pair[0:1] * 256.0 + pair[1:2]


def carried(block):
    return lane_ids(block.at[pl.ds(ROWS, 16)])


def column(lane):
    return jnp.broadcast_to(lane, (8, ROWS)).T[:, 0:1]


def coef_of(par, rows, row_ids, columns, column_ids):
    scale, offset = par[0], par[1]
    logits = scale * nt(rows, columns) + offset
    positive = (row_ids == column_ids).astype(F32)
    return (scale * (jax.nn.sigmoid(logits) - positive)).astype(BF16)


def unit_images(feats, head, half, u_out=None):
    for r in HALVES:
        u = nn(feats[r, :], head[...])
        half[r, :] = (u * inverse_norm(u)).astype(BF16)
        if u_out is not None:
            u_out[r, :] = u


def turn(feats, out):
    for k in range(D // 128):
        cols = pl.ds(k * 128, 128)
        out[cols, :] = feats[pl.ds(0, ROWS), cols].T


def project(inv, grad, x):
    return inv * (grad - x * jnp.sum(x * grad, axis=1, keepdims=True))


def project_u(grad, u):
    inv = inverse_norm(u)
    return project(inv, grad, u * inv).astype(BF16)


def prepare(_, loads, stores, __):
    text, image, text_lane, image_lane = loads
    text_out, image_out = stores
    image()
    text()
    for r in HALVES:
        image_out.buf[r, :] = image()[r, :]
    for load, out in ((image_lane, image_out), (text_lane, text_out)):
        if out is text_out:
            for r in HALVES:
                t = text()[r, :].astype(F32)
                out.buf[r, :] = (t * inverse_norm(t)).astype(BF16)
        out.buf[pl.ds(ROWS, 16), :] = jnp.zeros((16, D), BF16)
        row = lax.broadcasted_iota(jnp.int32, (16, ROWS), 0)
        ids = load()[...]
        high, low = (ids >> 8).astype(F32), (ids & 255).astype(F32)
        pair = jnp.where(row == 0, high, jnp.where(row == 1, low, 0.0))
        out.buf[pl.ds(ROWS, 16), pl.ds(0, ROWS)] = pair.astype(BF16)
        out.send()


def first(pars, loads, stores, _):
    (par,) = pars
    a0, head, y0 = loads
    u_out, half, a_t, gx, gy = stores
    unit_images(a0(), head(), half.buf, u_out.buf)
    u_out.send()
    half.send()
    t_lane, i_lane = carried(y0()), carried(a0())
    iid, tid = column(i_lane), column(t_lane)
    text, x = y0()[pl.ds(0, ROWS), :], half.buf
    for k, r in enumerate(HALVES):
        ids = slice(k * STEP, k * STEP + STEP)
        gx.buf[r, :] = nn(coef_of(par, x[r, :], iid[ids], text, t_lane), text)
        gy.buf[r, :] = nn(coef_of(par, y0()[r, :], tid[ids], x[...], i_lane), x[...])
        gx.send(k)
        gy.send(k)
    turn(a0(), a_t.buf)
    a_t.send()


def second(pars, loads, stores, scratch):
    par, starts = pars
    a1, head, y1, x0, y0, i_own, t_own, gx0, gy0, u0, at0 = loads
    u_out, half, a_t, gx, gy, near, away, mine = stores
    (g0,) = scratch
    unit_images(a1(), head(), half.buf, u_out.buf)
    u_out.send()
    half.send()
    tiles(par, y1, a1, half.buf, x0, y0, i_own, t_own, gx0, gy0, gx, gy)
    t_lane, ids1 = carried(y1()), column(carried(a1()))
    text = y1()[pl.ds(0, ROWS), :]
    u0()
    for k, r in enumerate(HALVES):
        ids = slice(k * STEP, k * STEP + STEP)
        near.buf[r, :] = nn(coef_of(par, half.buf[r, :], ids1[ids], text, t_lane), text)
        near.send(k)
        g0[r, :] = project_u(gx.buf[r, :], u0()[r, :])
    turn(a1(), a_t.buf)
    a_t.send()
    at0()
    for start, store in ((starts[0], away), (starts[1], mine)):
        cols = pl.ds(pl.multiple_of(start, 128), WIDE)
        for k in range(2):

            @pl.loop(2 * k, 2 * k + 2)
            def _(j):
                r = pl.ds(pl.multiple_of(j * 288, 288), 288)
                store.buf[r, :] = nn(at0()[r, :], g0[:, cols])

            store.send(k)


def tiles(par, y, a, x, x0, y0, i_own, t_own, gx0, gy0, gx, gy):
    t_lane, i_lane = carried(y()), carried(a())
    iid, tid = column(lane_ids(i_own())), column(lane_ids(t_own()))
    text = y()[pl.ds(0, ROWS), :]
    x0(), y0(), gx0(), gy0()
    for k, r in enumerate(HALVES):
        ids = slice(k * STEP, k * STEP + STEP)
        gx.buf[r, :] = gx0()[r, :] + nn(coef_of(par, x0()[r, :], iid[ids], text, t_lane), text)
        gy.buf[r, :] = gy0()[r, :] + nn(coef_of(par, y0()[r, :], tid[ids], x[...], i_lane), x[...])
        gx.send(k)
        gy.send(k)


def third(pars, loads, stores, scratch):
    par, starts = pars
    a2, head, y2, x1, i_near, near, u1, at1, away0, mine0 = loads
    half, low, high, mine = stores
    u2, at2, g1, g2 = scratch
    unit_images(a2(), head(), half.buf, u2)
    half.send()
    t_lane = carried(y2())
    ids1 = column(lane_ids(i_near()))
    ids2 = column(carried(a2()))
    text = y2()[pl.ds(0, ROWS), :]
    x1(), u1(), near()
    for k, r in enumerate(HALVES):
        ids = slice(k * STEP, k * STEP + STEP)
        grad = nn(coef_of(par, x1()[r, :], ids1[ids], text, t_lane), text)
        g1[r, :] = project_u(grad + near()[r, :], u1()[r, :])
        grad = nn(coef_of(par, half.buf[r, :], ids2[ids], text, t_lane), text)
        g2[r, :] = project_u(grad, u2[r, :])
    turn(a2(), at2)
    at1(), away0(), mine0()

    def summed(start, before, r):
        cols = pl.ds(pl.multiple_of(start, 128), WIDE)
        total = before()[r, :] + nn(at1()[r, :], g1[:, cols])
        return total + nn(at2[r, :], g2[:, cols])

    for i, store in enumerate((low, high)):

        @pl.loop(0, 2)
        def _(k):
            at = pl.multiple_of(k * 288, 288)
            rows = summed(starts[0], away0, pl.ds(at + 576 * i, 288))
            store.buf[pl.ds(at, 288), :] = rows.astype(BF16)

        store.send()
    for k in range(2):

        @pl.loop(2 * k, 2 * k + 2)
        def _(j):
            r = pl.ds(pl.multiple_of(j * 288, 288), 288)
            mine.buf[r, :] = summed(starts[1], mine0, r).astype(BF16)

        mine.send(k)


def to_pieces(direct, loads, stores, __):
    mine, (low, high) = loads[0](), direct
    out = stores[0].buf
    for k in range(8):
        other = (low, high)[k // 4]
        s = pl.ds(144 * (k % 4), 144)
        total = mine[pl.ds(144 * k, 144), :].astype(F32) + other[s, :].astype(F32)
        total = total.astype(BF16)
        out[2 * k] = total[:, :PART]
        out[2 * k + 1] = total[:, 256 : 256 + PART]
        if k % 4 == 3:
            stores[0].send(k // 4)


def add_pieces(direct, _, stores, __):
    got, out = direct[0], stores[0].buf
    total = got[0].astype(F32)
    for k in range(1, 16):
        total = total + got[k].astype(F32)
    for k in range(8):
        out[k] = total[18 * k : 18 * k + 18]
    stores[0].send()


def add_last(direct, _, stores, __):
    got = direct[0]
    total = got[0]
    for k in range(1, 8):
        total = total + got[k]
    stores[0].buf[...] = total * (1.0 / 256.0)
    stores[0].send()


def split(rows, tail, low, high):
    low.buf[pl.ds(0, STEP), :] = rows[pl.ds(0, STEP), :]
    low.buf[pl.ds(STEP, 16), :] = tail[pl.ds(ROWS, 16), :]
    low.send()
    high.buf[...] = rows[pl.ds(STEP, STEP), :]
    high.send()


def fourth(pars, loads, stores, scratch):
    (par,) = pars
    a3, head, y0, t_own, x2, i_far, gy0, y2, x0, i_own, gx0, y3 = loads
    x_low, x_high, y_low, y_high, gy, gx = stores
    (x3,) = scratch
    unit_images(a3(), head(), x3)
    split(x3, a3(), x_low, x_high)
    i_lane, far, tid = carried(a3()), lane_ids(i_far()), column(lane_ids(t_own()))
    y0(), x2(), gy0()
    near = x3[...]
    for k, r in enumerate(HALVES):
        ids = slice(k * STEP, k * STEP + STEP)
        total = gy0()[r, :] + nn(coef_of(par, y0()[r, :], tid[ids], x2()[...], far), x2()[...])
        total = total + nn(coef_of(par, y0()[r, :], tid[ids], near, i_lane), near)
        gy.buf[r, :] = total
        gy.send(k)
    split(y3(), y3(), y_low, y_high)
    texts = [(y()[pl.ds(0, ROWS), :], carried(y())) for y in (y2, y3)]
    iid = column(lane_ids(i_own()))
    x0(), gx0()
    for k, r in enumerate(HALVES):
        ids = slice(k * STEP, k * STEP + STEP)
        total = gx0()[r, :]
        for text, lane in texts:
            total = total + nn(coef_of(par, x0()[r, :], iid[ids], text, lane), text)
        gx.buf[r, :] = total
        gx.send(k)


def last_low(pars, loads, stores, _):
    (par,) = pars
    y4, x0, i_own, gx0, x4, y0, t_own, gy0 = loads
    gx, gy = stores
    for far, own, own_ids, before, out in ((y4, x0, i_own, gx0, gx), (x4, y0, t_own, gy0, gy)):
        lane = lane_ids(far().at[pl.ds(STEP, 16)])[:, :STEP]
        ids = column(lane_ids(own_ids()))
        rows = far()[pl.ds(0, STEP), :]
        own(), before()
        for k, r in enumerate(HALVES):
            part = coef_of(par, own()[r, :], ids[k * STEP : k * STEP + STEP], rows, lane)
            out.buf[r, :] = before()[r, :] + nn(part, rows)
            out.send(k)


def last(pars, loads, stores, _):
    (par,) = pars
    y4, x0, i_own, t_far, gx0, u0, head, x4, y0, t_own, i_far, gy0, text_in = loads
    g_image, g_text = stores
    x0()
    t_lane, iid = lane_ids(t_far())[:, STEP:], column(lane_ids(i_own()))
    text = y4()[...]
    for k, r in enumerate(HALVES):
        ids = slice(k * STEP, k * STEP + STEP)
        grad = gx0()[r, :] + nn(coef_of(par, x0()[r, :], iid[ids], text, t_lane), text)
        g_image.buf[r, :] = nt(project_u(grad, u0()[r, :]), head()[...]).astype(BF16)
        g_image.send(k)
    i_lane, tid = lane_ids(i_far())[:, STEP:], column(lane_ids(t_own()))
    image = x4()[...]
    for k, r in enumerate(HALVES):
        ids = slice(k * STEP, k * STEP + STEP)
        grad = gy0()[r, :] + nn(coef_of(par, y0()[r, :], tid[ids], image, i_lane), image)
        t = text_in()[r, :].astype(F32)
        inv = inverse_norm(t)
        g_text.buf[r, :] = project(inv, grad, t * inv).astype(BF16)
        g_text.send(k)


BLOCK = ((ROWS, D), BF16)
SUMS = ((ROWS, D), F32)
TURNED = ((D, ROWS), BF16)
TRAVEL = ((SENT, D), BF16)


def per_device(image_feats, text_feats, head, image_ids, text_ids, log_scale, bias):
    core = lax.axis_index("c")
    par = jnp.stack([jnp.exp(log_scale[0]), bias[0]])
    ids_of = lambda block: (block, ROWS, 16)
    y0, a0 = run(
        prepare, [TRAVEL, TRAVEL],
        [text_feats, image_feats, text_ids.reshape(1, ROWS), image_ids.reshape(1, ROWS)],
    )
    y1, a1 = shifted(y0, 1), shifted(a0, -1)
    u0, x0, at0, gx, gy = run(first, [SUMS, BLOCK, TURNED, SUMS, SUMS], [a0, head, y0], [par], eager=2)
    y2, a2 = shifted(after(y1, gx), 1), shifted(after(a1, gx), -1)
    own_y = (y0, 0, ROWS)
    starts = jnp.stack([512 * (1 - core), 512 * core])
    piece = ((D, WIDE), F32)
    u1, x1, at1, gx, gy, near, away, mine = run(
        second, [SUMS, BLOCK, TURNED, SUMS, SUMS, SUMS, piece, piece],
        [a1, head, y1, x0, own_y, ids_of(a0), ids_of(y0), gx, gy, u0, at0],
        [par, starts], [BLOCK], eager=2,
    )
    y3, a3 = shifted(after(y2, gx), 1), shifted(after(a2, gx), -1)
    part = ((D // 2, WIDE), BF16)
    x2, low, high, mine = run(
        third, [BLOCK, part, part, ((D, WIDE), BF16)],
        [a2, head, y2, x1, ids_of(a1), near, u1, at1, away, mine],
        [par, starts], [SUMS, TURNED, BLOCK, BLOCK], eager=2,
    )
    got = [lax.ppermute(half, "c", [(0, 1), (1, 0)]) for half in (low, high)]
    (pieces,) = run(to_pieces, [((16, 144, PART), BF16)], [mine], direct=got)
    spread = lax.all_to_all(pieces, ("y", "xl", "xh"), 0, 0)
    low, high = ((STEP + 16, D), BF16), ((STEP, D), BF16)
    x_low, x_high, y_low, y_high, gy, gx = run(
        fourth, [low, high, low, high, SUMS, SUMS],
        [a3, head, own_y, ids_of(y0), x2, ids_of(a2), gy, y2, x0, ids_of(a0),
         after(gx, pieces), y3],
        [par], [BLOCK], flops=10**11, eager=2,
    )
    y_low, x_low = shifted(after(y_low, spread), 1), shifted(after(x_low, spread), -1)
    (total,) = run(add_pieces, [((8, 18, PART), F32)], [], direct=[after(spread, gx)])
    spread = lax.all_to_all(total, "z", 0, 0)
    y_high, x_high = shifted(after(y_high, total), 1), shifted(after(x_high, total), -1)
    gx, gy = run(
        last_low, [SUMS, SUMS],
        [y_low, x0, ids_of(a0), gx, x_low, own_y, ids_of(y0), after(gy, total)],
        [par], flops=10**11, eager=4,
    )
    (total,) = run(add_last, [((18, PART), F32)], [], direct=[after(spread, gx)])
    parts = lax.all_gather(total, ("xh", "c"))
    tail = lambda block: (block, STEP, 16)
    grad_image, grad_text = run(
        last, [BLOCK, BLOCK],
        [y_high, x0, ids_of(a0), tail(y_low), gx, u0, head, x_high, own_y, ids_of(y0),
         tail(x_low), after(gy, parts), text_feats],
        [par], flops=10**11, eager=4,
    )
    grad_head = jnp.concatenate(
        [parts[0], parts[2][:, 128:], parts[1][:, 128:], parts[3][:, 128:]], axis=1
    )
    return grad_image, grad_text, grad_head


def solution(mesh):
    fine = Mesh(mesh.devices.reshape(4, 2, 8, 2, 2), AXES)
    placed = (P(AXES, None), P(AXES, None), P(), P(AXES), P(AXES), P(), P())
    return jax.shard_map(
        per_device,
        mesh=fine,
        in_specs=placed,
        out_specs=(P(AXES, None), P(AXES, None), P(CYCLE, None)),
        check_vma=False,
    )
```

```python
import jax
import jax.numpy as jnp
from jax import lax
from jax.experimental import pallas as pl
from jax.experimental.pallas import tpu as pltpu
from jax.sharding import Mesh, PartitionSpec as P

AXES = ("y", "xl", "z", "xh", "c")
CYCLE = ("y", "xl", "z")
F32 = jnp.float32
BF16 = jnp.bfloat16
D = 1152
ROWS = 512
SENT = 528
STEP = 256
WIDE = 640
PART = 384


def shifted(value, steps):
    count = lax.axis_size(CYCLE)
    return lax.ppermute(value, CYCLE, [(i, (i + steps) % count) for i in range(count)])


def after(value, *others):
    return lax.optimization_barrier((value,) + others)[0]


def nn(a, b):
    return jnp.dot(a, b, preferred_element_type=F32)


def nt(a, b):
    return lax.dot_general(a, b, (((1,), (1,)), ((), ())), preferred_element_type=F32)


class Load:
    def __init__(self, copy, buf):
        self.copy, self.buf, self.here, self.then = copy, buf, False, []

    def __call__(self):
        if not self.here:
            self.copy.wait()
            self.here = True
            for copy in self.then:
                copy.start()
        return self.buf


class Store:
    def __init__(self, out, buf, sems):
        self.out, self.buf, self.sems, self.sent = out, buf, sems, []

    def send(self, half=None):
        if half is None:
            copy = pltpu.make_async_copy(self.buf, self.out, self.sems.at[0])
        else:
            size = self.buf.shape[0] // 2
            rows = pl.ds(half * size, size)
            copy = pltpu.make_async_copy(self.buf.at[rows], self.out.at[rows], self.sems.at[half])
        copy.start()
        self.sent.append(copy)


def run(body, outs, ins, scalars=(), scratch=(), flops=0, vmem=56, direct=(), eager=99):
    ins = [i if isinstance(i, tuple) else (i, None, None) for i in ins]
    n_d, n_i, n_o = len(direct), len(ins), len(outs)
    n_s = len(scalars) + n_d

    def kernel(*refs):
        pars, refs = refs[:n_s], refs[n_s:]
        sources, refs = refs[:n_i], refs[n_i:]
        results, refs = refs[:n_o], refs[n_o:]
        in_bufs, refs = refs[:n_i], refs[n_i:]
        out_bufs, refs = refs[:n_o], refs[n_o:]
        in_sems, out_sems, extra = refs[0], refs[1], refs[2:]
        loads = []
        for k, (_, first, rows) in enumerate(ins):
            source = sources[k] if first is None else sources[k].at[pl.ds(first, rows)]
            copy = pltpu.make_async_copy(source, in_bufs[k], in_sems.at[k])
            loads.append(Load(copy, in_bufs[k]))
            if k < eager:
                copy.start()
            else:
                loads[eager - 1].then.append(copy)
        stores = [Store(results[k], out_bufs[k], out_sems.at[k]) for k in range(n_o)]
        body(pars, loads, stores, extra)
        for load in loads:
            load()
        for store in stores:
            for copy in store.sent:
                copy.wait()

    shapes = []
    for array, _, rows in ins:
        shape = array.shape if rows is None else (rows,) + array.shape[1:]
        shapes.append(pltpu.VMEM(shape, array.dtype))
    shapes += [pltpu.VMEM(s, t) for s, t in outs]
    shapes += [pltpu.SemaphoreType.DMA((max(n_i, 1),)), pltpu.SemaphoreType.DMA((n_o, 2))]
    shapes += [pltpu.VMEM(s, t) for s, t in scratch]
    return pl.pallas_call(
        kernel,
        out_shape=[jax.ShapeDtypeStruct(s, t) for s, t in outs],
        in_specs=[pl.BlockSpec(memory_space=pltpu.SMEM)] * len(scalars)
        + [pl.BlockSpec(memory_space=pltpu.VMEM)] * n_d
        + [pl.BlockSpec(memory_space=pl.ANY)] * n_i,
        out_specs=[pl.BlockSpec(memory_space=pl.ANY)] * n_o,
        scratch_shapes=shapes,
        compiler_params=pltpu.CompilerParams(vmem_limit_bytes=vmem * 2**20),
        cost_estimate=pl.CostEstimate(flops=flops, bytes_accessed=0, transcendentals=0),
    )(*scalars, *direct, *[i[0] for i in ins])


HALVES = [pl.ds(i * STEP, STEP) for i in range(ROWS // STEP)]


def inverse_norm(values):
    return lax.rsqrt(jnp.sum(values * values, axis=-1, keepdims=True) + 1e-06)


def lane_ids(pair):
    pair = pair[:, pl.ds(0, ROWS)].astype(F32)
    return pair[0:1] * 256.0 + pair[1:2]


def carried(block):
    return lane_ids(block.at[pl.ds(ROWS, 16)])


def column(lane):
    return jnp.broadcast_to(lane, (8, ROWS)).T[:, 0:1]


def coef_of(par, rows, row_ids, columns, column_ids):
    scale, offset = par[0], par[1]
    logits = scale * nt(rows, columns) + offset
    positive = (row_ids == column_ids).astype(F32)
    return (scale * (jax.nn.sigmoid(logits) - positive)).astype(BF16)


def unit_images(feats, head, half, u_out=None):
    for r in HALVES:
        u = nn(feats[r, :], head[...])
        half[r, :] = (u * inverse_norm(u)).astype(BF16)
        if u_out is not None:
            u_out[r, :] = u


def turn(feats, out):
    for k in range(D // 128):
        cols = pl.ds(k * 128, 128)
        out[cols, :] = feats[pl.ds(0, ROWS), cols].T


def project(inv, grad, x):
    return inv * (grad - x * jnp.sum(x * grad, axis=1, keepdims=True))


def project_u(grad, u):
    inv = inverse_norm(u)
    return project(inv, grad, u * inv).astype(BF16)


def prepare(_, loads, stores, __):
    text, image, text_lane, image_lane = loads
    text_out, image_out = stores
    image()
    text()
    for r in HALVES:
        image_out.buf[r, :] = image()[r, :]
    for load, out in ((image_lane, image_out), (text_lane, text_out)):
        if out is text_out:
            for r in HALVES:
                t = text()[r, :].astype(F32)
                out.buf[r, :] = (t * inverse_norm(t)).astype(BF16)
        out.buf[pl.ds(ROWS, 16), :] = jnp.zeros((16, D), BF16)
        row = lax.broadcasted_iota(jnp.int32, (16, ROWS), 0)
        ids = load()[...]
        high, low = (ids >> 8).astype(F32), (ids & 255).astype(F32)
        pair = jnp.where(row == 0, high, jnp.where(row == 1, low, 0.0))
        out.buf[pl.ds(ROWS, 16), pl.ds(0, ROWS)] = pair.astype(BF16)
        out.send()


def first(pars, loads, stores, _):
    (par,) = pars
    a0, head, y0 = loads
    u_out, half, a_t, gx, gy = stores
    unit_images(a0(), head(), half.buf, u_out.buf)
    u_out.send()
    half.send()
    t_lane, i_lane = carried(y0()), carried(a0())
    iid, tid = column(i_lane), column(t_lane)
    text, x = y0()[pl.ds(0, ROWS), :], half.buf
    for k, r in enumerate(HALVES):
        ids = slice(k * STEP, k * STEP + STEP)
        gx.buf[r, :] = nn(coef_of(par, x[r, :], iid[ids], text, t_lane), text)
        gy.buf[r, :] = nn(coef_of(par, y0()[r, :], tid[ids], x[...], i_lane), x[...])
        gx.send(k)
        gy.send(k)
    turn(a0(), a_t.buf)
    a_t.send()


def second(pars, loads, stores, scratch):
    par, starts = pars
    a1, head, y1, x0, y0, i_own, t_own, gx0, gy0, u0, at0 = loads
    u_out, half, a_t, gx, gy, near, away, mine = stores
    (g0,) = scratch
    unit_images(a1(), head(), half.buf, u_out.buf)
    u_out.send()
    half.send()
    tiles(par, y1, a1, half.buf, x0, y0, i_own, t_own, gx0, gy0, gx, gy)
    t_lane, ids1 = carried(y1()), column(carried(a1()))
    text = y1()[pl.ds(0, ROWS), :]
    u0()
    for k, r in enumerate(HALVES):
        ids = slice(k * STEP, k * STEP + STEP)
        near.buf[r, :] = nn(coef_of(par, half.buf[r, :], ids1[ids], text, t_lane), text)
        near.send(k)
        g0[r, :] = project_u(gx.buf[r, :], u0()[r, :])
    turn(a1(), a_t.buf)
    a_t.send()
    at0()
    for start, store in ((starts[0], away), (starts[1], mine)):
        cols = pl.ds(pl.multiple_of(start, 128), WIDE)
        for k in range(2):

            @pl.loop(2 * k, 2 * k + 2)
            def _(j):
                r = pl.ds(pl.multiple_of(j * 288, 288), 288)
                store.buf[r, :] = nn(at0()[r, :], g0[:, cols])

            store.send(k)


def tiles(par, y, a, x, x0, y0, i_own, t_own, gx0, gy0, gx, gy):
    t_lane, i_lane = carried(y()), carried(a())
    iid, tid = column(lane_ids(i_own())), column(lane_ids(t_own()))
    text = y()[pl.ds(0, ROWS), :]
    x0(), y0(), gx0(), gy0()
    for k, r in enumerate(HALVES):
        ids = slice(k * STEP, k * STEP + STEP)
        gx.buf[r, :] = gx0()[r, :] + nn(coef_of(par, x0()[r, :], iid[ids], text, t_lane), text)
        gy.buf[r, :] = gy0()[r, :] + nn(coef_of(par, y0()[r, :], tid[ids], x[...], i_lane), x[...])
        gx.send(k)
        gy.send(k)


def third(pars, loads, stores, scratch):
    par, starts = pars
    a2, head, y2, x1, i_near, near, u1, at1, away0, mine0 = loads
    half, low, high, mine = stores
    u2, at2, g1, g2 = scratch
    unit_images(a2(), head(), half.buf, u2)
    half.send()
    t_lane = carried(y2())
    ids1 = column(lane_ids(i_near()))
    ids2 = column(carried(a2()))
    text = y2()[pl.ds(0, ROWS), :]
    x1(), u1(), near()
    for k, r in enumerate(HALVES):
        ids = slice(k * STEP, k * STEP + STEP)
        grad = nn(coef_of(par, x1()[r, :], ids1[ids], text, t_lane), text)
        g1[r, :] = project_u(grad + near()[r, :], u1()[r, :])
        grad = nn(coef_of(par, half.buf[r, :], ids2[ids], text, t_lane), text)
        g2[r, :] = project_u(grad, u2[r, :])
    turn(a2(), at2)
    at1(), away0(), mine0()

    def summed(start, before, r):
        cols = pl.ds(pl.multiple_of(start, 128), WIDE)
        total = before()[r, :] + nn(at1()[r, :], g1[:, cols])
        return total + nn(at2[r, :], g2[:, cols])

    for i, store in enumerate((low, high)):

        @pl.loop(0, 2)
        def _(k):
            at = pl.multiple_of(k * 288, 288)
            rows = summed(starts[0], away0, pl.ds(at + 576 * i, 288))
            store.buf[pl.ds(at, 288), :] = rows.astype(BF16)

        store.send()
    for k in range(2):

        @pl.loop(2 * k, 2 * k + 2)
        def _(j):
            r = pl.ds(pl.multiple_of(j * 288, 288), 288)
            mine.buf[r, :] = summed(starts[1], mine0, r).astype(BF16)

        mine.send(k)


def to_pieces(direct, loads, stores, __):
    mine, (low, high) = loads[0](), direct
    out = stores[0].buf
    for k in range(8):
        other = (low, high)[k // 4]
        s = pl.ds(144 * (k % 4), 144)
        total = mine[pl.ds(144 * k, 144), :].astype(F32) + other[s, :].astype(F32)
        total = total.astype(BF16)
        out[2 * k] = total[:, :PART]
        out[2 * k + 1] = total[:, 256 : 256 + PART]
        if k % 4 == 3:
            stores[0].send(k // 4)


def add_pieces(direct, _, stores, __):
    got, out = direct[0], stores[0].buf
    total = got[0].astype(F32)
    for k in range(1, 16):
        total = total + got[k].astype(F32)
    for k in range(8):
        out[k] = total[18 * k : 18 * k + 18]
    stores[0].send()


def add_last(direct, _, stores, __):
    got = direct[0]
    total = got[0]
    for k in range(1, 8):
        total = total + got[k]
    stores[0].buf[...] = total * (1.0 / 256.0)
    stores[0].send()


def split(rows, tail, low, high):
    low.buf[pl.ds(0, STEP), :] = rows[pl.ds(0, STEP), :]
    low.buf[pl.ds(STEP, 16), :] = tail[pl.ds(ROWS, 16), :]
    low.send()
    high.buf[...] = rows[pl.ds(STEP, STEP), :]
    high.send()


def fourth(pars, loads, stores, scratch):
    (par,) = pars
    a3, head, y0, t_own, x2, i_far, gy0, y2, x0, i_own, gx0, y3 = loads
    x_low, x_high, y_low, y_high, gy, gx = stores
    (x3,) = scratch
    unit_images(a3(), head(), x3)
    split(x3, a3(), x_low, x_high)
    i_lane, far, tid = carried(a3()), lane_ids(i_far()), column(lane_ids(t_own()))
    y0(), x2(), gy0()
    near = x3[...]
    for k, r in enumerate(HALVES):
        ids = slice(k * STEP, k * STEP + STEP)
        total = gy0()[r, :] + nn(coef_of(par, y0()[r, :], tid[ids], x2()[...], far), x2()[...])
        total = total + nn(coef_of(par, y0()[r, :], tid[ids], near, i_lane), near)
        gy.buf[r, :] = total
        gy.send(k)
    split(y3(), y3(), y_low, y_high)
    texts = [(y()[pl.ds(0, ROWS), :], carried(y())) for y in (y2, y3)]
    iid = column(lane_ids(i_own()))
    x0(), gx0()
    for k, r in enumerate(HALVES):
        ids = slice(k * STEP, k * STEP + STEP)
        total = gx0()[r, :]
        for text, lane in texts:
            total = total + nn(coef_of(par, x0()[r, :], iid[ids], text, lane), text)
        gx.buf[r, :] = total
        gx.send(k)


def last(pars, loads, stores, _):
    (par,) = pars
    y_low, x0, i_own, gx0, y_high, u0, head, x_low, y0, t_own, gy0, x_high, text_in = loads
    g_image, g_text = stores

    def both(low, high):
        lanes = lane_ids(low().at[pl.ds(STEP, 16)])
        rows = low()[pl.ds(0, STEP), :], high()[...]
        return (rows[0], lanes[:, :STEP]), (rows[1], lanes[:, STEP:])

    x0()
    texts, iid = both(y_low, y_high), column(lane_ids(i_own()))
    for k, r in enumerate(HALVES):
        ids = slice(k * STEP, k * STEP + STEP)
        grad = gx0()[r, :]
        for text, lane in texts:
            grad = grad + nn(coef_of(par, x0()[r, :], iid[ids], text, lane), text)
        g_image.buf[r, :] = nt(project_u(grad, u0()[r, :]), head()[...]).astype(BF16)
        g_image.send(k)
    images, tid = both(x_low, x_high), column(lane_ids(t_own()))
    for k, r in enumerate(HALVES):
        ids = slice(k * STEP, k * STEP + STEP)
        grad = gy0()[r, :]
        for image, lane in images:
            grad = grad + nn(coef_of(par, y0()[r, :], tid[ids], image, lane), image)
        t = text_in()[r, :].astype(F32)
        inv = inverse_norm(t)
        g_text.buf[r, :] = project(inv, grad, t * inv).astype(BF16)
        g_text.send(k)


BLOCK = ((ROWS, D), BF16)
SUMS = ((ROWS, D), F32)
TURNED = ((D, ROWS), BF16)
TRAVEL = ((SENT, D), BF16)


def per_device(image_feats, text_feats, head, image_ids, text_ids, log_scale, bias):
    core = lax.axis_index("c")
    par = jnp.stack([jnp.exp(log_scale[0]), bias[0]])
    ids_of = lambda block: (block, ROWS, 16)
    y0, a0 = run(
        prepare, [TRAVEL, TRAVEL],
        [text_feats, image_feats, text_ids.reshape(1, ROWS), image_ids.reshape(1, ROWS)],
    )
    y1, a1 = shifted(y0, 1), shifted(a0, -1)
    u0, x0, at0, gx, gy = run(first, [SUMS, BLOCK, TURNED, SUMS, SUMS], [a0, head, y0], [par], eager=2)
    y2, a2 = shifted(after(y1, gx), 1), shifted(after(a1, gx), -1)
    own_y = (y0, 0, ROWS)
    starts = jnp.stack([512 * (1 - core), 512 * core])
    piece = ((D, WIDE), F32)
    u1, x1, at1, gx, gy, near, away, mine = run(
        second, [SUMS, BLOCK, TURNED, SUMS, SUMS, SUMS, piece, piece],
        [a1, head, y1, x0, own_y, ids_of(a0), ids_of(y0), gx, gy, u0, at0],
        [par, starts], [BLOCK], eager=2,
    )
    y3, a3 = shifted(after(y2, gx), 1), shifted(after(a2, gx), -1)
    part = ((D // 2, WIDE), BF16)
    x2, low, high, mine = run(
        third, [BLOCK, part, part, ((D, WIDE), BF16)],
        [a2, head, y2, x1, ids_of(a1), near, u1, at1, away, mine],
        [par, starts], [SUMS, TURNED, BLOCK, BLOCK], eager=2,
    )
    got = [lax.ppermute(half, "c", [(0, 1), (1, 0)]) for half in (low, high)]
    (pieces,) = run(to_pieces, [((16, 144, PART), BF16)], [mine], direct=got)
    spread = lax.all_to_all(pieces, ("y", "xl", "xh"), 0, 0)
    low, high = ((STEP + 16, D), BF16), ((STEP, D), BF16)
    x_low, x_high, y_low, y_high, gy, gx = run(
        fourth, [low, high, low, high, SUMS, SUMS],
        [a3, head, own_y, ids_of(y0), x2, ids_of(a2), gy, y2, x0, ids_of(a0),
         after(gx, pieces), y3],
        [par], [BLOCK], flops=10**11, eager=2,
    )
    y_low, x_low = shifted(after(y_low, spread), 1), shifted(after(x_low, spread), -1)
    (total,) = run(add_pieces, [((8, 18, PART), F32)], [], direct=[after(spread, gx)])
    spread = lax.all_to_all(total, "z", 0, 0)
    y_high, x_high = shifted(after(y_high, total), 1), shifted(after(x_high, total), -1)
    (total,) = run(
        add_last, [((18, PART), F32)], [], direct=[after(spread, y_low, x_low)], flops=10**11
    )
    parts = lax.all_gather(total, ("xh", "c"))
    grad_image, grad_text = run(
        last, [BLOCK, BLOCK],
        [y_low, x0, ids_of(a0), gx, y_high, u0, head, x_low, own_y, ids_of(y0),
         after(gy, parts), x_high, text_feats],
        [par], flops=10**11, eager=5,
    )
    grad_head = jnp.concatenate(
        [parts[0], parts[2][:, 128:], parts[1][:, 128:], parts[3][:, 128:]], axis=1
    )
    return grad_image, grad_text, grad_head


def solution(mesh):
    fine = Mesh(mesh.devices.reshape(4, 2, 8, 2, 2), AXES)
    placed = (P(AXES, None), P(AXES, None), P(), P(AXES), P(AXES), P(), P())
    return jax.shard_map(
        per_device,
        mesh=fine,
        in_specs=placed,
        out_specs=(P(AXES, None), P(AXES, None), P(CYCLE, None)),
        check_vma=False,
    )
```

```python
import jax
import jax.numpy as jnp
from jax import lax
from jax.experimental import pallas as pl
from jax.experimental.pallas import tpu as pltpu
from jax.sharding import Mesh, PartitionSpec as P

AXES = ("y", "xl", "z", "xh", "c")
CYCLE = ("y", "xl", "z")
F32 = jnp.float32
BF16 = jnp.bfloat16
D = 1152
ROWS = 512
SENT = 528
STEP = 256
WIDE = 640
PART = 384


def shifted(value, steps):
    count = lax.axis_size(CYCLE)
    return lax.ppermute(value, CYCLE, [(i, (i + steps) % count) for i in range(count)])


def after(value, *others):
    return lax.optimization_barrier((value,) + others)[0]


def nn(a, b):
    return jnp.dot(a, b, preferred_element_type=F32)


def nt(a, b):
    return lax.dot_general(a, b, (((1,), (1,)), ((), ())), preferred_element_type=F32)


class Load:
    def __init__(self, copy, buf):
        self.copy, self.buf, self.here, self.then = copy, buf, False, []

    def __call__(self):
        if not self.here:
            self.copy.wait()
            self.here = True
            for copy in self.then:
                copy.start()
        return self.buf


class Store:
    def __init__(self, out, buf, sems):
        self.out, self.buf, self.sems, self.sent = out, buf, sems, []

    def send(self, half=None):
        if half is None:
            copy = pltpu.make_async_copy(self.buf, self.out, self.sems.at[0])
        else:
            size = self.buf.shape[0] // 2
            rows = pl.ds(half * size, size)
            copy = pltpu.make_async_copy(self.buf.at[rows], self.out.at[rows], self.sems.at[half])
        copy.start()
        self.sent.append(copy)


def run(body, outs, ins, scalars=(), scratch=(), flops=0, vmem=56, direct=(), eager=99):
    ins = [i if isinstance(i, tuple) else (i, None, None) for i in ins]
    n_d, n_i, n_o = len(direct), len(ins), len(outs)
    n_s = len(scalars) + n_d

    def kernel(*refs):
        pars, refs = refs[:n_s], refs[n_s:]
        sources, refs = refs[:n_i], refs[n_i:]
        results, refs = refs[:n_o], refs[n_o:]
        in_bufs, refs = refs[:n_i], refs[n_i:]
        out_bufs, refs = refs[:n_o], refs[n_o:]
        in_sems, out_sems, extra = refs[0], refs[1], refs[2:]
        loads = []
        for k, (_, first, rows) in enumerate(ins):
            source = sources[k] if first is None else sources[k].at[pl.ds(first, rows)]
            copy = pltpu.make_async_copy(source, in_bufs[k], in_sems.at[k])
            loads.append(Load(copy, in_bufs[k]))
            if k < eager:
                copy.start()
            else:
                loads[eager - 1].then.append(copy)
        stores = [Store(results[k], out_bufs[k], out_sems.at[k]) for k in range(n_o)]
        body(pars, loads, stores, extra)
        for load in loads:
            load()
        for store in stores:
            for copy in store.sent:
                copy.wait()

    shapes = []
    for array, _, rows in ins:
        shape = array.shape if rows is None else (rows,) + array.shape[1:]
        shapes.append(pltpu.VMEM(shape, array.dtype))
    shapes += [pltpu.VMEM(s, t) for s, t in outs]
    shapes += [pltpu.SemaphoreType.DMA((max(n_i, 1),)), pltpu.SemaphoreType.DMA((n_o, 2))]
    shapes += [pltpu.VMEM(s, t) for s, t in scratch]
    return pl.pallas_call(
        kernel,
        out_shape=[jax.ShapeDtypeStruct(s, t) for s, t in outs],
        in_specs=[pl.BlockSpec(memory_space=pltpu.SMEM)] * len(scalars)
        + [pl.BlockSpec(memory_space=pltpu.VMEM)] * n_d
        + [pl.BlockSpec(memory_space=pl.ANY)] * n_i,
        out_specs=[pl.BlockSpec(memory_space=pl.ANY)] * n_o,
        scratch_shapes=shapes,
        compiler_params=pltpu.CompilerParams(vmem_limit_bytes=vmem * 2**20),
        cost_estimate=pl.CostEstimate(flops=flops, bytes_accessed=0, transcendentals=0),
    )(*scalars, *direct, *[i[0] for i in ins])


HALVES = [pl.ds(i * STEP, STEP) for i in range(ROWS // STEP)]


def inverse_norm(values):
    return lax.rsqrt(jnp.sum(values * values, axis=-1, keepdims=True) + 1e-06)


def lane_ids(pair):
    pair = pair[:, pl.ds(0, ROWS)].astype(F32)
    return pair[0:1] * 256.0 + pair[1:2]


def carried(block):
    return lane_ids(block.at[pl.ds(ROWS, 16)])


def column(lane):
    return jnp.broadcast_to(lane, (8, ROWS)).T[:, 0:1]


def coef_of(par, rows, row_ids, columns, column_ids):
    scale, offset = par[0], par[1]
    logits = scale * nt(rows, columns) + offset
    positive = (row_ids == column_ids).astype(F32)
    return (scale * (jax.nn.sigmoid(logits) - positive)).astype(BF16)


def unit_images(feats, head, half, u_out=None):
    for r in HALVES:
        u = nn(feats[r, :], head[...])
        half[r, :] = (u * inverse_norm(u)).astype(BF16)
        if u_out is not None:
            u_out[r, :] = u


def turn(feats, out):
    for k in range(D // 128):
        cols = pl.ds(k * 128, 128)
        out[cols, :] = feats[pl.ds(0, ROWS), cols].T


def project(inv, grad, x):
    return inv * (grad - x * jnp.sum(x * grad, axis=1, keepdims=True))


def project_u(grad, u):
    inv = inverse_norm(u)
    return project(inv, grad, u * inv).astype(BF16)


def prepare(_, loads, stores, __):
    text, image, text_lane, image_lane = loads
    text_out, image_out = stores
    image()
    text()
    for r in HALVES:
        image_out.buf[r, :] = image()[r, :]
    for load, out in ((image_lane, image_out), (text_lane, text_out)):
        if out is text_out:
            for r in HALVES:
                t = text()[r, :].astype(F32)
                out.buf[r, :] = (t * inverse_norm(t)).astype(BF16)
        out.buf[pl.ds(ROWS, 16), :] = jnp.zeros((16, D), BF16)
        row = lax.broadcasted_iota(jnp.int32, (16, ROWS), 0)
        ids = load()[...]
        high, low = (ids >> 8).astype(F32), (ids & 255).astype(F32)
        pair = jnp.where(row == 0, high, jnp.where(row == 1, low, 0.0))
        out.buf[pl.ds(ROWS, 16), pl.ds(0, ROWS)] = pair.astype(BF16)
        out.send()


def first(pars, loads, stores, _):
    (par,) = pars
    a0, head, y0 = loads
    u_out, half, a_t, gx, gy = stores
    unit_images(a0(), head(), half.buf, u_out.buf)
    u_out.send()
    half.send()
    t_lane, i_lane = carried(y0()), carried(a0())
    iid, tid = column(i_lane), column(t_lane)
    text, x = y0()[pl.ds(0, ROWS), :], half.buf
    for k, r in enumerate(HALVES):
        ids = slice(k * STEP, k * STEP + STEP)
        gx.buf[r, :] = nn(coef_of(par, x[r, :], iid[ids], text, t_lane), text)
        gy.buf[r, :] = nn(coef_of(par, y0()[r, :], tid[ids], x[...], i_lane), x[...])
        gx.send(k)
        gy.send(k)
    turn(a0(), a_t.buf)
    a_t.send()


def second(pars, loads, stores, scratch):
    par, starts = pars
    a1, head, y1, x0, y0, i_own, t_own, gx0, gy0, u0, at0 = loads
    u_out, half, a_t, gx, gy, near, away, mine = stores
    (g0,) = scratch
    unit_images(a1(), head(), half.buf, u_out.buf)
    u_out.send()
    half.send()
    tiles(par, y1, a1, half.buf, x0, y0, i_own, t_own, gx0, gy0, gx, gy)
    t_lane, ids1 = carried(y1()), column(carried(a1()))
    text = y1()[pl.ds(0, ROWS), :]
    u0()
    for k, r in enumerate(HALVES):
        ids = slice(k * STEP, k * STEP + STEP)
        near.buf[r, :] = nn(coef_of(par, half.buf[r, :], ids1[ids], text, t_lane), text)
        near.send(k)
        g0[r, :] = project_u(gx.buf[r, :], u0()[r, :])
    turn(a1(), a_t.buf)
    a_t.send()
    at0()
    for start, store in ((starts[0], away), (starts[1], mine)):
        cols = pl.ds(pl.multiple_of(start, 128), WIDE)
        for k in range(2):

            @pl.loop(2 * k, 2 * k + 2)
            def _(j):
                r = pl.ds(pl.multiple_of(j * 288, 288), 288)
                store.buf[r, :] = nn(at0()[r, :], g0[:, cols])

            store.send(k)


def tiles(par, y, a, x, x0, y0, i_own, t_own, gx0, gy0, gx, gy):
    t_lane, i_lane = carried(y()), carried(a())
    iid, tid = column(lane_ids(i_own())), column(lane_ids(t_own()))
    text = y()[pl.ds(0, ROWS), :]
    x0(), y0(), gx0(), gy0()
    for k, r in enumerate(HALVES):
        ids = slice(k * STEP, k * STEP + STEP)
        gx.buf[r, :] = gx0()[r, :] + nn(coef_of(par, x0()[r, :], iid[ids], text, t_lane), text)
        gy.buf[r, :] = gy0()[r, :] + nn(coef_of(par, y0()[r, :], tid[ids], x[...], i_lane), x[...])
        gx.send(k)
        gy.send(k)


def third(pars, loads, stores, scratch):
    par, starts = pars
    a2, head, y2, x1, i_near, near, u1, at1, away0, mine0 = loads
    half, low, high, mine = stores
    u2, at2, g1, g2 = scratch
    unit_images(a2(), head(), half.buf, u2)
    half.send()
    t_lane = carried(y2())
    ids1 = column(lane_ids(i_near()))
    ids2 = column(carried(a2()))
    text = y2()[pl.ds(0, ROWS), :]
    x1(), u1(), near()
    for k, r in enumerate(HALVES):
        ids = slice(k * STEP, k * STEP + STEP)
        grad = nn(coef_of(par, x1()[r, :], ids1[ids], text, t_lane), text)
        g1[r, :] = project_u(grad + near()[r, :], u1()[r, :])
        grad = nn(coef_of(par, half.buf[r, :], ids2[ids], text, t_lane), text)
        g2[r, :] = project_u(grad, u2[r, :])
    turn(a2(), at2)
    at1(), away0(), mine0()

    def summed(start, before, r):
        cols = pl.ds(pl.multiple_of(start, 128), WIDE)
        total = before()[r, :] + nn(at1()[r, :], g1[:, cols])
        return total + nn(at2[r, :], g2[:, cols])

    for i, store in enumerate((low, high)):

        @pl.loop(0, 2)
        def _(k):
            at = pl.multiple_of(k * 288, 288)
            rows = summed(starts[0], away0, pl.ds(at + 576 * i, 288))
            store.buf[pl.ds(at, 288), :] = rows.astype(BF16)

        store.send()
    for k in range(2):

        @pl.loop(2 * k, 2 * k + 2)
        def _(j):
            r = pl.ds(pl.multiple_of(j * 288, 288), 288)
            mine.buf[r, :] = summed(starts[1], mine0, r).astype(BF16)

        mine.send(k)


def to_pieces(direct, loads, stores, __):
    mine, (low, high) = loads[0](), direct
    out = stores[0].buf
    for k in range(8):
        other = (low, high)[k // 4]
        s = pl.ds(144 * (k % 4), 144)
        total = mine[pl.ds(144 * k, 144), :].astype(F32) + other[s, :].astype(F32)
        total = total.astype(BF16)
        out[2 * k] = total[:, :PART]
        out[2 * k + 1] = total[:, 256 : 256 + PART]
        if k % 4 == 3:
            stores[0].send(k // 4)


def add_pieces(direct, _, stores, __):
    got, out = direct[0], stores[0].buf
    total = got[0].astype(F32)
    for k in range(1, 16):
        total = total + got[k].astype(F32)
    for k in range(8):
        out[k] = total[18 * k : 18 * k + 18]
    stores[0].send()


def add_last(direct, _, stores, __):
    got = direct[0]
    total = got[0]
    for k in range(1, 8):
        total = total + got[k]
    stores[0].buf[...] = total * (1.0 / 256.0)
    stores[0].send()


def split(rows, tail, low, high):
    low.buf[pl.ds(0, STEP), :] = rows[pl.ds(0, STEP), :]
    low.buf[pl.ds(STEP, 16), :] = tail[pl.ds(ROWS, 16), :]
    low.send()
    high.buf[...] = rows[pl.ds(STEP, STEP), :]
    high.send()


def fourth(pars, loads, stores, scratch):
    (par,) = pars
    a3, head, y0, t_own, x2, i_far, gy0, y2, x0, i_own, gx0, y3 = loads
    x_low, x_high, y_low, y_high, gy, gx = stores
    (x3,) = scratch
    unit_images(a3(), head(), x3)
    split(x3, a3(), x_low, x_high)
    i_lane, far, tid = carried(a3()), lane_ids(i_far()), column(lane_ids(t_own()))
    y0(), x2(), gy0()
    near = x3[...]
    for k, r in enumerate(HALVES):
        ids = slice(k * STEP, k * STEP + STEP)
        total = gy0()[r, :] + nn(coef_of(par, y0()[r, :], tid[ids], x2()[...], far), x2()[...])
        total = total + nn(coef_of(par, y0()[r, :], tid[ids], near, i_lane), near)
        gy.buf[r, :] = total
        gy.send(k)
    split(y3(), y3(), y_low, y_high)
    texts = [(y()[pl.ds(0, ROWS), :], carried(y())) for y in (y2, y3)]
    iid = column(lane_ids(i_own()))
    x0(), gx0()
    for k, r in enumerate(HALVES):
        ids = slice(k * STEP, k * STEP + STEP)
        total = gx0()[r, :]
        for text, lane in texts:
            total = total + nn(coef_of(par, x0()[r, :], iid[ids], text, lane), text)
        gx.buf[r, :] = total
        gx.send(k)


def last(pars, loads, stores, _):
    par, y_high, x_high = pars
    y_low, x0, i_own, gx0, u0, head, x_low, y0, t_own, gy0, text_in = loads
    g_image, g_text = stores

    def both(low, high):
        lanes = lane_ids(low().at[pl.ds(STEP, 16)])
        rows = low()[pl.ds(0, STEP), :], high[...]
        return (rows[0], lanes[:, :STEP]), (rows[1], lanes[:, STEP:])

    x0()
    texts, iid = both(y_low, y_high), column(lane_ids(i_own()))
    for k, r in enumerate(HALVES):
        ids = slice(k * STEP, k * STEP + STEP)
        grad = gx0()[r, :]
        for text, lane in texts:
            grad = grad + nn(coef_of(par, x0()[r, :], iid[ids], text, lane), text)
        g_image.buf[r, :] = nt(project_u(grad, u0()[r, :]), head()[...]).astype(BF16)
        g_image.send(k)
    images, tid = both(x_low, x_high), column(lane_ids(t_own()))
    for k, r in enumerate(HALVES):
        ids = slice(k * STEP, k * STEP + STEP)
        grad = gy0()[r, :]
        for image, lane in images:
            grad = grad + nn(coef_of(par, y0()[r, :], tid[ids], image, lane), image)
        t = text_in()[r, :].astype(F32)
        inv = inverse_norm(t)
        g_text.buf[r, :] = project(inv, grad, t * inv).astype(BF16)
        g_text.send(k)


BLOCK = ((ROWS, D), BF16)
SUMS = ((ROWS, D), F32)
TURNED = ((D, ROWS), BF16)
TRAVEL = ((SENT, D), BF16)


def per_device(image_feats, text_feats, head, image_ids, text_ids, log_scale, bias):
    core = lax.axis_index("c")
    par = jnp.stack([jnp.exp(log_scale[0]), bias[0]])
    ids_of = lambda block: (block, ROWS, 16)
    y0, a0 = run(
        prepare, [TRAVEL, TRAVEL],
        [text_feats, image_feats, text_ids.reshape(1, ROWS), image_ids.reshape(1, ROWS)],
    )
    y1, a1 = shifted(y0, 1), shifted(a0, -1)
    u0, x0, at0, gx, gy = run(first, [SUMS, BLOCK, TURNED, SUMS, SUMS], [a0, head, y0], [par], eager=2)
    y2, a2 = shifted(after(y1, gx), 1), shifted(after(a1, gx), -1)
    own_y = (y0, 0, ROWS)
    starts = jnp.stack([512 * (1 - core), 512 * core])
    piece = ((D, WIDE), F32)
    u1, x1, at1, gx, gy, near, away, mine = run(
        second, [SUMS, BLOCK, TURNED, SUMS, SUMS, SUMS, piece, piece],
        [a1, head, y1, x0, own_y, ids_of(a0), ids_of(y0), gx, gy, u0, at0],
        [par, starts], [BLOCK], eager=2,
    )
    y3, a3 = shifted(after(y2, gx), 1), shifted(after(a2, gx), -1)
    part = ((D // 2, WIDE), BF16)
    x2, low, high, mine = run(
        third, [BLOCK, part, part, ((D, WIDE), BF16)],
        [a2, head, y2, x1, ids_of(a1), near, u1, at1, away, mine],
        [par, starts], [SUMS, TURNED, BLOCK, BLOCK], eager=2,
    )
    got = [lax.ppermute(half, "c", [(0, 1), (1, 0)]) for half in (low, high)]
    (pieces,) = run(to_pieces, [((16, 144, PART), BF16)], [mine], direct=got, vmem=16)
    spread = lax.all_to_all(pieces, ("y", "xl", "xh"), 0, 0)
    low, high = ((STEP + 16, D), BF16), ((STEP, D), BF16)
    x_low, x_high, y_low, y_high, gy, gx = run(
        fourth, [low, high, low, high, SUMS, SUMS],
        [a3, head, own_y, ids_of(y0), x2, ids_of(a2), gy, y2, x0, ids_of(a0),
         after(gx, pieces), y3],
        [par], [BLOCK], flops=10**11, eager=2,
    )
    y_low, x_low = shifted(after(y_low, spread), 1), shifted(after(x_low, spread), -1)
    (total,) = run(add_pieces, [((8, 18, PART), F32)], [], direct=[after(spread, gx)], vmem=16)
    spread = lax.all_to_all(total, "z", 0, 0)
    y_high, x_high = shifted(after(y_high, total), 1), shifted(after(x_high, total), -1)
    (total,) = run(
        add_last, [((18, PART), F32)], [], direct=[after(spread, y_low, x_low)], flops=10**11,
        vmem=16,
    )
    swap = [(0, 1), (1, 0)]
    other = lax.ppermute(total, "xh", swap)
    grad_image, grad_text = run(
        last, [BLOCK, BLOCK],
        [y_low, x0, ids_of(a0), gx, u0, head, x_low, own_y, ids_of(y0), after(gy, total),
         text_feats],
        [par], flops=10**11, eager=4, direct=[y_high, x_high], vmem=36,
    )
    other = after(other, grad_text)
    even = lax.axis_index("xh") == 0
    left, right = jnp.where(even, total, other), jnp.where(even, other, total)
    wide = jnp.concatenate([left, right[:, 128:]], axis=1)
    other = lax.ppermute(wide, "c", swap)
    left, right = jnp.where(core == 0, wide, other), jnp.where(core == 0, other, wide)
    grad_head = jnp.concatenate([left, right[:, 128:]], axis=1)
    return grad_image, grad_text, grad_head


def solution(mesh):
    fine = Mesh(mesh.devices.reshape(4, 2, 8, 2, 2), AXES)
    placed = (P(AXES, None), P(AXES, None), P(), P(AXES), P(AXES), P(), P())
    return jax.shard_map(
        per_device,
        mesh=fine,
        in_specs=placed,
        out_specs=(P(AXES, None), P(AXES, None), P(CYCLE, None)),
        check_vma=False,
    )
```

```python
import jax
import jax.numpy as jnp
from jax import lax
from jax.experimental import pallas as pl
from jax.experimental.pallas import tpu as pltpu
from jax.sharding import Mesh, PartitionSpec as P

AXES = ("y", "xl", "z", "xh", "c")
CYCLE = ("y", "xl", "z")
F32 = jnp.float32
BF16 = jnp.bfloat16
D = 1152
ROWS = 512
SENT = 528
STEP = 256
LOW = 384
WIDE = 640
PART = 384


def shifted(value, steps):
    count = lax.axis_size(CYCLE)
    return lax.ppermute(value, CYCLE, [(i, (i + steps) % count) for i in range(count)])


def after(value, *others):
    return lax.optimization_barrier((value,) + others)[0]


def nn(a, b):
    return jnp.dot(a, b, preferred_element_type=F32)


def nt(a, b):
    return lax.dot_general(a, b, (((1,), (1,)), ((), ())), preferred_element_type=F32)


class Load:
    def __init__(self, copy, buf):
        self.copy, self.buf, self.here, self.then = copy, buf, False, []

    def __call__(self):
        if not self.here:
            self.copy.wait()
            self.here = True
            for copy in self.then:
                copy.start()
        return self.buf


class Store:
    def __init__(self, out, buf, sems):
        self.out, self.buf, self.sems, self.sent = out, buf, sems, []

    def send(self, half=None):
        if half is None:
            copy = pltpu.make_async_copy(self.buf, self.out, self.sems.at[0])
        else:
            size = self.buf.shape[0] // 2
            rows = pl.ds(half * size, size)
            copy = pltpu.make_async_copy(self.buf.at[rows], self.out.at[rows], self.sems.at[half])
        copy.start()
        self.sent.append(copy)


def run(body, outs, ins, scalars=(), scratch=(), flops=0, vmem=56, direct=(), eager=99):
    ins = [i if isinstance(i, tuple) else (i, None, None) for i in ins]
    n_d, n_i, n_o = len(direct), len(ins), len(outs)
    n_s = len(scalars) + n_d

    def kernel(*refs):
        pars, refs = refs[:n_s], refs[n_s:]
        sources, refs = refs[:n_i], refs[n_i:]
        results, refs = refs[:n_o], refs[n_o:]
        in_bufs, refs = refs[:n_i], refs[n_i:]
        out_bufs, refs = refs[:n_o], refs[n_o:]
        in_sems, out_sems, extra = refs[0], refs[1], refs[2:]
        loads = []
        for k, (_, first, rows) in enumerate(ins):
            source = sources[k] if first is None else sources[k].at[pl.ds(first, rows)]
            copy = pltpu.make_async_copy(source, in_bufs[k], in_sems.at[k])
            loads.append(Load(copy, in_bufs[k]))
            if k < eager:
                copy.start()
            else:
                loads[eager - 1].then.append(copy)
        stores = [Store(results[k], out_bufs[k], out_sems.at[k]) for k in range(n_o)]
        body(pars, loads, stores, extra)
        for load in loads:
            load()
        for store in stores:
            for copy in store.sent:
                copy.wait()

    shapes = []
    for array, _, rows in ins:
        shape = array.shape if rows is None else (rows,) + array.shape[1:]
        shapes.append(pltpu.VMEM(shape, array.dtype))
    shapes += [pltpu.VMEM(s, t) for s, t in outs]
    shapes += [pltpu.SemaphoreType.DMA((max(n_i, 1),)), pltpu.SemaphoreType.DMA((n_o, 2))]
    shapes += [pltpu.VMEM(s, t) for s, t in scratch]
    return pl.pallas_call(
        kernel,
        out_shape=[jax.ShapeDtypeStruct(s, t) for s, t in outs],
        in_specs=[pl.BlockSpec(memory_space=pltpu.SMEM)] * len(scalars)
        + [pl.BlockSpec(memory_space=pltpu.VMEM)] * n_d
        + [pl.BlockSpec(memory_space=pl.ANY)] * n_i,
        out_specs=[pl.BlockSpec(memory_space=pl.ANY)] * n_o,
        scratch_shapes=shapes,
        compiler_params=pltpu.CompilerParams(vmem_limit_bytes=vmem * 2**20),
        cost_estimate=pl.CostEstimate(flops=flops, bytes_accessed=0, transcendentals=0),
    )(*scalars, *direct, *[i[0] for i in ins])


HALVES = [pl.ds(i * STEP, STEP) for i in range(ROWS // STEP)]


def inverse_norm(values):
    return lax.rsqrt(jnp.sum(values * values, axis=-1, keepdims=True) + 1e-06)


def lane_ids(pair):
    pair = pair[:, pl.ds(0, ROWS)].astype(F32)
    return pair[0:1] * 256.0 + pair[1:2]


def carried(block):
    return lane_ids(block.at[pl.ds(ROWS, 16)])


def column(lane):
    return jnp.broadcast_to(lane, (8, ROWS)).T[:, 0:1]


def coef_of(par, rows, row_ids, columns, column_ids):
    scale, offset = par[0], par[1]
    logits = scale * nt(rows, columns) + offset
    positive = (row_ids == column_ids).astype(F32)
    return (scale * (jax.nn.sigmoid(logits) - positive)).astype(BF16)


def unit_images(feats, head, half, u_out=None):
    for r in HALVES:
        u = nn(feats[r, :], head[...])
        half[r, :] = (u * inverse_norm(u)).astype(BF16)
        if u_out is not None:
            u_out[r, :] = u


def turn(feats, out):
    for k in range(D // 128):
        cols = pl.ds(k * 128, 128)
        out[cols, :] = feats[pl.ds(0, ROWS), cols].T


def project(inv, grad, x):
    return inv * (grad - x * jnp.sum(x * grad, axis=1, keepdims=True))


def project_u(grad, u):
    inv = inverse_norm(u)
    return project(inv, grad, u * inv).astype(BF16)


def prepare(_, loads, stores, __):
    text, image, text_lane, image_lane = loads
    text_out, image_out = stores
    image()
    text()
    for r in HALVES:
        image_out.buf[r, :] = image()[r, :]
    for load, out in ((image_lane, image_out), (text_lane, text_out)):
        if out is text_out:
            for r in HALVES:
                t = text()[r, :].astype(F32)
                out.buf[r, :] = (t * inverse_norm(t)).astype(BF16)
        out.buf[pl.ds(ROWS, 16), :] = jnp.zeros((16, D), BF16)
        row = lax.broadcasted_iota(jnp.int32, (16, ROWS), 0)
        ids = load()[...]
        high, low = (ids >> 8).astype(F32), (ids & 255).astype(F32)
        pair = jnp.where(row == 0, high, jnp.where(row == 1, low, 0.0))
        out.buf[pl.ds(ROWS, 16), pl.ds(0, ROWS)] = pair.astype(BF16)
        out.send()


def first(pars, loads, stores, _):
    (par,) = pars
    a0, head, y0 = loads
    u_out, half, a_t, gx, gy = stores
    unit_images(a0(), head(), half.buf, u_out.buf)
    u_out.send()
    half.send()
    t_lane, i_lane = carried(y0()), carried(a0())
    iid, tid = column(i_lane), column(t_lane)
    text, x = y0()[pl.ds(0, ROWS), :], half.buf
    for k, r in enumerate(HALVES):
        ids = slice(k * STEP, k * STEP + STEP)
        gx.buf[r, :] = nn(coef_of(par, x[r, :], iid[ids], text, t_lane), text)
        gy.buf[r, :] = nn(coef_of(par, y0()[r, :], tid[ids], x[...], i_lane), x[...])
        gx.send(k)
        gy.send(k)
    turn(a0(), a_t.buf)
    a_t.send()


def second(pars, loads, stores, scratch):
    par, starts = pars
    a1, head, y1, x0, y0, i_own, t_own, gx0, gy0, u0, at0 = loads
    u_out, half, a_t, gx, gy, near, away, mine = stores
    (g0,) = scratch
    unit_images(a1(), head(), half.buf, u_out.buf)
    u_out.send()
    half.send()
    tiles(par, y1, a1, half.buf, x0, y0, i_own, t_own, gx0, gy0, gx, gy)
    t_lane, ids1 = carried(y1()), column(carried(a1()))
    text = y1()[pl.ds(0, ROWS), :]
    u0()
    for k, r in enumerate(HALVES):
        ids = slice(k * STEP, k * STEP + STEP)
        near.buf[r, :] = nn(coef_of(par, half.buf[r, :], ids1[ids], text, t_lane), text)
        near.send(k)
        g0[r, :] = project_u(gx.buf[r, :], u0()[r, :])
    turn(a1(), a_t.buf)
    a_t.send()
    at0()
    for start, store in ((starts[0], away), (starts[1], mine)):
        cols = pl.ds(pl.multiple_of(start, 128), WIDE)
        for k in range(2):

            @pl.loop(2 * k, 2 * k + 2)
            def _(j):
                r = pl.ds(pl.multiple_of(j * 288, 288), 288)
                store.buf[r, :] = nn(at0()[r, :], g0[:, cols])

            store.send(k)


def tiles(par, y, a, x, x0, y0, i_own, t_own, gx0, gy0, gx, gy):
    t_lane, i_lane = carried(y()), carried(a())
    iid, tid = column(lane_ids(i_own())), column(lane_ids(t_own()))
    text = y()[pl.ds(0, ROWS), :]
    x0(), y0(), gx0(), gy0()
    for k, r in enumerate(HALVES):
        ids = slice(k * STEP, k * STEP + STEP)
        gx.buf[r, :] = gx0()[r, :] + nn(coef_of(par, x0()[r, :], iid[ids], text, t_lane), text)
        gy.buf[r, :] = gy0()[r, :] + nn(coef_of(par, y0()[r, :], tid[ids], x[...], i_lane), x[...])
        gx.send(k)
        gy.send(k)


def third(pars, loads, stores, scratch):
    par, starts = pars
    a2, head, y2, x1, i_near, near, u1, at1, away0, mine0 = loads
    half, low, high, mine = stores
    u2, at2, g1, g2 = scratch
    unit_images(a2(), head(), half.buf, u2)
    half.send()
    t_lane = carried(y2())
    ids1 = column(lane_ids(i_near()))
    ids2 = column(carried(a2()))
    text = y2()[pl.ds(0, ROWS), :]
    x1(), u1(), near()
    for k, r in enumerate(HALVES):
        ids = slice(k * STEP, k * STEP + STEP)
        grad = nn(coef_of(par, x1()[r, :], ids1[ids], text, t_lane), text)
        g1[r, :] = project_u(grad + near()[r, :], u1()[r, :])
        grad = nn(coef_of(par, half.buf[r, :], ids2[ids], text, t_lane), text)
        g2[r, :] = project_u(grad, u2[r, :])
    turn(a2(), at2)
    at1(), away0(), mine0()

    def summed(start, before, r):
        cols = pl.ds(pl.multiple_of(start, 128), WIDE)
        total = before()[r, :] + nn(at1()[r, :], g1[:, cols])
        return total + nn(at2[r, :], g2[:, cols])

    for i, store in enumerate((low, high)):

        @pl.loop(0, 2)
        def _(k):
            at = pl.multiple_of(k * 288, 288)
            rows = summed(starts[0], away0, pl.ds(at + 576 * i, 288))
            store.buf[pl.ds(at, 288), :] = rows.astype(BF16)

        store.send()
    for k in range(2):

        @pl.loop(2 * k, 2 * k + 2)
        def _(j):
            r = pl.ds(pl.multiple_of(j * 288, 288), 288)
            mine.buf[r, :] = summed(starts[1], mine0, r).astype(BF16)

        mine.send(k)


def to_pieces(direct, loads, stores, __):
    mine, (low, high) = loads[0](), direct
    out = stores[0].buf
    for k in range(8):
        other = (low, high)[k // 4]
        s = pl.ds(144 * (k % 4), 144)
        total = mine[pl.ds(144 * k, 144), :].astype(F32) + other[s, :].astype(F32)
        total = total.astype(BF16)
        out[2 * k] = total[:, :PART]
        out[2 * k + 1] = total[:, 256 : 256 + PART]
        if k % 4 == 3:
            stores[0].send(k // 4)


def add_pieces(direct, _, stores, __):
    got, out = direct[0], stores[0].buf
    total = got[0].astype(F32)
    for k in range(1, 16):
        total = total + got[k].astype(F32)
    for k in range(8):
        out[k] = total[18 * k : 18 * k + 18]
    stores[0].send()


def add_last(direct, _, stores, __):
    got = direct[0]
    total = got[0]
    for k in range(1, 8):
        total = total + got[k]
    stores[0].buf[...] = total * (1.0 / 256.0)
    stores[0].send()


def split(rows, tail, low, high):
    low.buf[pl.ds(0, LOW), :] = rows[pl.ds(0, LOW), :]
    low.buf[pl.ds(LOW, 16), :] = tail[pl.ds(ROWS, 16), :]
    low.send()
    high.buf[...] = rows[pl.ds(LOW, ROWS - LOW), :]
    high.send()


def fourth(pars, loads, stores, scratch):
    (par,) = pars
    a3, head, y0, t_own, x2, i_far, gy0, y2, x0, i_own, gx0, y3 = loads
    x_low, x_high, y_low, y_high, gy, gx = stores
    (x3,) = scratch
    unit_images(a3(), head(), x3)
    split(x3, a3(), x_low, x_high)
    i_lane, far, tid = carried(a3()), lane_ids(i_far()), column(lane_ids(t_own()))
    y0(), x2(), gy0()
    near = x3[...]
    for k, r in enumerate(HALVES):
        ids = slice(k * STEP, k * STEP + STEP)
        total = gy0()[r, :] + nn(coef_of(par, y0()[r, :], tid[ids], x2()[...], far), x2()[...])
        total = total + nn(coef_of(par, y0()[r, :], tid[ids], near, i_lane), near)
        gy.buf[r, :] = total
        gy.send(k)
    split(y3(), y3(), y_low, y_high)
    texts = [(y()[pl.ds(0, ROWS), :], carried(y())) for y in (y2, y3)]
    iid = column(lane_ids(i_own()))
    x0(), gx0()
    for k, r in enumerate(HALVES):
        ids = slice(k * STEP, k * STEP + STEP)
        total = gx0()[r, :]
        for text, lane in texts:
            total = total + nn(coef_of(par, x0()[r, :], iid[ids], text, lane), text)
        gx.buf[r, :] = total
        gx.send(k)


def last(pars, loads, stores, scratch):
    par, y_high, x_high = pars
    y_low, x0, i_own, gx0, u0, head, x_low, y0, t_own, gy0, text_in = loads
    g_image, g_text = stores

    def joined(low, high, out):
        out[pl.ds(0, LOW), :] = low()[pl.ds(0, LOW), :]
        out[pl.ds(LOW, ROWS - LOW), :] = high[...]
        return out[...], lane_ids(low().at[pl.ds(LOW, 16)])

    x0()
    (text, t_lane), iid = joined(y_low, y_high, scratch[0]), column(lane_ids(i_own()))
    for k, r in enumerate(HALVES):
        ids = slice(k * STEP, k * STEP + STEP)
        grad = gx0()[r, :] + nn(coef_of(par, x0()[r, :], iid[ids], text, t_lane), text)
        g_image.buf[r, :] = nt(project_u(grad, u0()[r, :]), head()[...]).astype(BF16)
        g_image.send(k)
    (image, i_lane), tid = joined(x_low, x_high, scratch[1]), column(lane_ids(t_own()))
    for k, r in enumerate(HALVES):
        ids = slice(k * STEP, k * STEP + STEP)
        grad = gy0()[r, :] + nn(coef_of(par, y0()[r, :], tid[ids], image, i_lane), image)
        t = text_in()[r, :].astype(F32)
        inv = inverse_norm(t)
        g_text.buf[r, :] = project(inv, grad, t * inv).astype(BF16)
        g_text.send(k)


BLOCK = ((ROWS, D), BF16)
SUMS = ((ROWS, D), F32)
TURNED = ((D, ROWS), BF16)
TRAVEL = ((SENT, D), BF16)


def per_device(image_feats, text_feats, head, image_ids, text_ids, log_scale, bias):
    core = lax.axis_index("c")
    par = jnp.stack([jnp.exp(log_scale[0]), bias[0]])
    ids_of = lambda block: (block, ROWS, 16)
    y0, a0 = run(
        prepare, [TRAVEL, TRAVEL],
        [text_feats, image_feats, text_ids.reshape(1, ROWS), image_ids.reshape(1, ROWS)],
    )
    y1, a1 = shifted(y0, 1), shifted(a0, -1)
    u0, x0, at0, gx, gy = run(first, [SUMS, BLOCK, TURNED, SUMS, SUMS], [a0, head, y0], [par], eager=2)
    y2, a2 = shifted(after(y1, gx), 1), shifted(after(a1, gx), -1)
    own_y = (y0, 0, ROWS)
    starts = jnp.stack([512 * (1 - core), 512 * core])
    piece = ((D, WIDE), F32)
    u1, x1, at1, gx, gy, near, away, mine = run(
        second, [SUMS, BLOCK, TURNED, SUMS, SUMS, SUMS, piece, piece],
        [a1, head, y1, x0, own_y, ids_of(a0), ids_of(y0), gx, gy, u0, at0],
        [par, starts], [BLOCK], eager=2,
    )
    y3, a3 = shifted(after(y2, gx), 1), shifted(after(a2, gx), -1)
    part = ((D // 2, WIDE), BF16)
    x2, low, high, mine = run(
        third, [BLOCK, part, part, ((D, WIDE), BF16)],
        [a2, head, y2, x1, ids_of(a1), near, u1, at1, away, mine],
        [par, starts], [SUMS, TURNED, BLOCK, BLOCK], eager=2,
    )
    got = [lax.ppermute(half, "c", [(0, 1), (1, 0)]) for half in (low, high)]
    (pieces,) = run(to_pieces, [((16, 144, PART), BF16)], [mine], direct=got, vmem=16)
    spread = lax.all_to_all(pieces, ("y", "xl", "xh"), 0, 0)
    low, high = ((LOW + 16, D), BF16), ((ROWS - LOW, D), BF16)
    x_low, x_high, y_low, y_high, gy, gx = run(
        fourth, [low, high, low, high, SUMS, SUMS],
        [a3, head, own_y, ids_of(y0), x2, ids_of(a2), gy, y2, x0, ids_of(a0),
         after(gx, pieces), y3],
        [par], [BLOCK], flops=10**11, eager=2,
    )
    y_low, x_low = shifted(after(y_low, spread), 1), shifted(after(x_low, spread), -1)
    (total,) = run(add_pieces, [((8, 18, PART), F32)], [], direct=[after(spread, gx)], vmem=16)
    spread = lax.all_to_all(total, "z", 0, 0)
    y_high, x_high = shifted(after(y_high, total), 1), shifted(after(x_high, total), -1)
    (total,) = run(
        add_last, [((18, PART), F32)], [], direct=[after(spread, y_low, x_low)], flops=10**11,
        vmem=16,
    )
    swap = [(0, 1), (1, 0)]
    other = lax.ppermute(total, "xh", swap)
    grad_image, grad_text = run(
        last, [BLOCK, BLOCK],
        [y_low, x0, ids_of(a0), gx, u0, head, x_low, own_y, ids_of(y0), after(gy, total),
         text_feats],
        [par], [BLOCK, BLOCK], flops=10**11, eager=4, direct=[y_high, x_high], vmem=36,
    )
    other = after(other, grad_text)
    even = lax.axis_index("xh") == 0
    left, right = jnp.where(even, total, other), jnp.where(even, other, total)
    wide = jnp.concatenate([left, right[:, 128:]], axis=1)
    other = lax.ppermute(wide, "c", swap)
    left, right = jnp.where(core == 0, wide, other), jnp.where(core == 0, other, wide)
    grad_head = jnp.concatenate([left, right[:, 128:]], axis=1)
    return grad_image, grad_text, grad_head


def solution(mesh):
    fine = Mesh(mesh.devices.reshape(4, 2, 8, 2, 2), AXES)
    placed = (P(AXES, None), P(AXES, None), P(), P(AXES), P(AXES), P(), P())
    return jax.shard_map(
        per_device,
        mesh=fine,
        in_specs=placed,
        out_specs=(P(AXES, None), P(AXES, None), P(CYCLE, None)),
        check_vma=False,
    )
```

```python
import jax
import jax.numpy as jnp
from jax import lax
from jax.experimental import pallas as pl
from jax.experimental.pallas import tpu as pltpu
from jax.sharding import Mesh, PartitionSpec as P

AXES = ("y", "xl", "z", "xh", "c")
CYCLE = ("y", "xl", "z")
F32 = jnp.float32
BF16 = jnp.bfloat16
D = 1152
ROWS = 512
SENT = 528
STEP = 256
LOW = 384
WIDE = 640
PART = 384


def shifted(value, steps):
    count = lax.axis_size(CYCLE)
    return lax.ppermute(value, CYCLE, [(i, (i + steps) % count) for i in range(count)])


def after(value, *others):
    return lax.optimization_barrier((value,) + others)[0]


def nn(a, b):
    return jnp.dot(a, b, preferred_element_type=F32)


def nt(a, b):
    return lax.dot_general(a, b, (((1,), (1,)), ((), ())), preferred_element_type=F32)


class Load:
    def __init__(self, copy, buf):
        self.copy, self.buf, self.here, self.then = copy, buf, False, []

    def __call__(self):
        if not self.here:
            self.copy.wait()
            self.here = True
            for copy in self.then:
                copy.start()
        return self.buf


class Store:
    def __init__(self, out, buf, sems):
        self.out, self.buf, self.sems, self.sent = out, buf, sems, []

    def send(self, half=None):
        if half is None:
            copy = pltpu.make_async_copy(self.buf, self.out, self.sems.at[0])
        else:
            size = self.buf.shape[0] // 2
            rows = pl.ds(half * size, size)
            copy = pltpu.make_async_copy(self.buf.at[rows], self.out.at[rows], self.sems.at[half])
        copy.start()
        self.sent.append(copy)


def run(body, outs, ins, scalars=(), scratch=(), flops=0, vmem=56, direct=(), eager=99):
    ins = [i if isinstance(i, tuple) else (i, None, None) for i in ins]
    n_d, n_i, n_o = len(direct), len(ins), len(outs)
    n_s = len(scalars) + n_d

    def kernel(*refs):
        pars, refs = refs[:n_s], refs[n_s:]
        sources, refs = refs[:n_i], refs[n_i:]
        results, refs = refs[:n_o], refs[n_o:]
        in_bufs, refs = refs[:n_i], refs[n_i:]
        out_bufs, refs = refs[:n_o], refs[n_o:]
        in_sems, out_sems, extra = refs[0], refs[1], refs[2:]
        loads = []
        for k, (_, first, rows) in enumerate(ins):
            source = sources[k] if first is None else sources[k].at[pl.ds(first, rows)]
            copy = pltpu.make_async_copy(source, in_bufs[k], in_sems.at[k])
            loads.append(Load(copy, in_bufs[k]))
            if k < eager:
                copy.start()
            else:
                loads[eager - 1].then.append(copy)
        stores = [Store(results[k], out_bufs[k], out_sems.at[k]) for k in range(n_o)]
        body(pars, loads, stores, extra)
        for load in loads:
            load()
        for store in stores:
            for copy in store.sent:
                copy.wait()

    shapes = []
    for array, _, rows in ins:
        shape = array.shape if rows is None else (rows,) + array.shape[1:]
        shapes.append(pltpu.VMEM(shape, array.dtype))
    shapes += [pltpu.VMEM(s, t) for s, t in outs]
    shapes += [pltpu.SemaphoreType.DMA((max(n_i, 1),)), pltpu.SemaphoreType.DMA((n_o, 2))]
    shapes += [pltpu.VMEM(s, t) for s, t in scratch]
    return pl.pallas_call(
        kernel,
        out_shape=[jax.ShapeDtypeStruct(s, t) for s, t in outs],
        in_specs=[pl.BlockSpec(memory_space=pltpu.SMEM)] * len(scalars)
        + [pl.BlockSpec(memory_space=pltpu.VMEM)] * n_d
        + [pl.BlockSpec(memory_space=pl.ANY)] * n_i,
        out_specs=[pl.BlockSpec(memory_space=pl.ANY)] * n_o,
        scratch_shapes=shapes,
        compiler_params=pltpu.CompilerParams(vmem_limit_bytes=vmem * 2**20),
        cost_estimate=pl.CostEstimate(flops=flops, bytes_accessed=0, transcendentals=0),
    )(*scalars, *direct, *[i[0] for i in ins])


HALVES = [pl.ds(i * STEP, STEP) for i in range(ROWS // STEP)]


def inverse_norm(values):
    return lax.rsqrt(jnp.sum(values * values, axis=-1, keepdims=True) + 1e-06)


def lane_ids(pair):
    pair = pair[:, pl.ds(0, ROWS)].astype(F32)
    return pair[0:1] * 256.0 + pair[1:2]


def carried(block):
    return lane_ids(block.at[pl.ds(ROWS, 16)])


def column(lane):
    return jnp.broadcast_to(lane, (8, ROWS)).T[:, 0:1]


def coef_of(par, rows, row_ids, columns, column_ids):
    scale, offset = par[0], par[1]
    logits = scale * nt(rows, columns) + offset
    positive = (row_ids == column_ids).astype(F32)
    return (scale * (jax.nn.sigmoid(logits) - positive)).astype(BF16)


def unit_images(feats, head, half, u_out=None):
    for r in HALVES:
        u = nn(feats[r, :], head[...])
        half[r, :] = (u * inverse_norm(u)).astype(BF16)
        if u_out is not None:
            u_out[r, :] = u


def turn(feats, out):
    for k in range(D // 128):
        cols = pl.ds(k * 128, 128)
        out[cols, :] = feats[pl.ds(0, ROWS), cols].T


def project(inv, grad, x):
    return inv * (grad - x * jnp.sum(x * grad, axis=1, keepdims=True))


def project_u(grad, u):
    inv = inverse_norm(u)
    return project(inv, grad, u * inv).astype(BF16)


def prepare(_, loads, stores, __):
    text, image, text_lane, image_lane = loads
    text_out, image_out = stores
    image()
    text()
    for r in HALVES:
        image_out.buf[r, :] = image()[r, :]
    for load, out in ((image_lane, image_out), (text_lane, text_out)):
        if out is text_out:
            for r in HALVES:
                t = text()[r, :].astype(F32)
                out.buf[r, :] = (t * inverse_norm(t)).astype(BF16)
        out.buf[pl.ds(ROWS, 16), :] = jnp.zeros((16, D), BF16)
        row = lax.broadcasted_iota(jnp.int32, (16, ROWS), 0)
        ids = load()[...]
        high, low = (ids >> 8).astype(F32), (ids & 255).astype(F32)
        pair = jnp.where(row == 0, high, jnp.where(row == 1, low, 0.0))
        out.buf[pl.ds(ROWS, 16), pl.ds(0, ROWS)] = pair.astype(BF16)
        out.send()


def first(pars, loads, stores, _):
    (par,) = pars
    a0, head, y0 = loads
    u_out, half, a_t, gx, gy = stores
    unit_images(a0(), head(), half.buf, u_out.buf)
    u_out.send()
    half.send()
    t_lane, i_lane = carried(y0()), carried(a0())
    iid, tid = column(i_lane), column(t_lane)
    text, x = y0()[pl.ds(0, ROWS), :], half.buf
    for k, r in enumerate(HALVES):
        ids = slice(k * STEP, k * STEP + STEP)
        gx.buf[r, :] = nn(coef_of(par, x[r, :], iid[ids], text, t_lane), text)
        gy.buf[r, :] = nn(coef_of(par, y0()[r, :], tid[ids], x[...], i_lane), x[...])
        gx.send(k)
        gy.send(k)
    turn(a0(), a_t.buf)
    a_t.send()


def second(pars, loads, stores, scratch):
    par, starts = pars
    a1, head, y1, x0, y0, i_own, t_own, gx0, gy0, u0, at0 = loads
    u_out, half, a_t, gx, gy, near, away, mine = stores
    (g0,) = scratch
    unit_images(a1(), head(), half.buf, u_out.buf)
    u_out.send()
    half.send()
    tiles(par, y1, a1, half.buf, x0, y0, i_own, t_own, gx0, gy0, gx, gy)
    t_lane, ids1 = carried(y1()), column(carried(a1()))
    text = y1()[pl.ds(0, ROWS), :]
    u0()
    for k, r in enumerate(HALVES):
        ids = slice(k * STEP, k * STEP + STEP)
        near.buf[r, :] = nn(coef_of(par, half.buf[r, :], ids1[ids], text, t_lane), text)
        near.send(k)
        g0[r, :] = project_u(gx.buf[r, :], u0()[r, :])
    turn(a1(), a_t.buf)
    a_t.send()
    at0()
    for start, store in ((starts[0], away), (starts[1], mine)):
        cols = pl.ds(pl.multiple_of(start, 128), WIDE)
        for k in range(2):

            @pl.loop(2 * k, 2 * k + 2)
            def _(j):
                r = pl.ds(pl.multiple_of(j * 288, 288), 288)
                store.buf[r, :] = nn(at0()[r, :], g0[:, cols])

            store.send(k)


def tiles(par, y, a, x, x0, y0, i_own, t_own, gx0, gy0, gx, gy):
    t_lane, i_lane = carried(y()), carried(a())
    iid, tid = column(lane_ids(i_own())), column(lane_ids(t_own()))
    text = y()[pl.ds(0, ROWS), :]
    x0(), y0(), gx0(), gy0()
    for k, r in enumerate(HALVES):
        ids = slice(k * STEP, k * STEP + STEP)
        gx.buf[r, :] = gx0()[r, :] + nn(coef_of(par, x0()[r, :], iid[ids], text, t_lane), text)
        gy.buf[r, :] = gy0()[r, :] + nn(coef_of(par, y0()[r, :], tid[ids], x[...], i_lane), x[...])
        gx.send(k)
        gy.send(k)


def third(pars, loads, stores, scratch):
    par, starts = pars
    a2, head, y2, x1, i_near, near, u1, at1, away0, mine0 = loads
    half, low, high, mine = stores
    u2, at2, g1, g2 = scratch
    unit_images(a2(), head(), half.buf, u2)
    half.send()
    t_lane = carried(y2())
    ids1 = column(lane_ids(i_near()))
    ids2 = column(carried(a2()))
    text = y2()[pl.ds(0, ROWS), :]
    x1(), u1(), near()
    for k, r in enumerate(HALVES):
        ids = slice(k * STEP, k * STEP + STEP)
        grad = nn(coef_of(par, x1()[r, :], ids1[ids], text, t_lane), text)
        g1[r, :] = project_u(grad + near()[r, :], u1()[r, :])
        grad = nn(coef_of(par, half.buf[r, :], ids2[ids], text, t_lane), text)
        g2[r, :] = project_u(grad, u2[r, :])
    turn(a2(), at2)
    at1(), away0(), mine0()

    def summed(start, before, r):
        cols = pl.ds(pl.multiple_of(start, 128), WIDE)
        total = before()[r, :] + nn(at1()[r, :], g1[:, cols])
        return total + nn(at2[r, :], g2[:, cols])

    for i, store in enumerate((low, high)):

        @pl.loop(0, 2)
        def _(k):
            at = pl.multiple_of(k * 288, 288)
            rows = summed(starts[0], away0, pl.ds(at + 576 * i, 288))
            store.buf[pl.ds(at, 288), :] = rows.astype(BF16)

        store.send()
    for k in range(2):

        @pl.loop(2 * k, 2 * k + 2)
        def _(j):
            r = pl.ds(pl.multiple_of(j * 288, 288), 288)
            mine.buf[r, :] = summed(starts[1], mine0, r).astype(BF16)

        mine.send(k)


def to_pieces(direct, loads, stores, __):
    mine, (low, high) = loads[0](), direct
    out = stores[0].buf
    for k in range(8):
        other = (low, high)[k // 4]
        s = pl.ds(144 * (k % 4), 144)
        total = mine[pl.ds(144 * k, 144), :].astype(F32) + other[s, :].astype(F32)
        total = total.astype(BF16)
        out[2 * k] = total[:, :PART]
        out[2 * k + 1] = total[:, 256 : 256 + PART]
        if k % 4 == 3:
            stores[0].send(k // 4)


def add_pieces(direct, _, stores, __):
    got, out = direct[0], stores[0].buf
    total = got[0].astype(F32)
    for k in range(1, 16):
        total = total + got[k].astype(F32)
    for k in range(8):
        out[k] = total[18 * k : 18 * k + 18].astype(BF16)
    stores[0].send()


def add_last(direct, _, stores, __):
    got = direct[0]
    total = got[0].astype(F32)
    for k in range(1, 8):
        total = total + got[k].astype(F32)
    stores[0].buf[...] = total * (1.0 / 256.0)
    stores[0].send()


def split(rows, tail, low, high):
    low.buf[pl.ds(0, LOW), :] = rows[pl.ds(0, LOW), :]
    low.buf[pl.ds(LOW, 16), :] = tail[pl.ds(ROWS, 16), :]
    low.send()
    high.buf[...] = rows[pl.ds(LOW, ROWS - LOW), :]
    high.send()


def fourth(pars, loads, stores, scratch):
    (par,) = pars
    a3, head, y0, t_own, x2, i_far, gy0, y2, x0, i_own, gx0, y3 = loads
    x_low, x_high, y_low, y_high, gy, gx = stores
    (x3,) = scratch
    unit_images(a3(), head(), x3)
    split(x3, a3(), x_low, x_high)
    i_lane, far, tid = carried(a3()), lane_ids(i_far()), column(lane_ids(t_own()))
    y0(), x2(), gy0()
    near = x3[...]
    for k, r in enumerate(HALVES):
        ids = slice(k * STEP, k * STEP + STEP)
        total = gy0()[r, :] + nn(coef_of(par, y0()[r, :], tid[ids], x2()[...], far), x2()[...])
        total = total + nn(coef_of(par, y0()[r, :], tid[ids], near, i_lane), near)
        gy.buf[r, :] = total
        gy.send(k)
    split(y3(), y3(), y_low, y_high)
    texts = [(y()[pl.ds(0, ROWS), :], carried(y())) for y in (y2, y3)]
    iid = column(lane_ids(i_own()))
    x0(), gx0()
    for k, r in enumerate(HALVES):
        ids = slice(k * STEP, k * STEP + STEP)
        total = gx0()[r, :]
        for text, lane in texts:
            total = total + nn(coef_of(par, x0()[r, :], iid[ids], text, lane), text)
        gx.buf[r, :] = total
        gx.send(k)


def last(pars, loads, stores, scratch):
    par, y_high, x_high = pars
    y_low, x0, i_own, gx0, u0, head, x_low, y0, t_own, gy0, text_in = loads
    g_image, g_text = stores

    def joined(low, high, out):
        out[pl.ds(0, LOW), :] = low()[pl.ds(0, LOW), :]
        out[pl.ds(LOW, ROWS - LOW), :] = high[...]
        return out[...], lane_ids(low().at[pl.ds(LOW, 16)])

    x0()
    (text, t_lane), iid = joined(y_low, y_high, scratch[0]), column(lane_ids(i_own()))
    for k, r in enumerate(HALVES):
        ids = slice(k * STEP, k * STEP + STEP)
        grad = gx0()[r, :] + nn(coef_of(par, x0()[r, :], iid[ids], text, t_lane), text)
        g_image.buf[r, :] = nt(project_u(grad, u0()[r, :]), head()[...]).astype(BF16)
        g_image.send(k)
    (image, i_lane), tid = joined(x_low, x_high, scratch[1]), column(lane_ids(t_own()))
    for k, r in enumerate(HALVES):
        ids = slice(k * STEP, k * STEP + STEP)
        grad = gy0()[r, :] + nn(coef_of(par, y0()[r, :], tid[ids], image, i_lane), image)
        t = text_in()[r, :].astype(F32)
        inv = inverse_norm(t)
        g_text.buf[r, :] = project(inv, grad, t * inv).astype(BF16)
        g_text.send(k)


BLOCK = ((ROWS, D), BF16)
SUMS = ((ROWS, D), F32)
TURNED = ((D, ROWS), BF16)
TRAVEL = ((SENT, D), BF16)


def per_device(image_feats, text_feats, head, image_ids, text_ids, log_scale, bias):
    core = lax.axis_index("c")
    par = jnp.stack([jnp.exp(log_scale[0]), bias[0]])
    ids_of = lambda block: (block, ROWS, 16)
    y0, a0 = run(
        prepare, [TRAVEL, TRAVEL],
        [text_feats, image_feats, text_ids.reshape(1, ROWS), image_ids.reshape(1, ROWS)],
    )
    y1, a1 = shifted(y0, 1), shifted(a0, -1)
    u0, x0, at0, gx, gy = run(first, [SUMS, BLOCK, TURNED, SUMS, SUMS], [a0, head, y0], [par], eager=2)
    y2, a2 = shifted(after(y1, gx), 1), shifted(after(a1, gx), -1)
    own_y = (y0, 0, ROWS)
    starts = jnp.stack([512 * (1 - core), 512 * core])
    piece = ((D, WIDE), F32)
    u1, x1, at1, gx, gy, near, away, mine = run(
        second, [SUMS, BLOCK, TURNED, SUMS, SUMS, SUMS, piece, piece],
        [a1, head, y1, x0, own_y, ids_of(a0), ids_of(y0), gx, gy, u0, at0],
        [par, starts], [BLOCK], eager=2,
    )
    y3, a3 = shifted(after(y2, gx), 1), shifted(after(a2, gx), -1)
    part = ((D // 2, WIDE), BF16)
    x2, low, high, mine = run(
        third, [BLOCK, part, part, ((D, WIDE), BF16)],
        [a2, head, y2, x1, ids_of(a1), near, u1, at1, away, mine],
        [par, starts], [SUMS, TURNED, BLOCK, BLOCK], eager=2,
    )
    got = [lax.ppermute(half, "c", [(0, 1), (1, 0)]) for half in (low, high)]
    (pieces,) = run(to_pieces, [((16, 144, PART), BF16)], [mine], direct=got, vmem=16)
    spread = lax.all_to_all(pieces, ("y", "xl", "xh"), 0, 0)
    low, high = ((LOW + 16, D), BF16), ((ROWS - LOW, D), BF16)
    x_low, x_high, y_low, y_high, gy, gx = run(
        fourth, [low, high, low, high, SUMS, SUMS],
        [a3, head, own_y, ids_of(y0), x2, ids_of(a2), gy, y2, x0, ids_of(a0),
         after(gx, pieces), y3],
        [par], [BLOCK], flops=10**11, eager=2,
    )
    y_low, x_low = shifted(after(y_low, spread), 1), shifted(after(x_low, spread), -1)
    (total,) = run(add_pieces, [((8, 18, PART), BF16)], [], direct=[after(spread, gx)], vmem=16)
    spread = lax.all_to_all(total, "z", 0, 0)
    y_high, x_high = shifted(after(y_high, total), 1), shifted(after(x_high, total), -1)
    (total,) = run(
        add_last, [((18, PART), F32)], [], direct=[after(spread, y_low, x_low)], flops=10**11,
        vmem=16,
    )
    swap = [(0, 1), (1, 0)]
    other = lax.ppermute(total, "xh", swap)
    grad_image, grad_text = run(
        last, [BLOCK, BLOCK],
        [y_low, x0, ids_of(a0), gx, u0, head, x_low, own_y, ids_of(y0), after(gy, total),
         text_feats],
        [par], [BLOCK, BLOCK], flops=10**11, eager=4, direct=[y_high, x_high], vmem=36,
    )
    other = after(other, grad_text)
    even = lax.axis_index("xh") == 0
    left, right = jnp.where(even, total, other), jnp.where(even, other, total)
    wide = jnp.concatenate([left, right[:, 128:]], axis=1)
    other = lax.ppermute(wide, "c", swap)
    left, right = jnp.where(core == 0, wide, other), jnp.where(core == 0, other, wide)
    grad_head = jnp.concatenate([left, right[:, 128:]], axis=1)
    return grad_image, grad_text, grad_head


def solution(mesh):
    fine = Mesh(mesh.devices.reshape(4, 2, 8, 2, 2), AXES)
    placed = (P(AXES, None), P(AXES, None), P(), P(AXES), P(AXES), P(), P())
    return jax.shard_map(
        per_device,
        mesh=fine,
        in_specs=placed,
        out_specs=(P(AXES, None), P(AXES, None), P(CYCLE, None)),
        check_vma=False,
    )
```

```python
import jax
import jax.numpy as jnp
from jax import lax
from jax.experimental import pallas as pl
from jax.experimental.pallas import tpu as pltpu
from jax.sharding import Mesh, PartitionSpec as P

AXES = ("y", "xl", "z", "xh", "c")
CYCLE = ("y", "xl", "z")
F32 = jnp.float32
BF16 = jnp.bfloat16
D = 1152
ROWS = 512
SENT = 528
STEP = 256
LOW = 384
WIDE = 640
PART = 384


def shifted(value, steps):
    count = lax.axis_size(CYCLE)
    return lax.ppermute(value, CYCLE, [(i, (i + steps) % count) for i in range(count)])


def after(value, *others):
    return lax.optimization_barrier((value,) + others)[0]


def nn(a, b):
    return jnp.dot(a, b, preferred_element_type=F32)


def nt(a, b):
    return lax.dot_general(a, b, (((1,), (1,)), ((), ())), preferred_element_type=F32)


class Load:
    def __init__(self, copy, buf):
        self.copy, self.buf, self.here, self.then = copy, buf, False, []

    def __call__(self):
        if not self.here:
            self.copy.wait()
            self.here = True
            for copy in self.then:
                copy.start()
        return self.buf


class Store:
    def __init__(self, out, buf, sems):
        self.out, self.buf, self.sems, self.sent = out, buf, sems, []

    def send(self, half=None):
        if self.out is self.buf:
            return
        if half is None:
            copy = pltpu.make_async_copy(self.buf, self.out, self.sems.at[0])
        else:
            size = self.buf.shape[0] // 2
            rows = pl.ds(half * size, size)
            copy = pltpu.make_async_copy(self.buf.at[rows], self.out.at[rows], self.sems.at[half])
        copy.start()
        self.sent.append(copy)


def run(body, outs, ins, scalars=(), scratch=(), flops=0, vmem=56, direct=(), eager=99, kept=()):
    ins = [i if isinstance(i, tuple) else (i, None, None) for i in ins]
    n_d, n_i, n_o = len(direct), len(ins), len(outs)
    n_s = len(scalars) + n_d

    def kernel(*refs):
        pars, refs = refs[:n_s], refs[n_s:]
        sources, refs = refs[:n_i], refs[n_i:]
        results, refs = refs[:n_o], refs[n_o:]
        in_bufs, refs = refs[:n_i], refs[n_i:]
        out_bufs, refs = list(refs[: n_o - len(kept)]), refs[n_o - len(kept) :]
        for k in sorted(kept):
            out_bufs.insert(k, results[k])
        in_sems, out_sems, extra = refs[0], refs[1], refs[2:]
        loads = []
        for k, (_, first, rows) in enumerate(ins):
            source = sources[k] if first is None else sources[k].at[pl.ds(first, rows)]
            copy = pltpu.make_async_copy(source, in_bufs[k], in_sems.at[k])
            loads.append(Load(copy, in_bufs[k]))
            if k < eager:
                copy.start()
            else:
                loads[eager - 1].then.append(copy)
        stores = [Store(results[k], out_bufs[k], out_sems.at[k]) for k in range(n_o)]
        body(pars, loads, stores, extra)
        for load in loads:
            load()
        for store in stores:
            for copy in store.sent:
                copy.wait()

    shapes = []
    for array, _, rows in ins:
        shape = array.shape if rows is None else (rows,) + array.shape[1:]
        shapes.append(pltpu.VMEM(shape, array.dtype))
    shapes += [pltpu.VMEM(s, t) for k, (s, t) in enumerate(outs) if k not in kept]
    shapes += [pltpu.SemaphoreType.DMA((max(n_i, 1),)), pltpu.SemaphoreType.DMA((n_o, 2))]
    shapes += [pltpu.VMEM(s, t) for s, t in scratch]
    return pl.pallas_call(
        kernel,
        out_shape=[jax.ShapeDtypeStruct(s, t) for s, t in outs],
        in_specs=[pl.BlockSpec(memory_space=pltpu.SMEM)] * len(scalars)
        + [pl.BlockSpec(memory_space=pltpu.VMEM)] * n_d
        + [pl.BlockSpec(memory_space=pl.ANY)] * n_i,
        out_specs=[
            pl.BlockSpec(memory_space=pltpu.VMEM if k in kept else pl.ANY) for k in range(n_o)
        ],
        scratch_shapes=shapes,
        compiler_params=pltpu.CompilerParams(vmem_limit_bytes=vmem * 2**20),
        cost_estimate=pl.CostEstimate(flops=flops, bytes_accessed=0, transcendentals=0),
    )(*scalars, *direct, *[i[0] for i in ins])


HALVES = [pl.ds(i * STEP, STEP) for i in range(ROWS // STEP)]


def inverse_norm(values):
    return lax.rsqrt(jnp.sum(values * values, axis=-1, keepdims=True) + 1e-06)


def lane_ids(pair):
    pair = pair[:, pl.ds(0, ROWS)].astype(F32)
    return pair[0:1] * 256.0 + pair[1:2]


def carried(block):
    return lane_ids(block.at[pl.ds(ROWS, 16)])


def column(lane):
    return jnp.broadcast_to(lane, (8, ROWS)).T[:, 0:1]


def coef_of(par, rows, row_ids, columns, column_ids):
    scale, offset = par[0], par[1]
    logits = scale * nt(rows, columns) + offset
    positive = (row_ids == column_ids).astype(F32)
    return (scale * (jax.nn.sigmoid(logits) - positive)).astype(BF16)


def unit_images(feats, head, half, u_out=None):
    for r in HALVES:
        u = nn(feats[r, :], head[...])
        half[r, :] = (u * inverse_norm(u)).astype(BF16)
        if u_out is not None:
            u_out[r, :] = u


def turn(feats, out):
    for k in range(D // 128):
        cols = pl.ds(k * 128, 128)
        out[cols, :] = feats[pl.ds(0, ROWS), cols].T


def project(inv, grad, x):
    return inv * (grad - x * jnp.sum(x * grad, axis=1, keepdims=True))


def project_u(grad, u):
    inv = inverse_norm(u)
    return project(inv, grad, u * inv).astype(BF16)


def prepare(_, loads, stores, __):
    text, image, text_lane, image_lane = loads
    text_out, image_out = stores
    image()
    text()
    for r in HALVES:
        image_out.buf[r, :] = image()[r, :]
    for load, out in ((image_lane, image_out), (text_lane, text_out)):
        if out is text_out:
            for r in HALVES:
                t = text()[r, :].astype(F32)
                out.buf[r, :] = (t * inverse_norm(t)).astype(BF16)
        out.buf[pl.ds(ROWS, 16), :] = jnp.zeros((16, D), BF16)
        row = lax.broadcasted_iota(jnp.int32, (16, ROWS), 0)
        ids = load()[...]
        high, low = (ids >> 8).astype(F32), (ids & 255).astype(F32)
        pair = jnp.where(row == 0, high, jnp.where(row == 1, low, 0.0))
        out.buf[pl.ds(ROWS, 16), pl.ds(0, ROWS)] = pair.astype(BF16)
        out.send()


def first(pars, loads, stores, _):
    (par,) = pars
    a0, head, y0 = loads
    u_out, half, a_t, gx, gy = stores
    unit_images(a0(), head(), half.buf, u_out.buf)
    u_out.send()
    half.send()
    t_lane, i_lane = carried(y0()), carried(a0())
    iid, tid = column(i_lane), column(t_lane)
    text, x = y0()[pl.ds(0, ROWS), :], half.buf
    for k, r in enumerate(HALVES):
        ids = slice(k * STEP, k * STEP + STEP)
        gx.buf[r, :] = nn(coef_of(par, x[r, :], iid[ids], text, t_lane), text)
        gy.buf[r, :] = nn(coef_of(par, y0()[r, :], tid[ids], x[...], i_lane), x[...])
        gx.send(k)
        gy.send(k)
    turn(a0(), a_t.buf)
    a_t.send()


def second(pars, loads, stores, scratch):
    par, starts = pars
    a1, head, y1, x0, y0, i_own, t_own, gx0, gy0, u0, at0 = loads
    u_out, half, a_t, gx, gy, near, away, mine = stores
    (g0,) = scratch
    unit_images(a1(), head(), half.buf, u_out.buf)
    u_out.send()
    half.send()
    tiles(par, y1, a1, half.buf, x0, y0, i_own, t_own, gx0, gy0, gx, gy)
    t_lane, ids1 = carried(y1()), column(carried(a1()))
    text = y1()[pl.ds(0, ROWS), :]
    u0()
    for k, r in enumerate(HALVES):
        ids = slice(k * STEP, k * STEP + STEP)
        near.buf[r, :] = nn(coef_of(par, half.buf[r, :], ids1[ids], text, t_lane), text)
        near.send(k)
        g0[r, :] = project_u(gx.buf[r, :], u0()[r, :])
    turn(a1(), a_t.buf)
    a_t.send()
    at0()
    for start, store in ((starts[0], away), (starts[1], mine)):
        cols = pl.ds(pl.multiple_of(start, 128), WIDE)
        for k in range(2):

            @pl.loop(2 * k, 2 * k + 2)
            def _(j):
                r = pl.ds(pl.multiple_of(j * 288, 288), 288)
                store.buf[r, :] = nn(at0()[r, :], g0[:, cols])

            store.send(k)


def tiles(par, y, a, x, x0, y0, i_own, t_own, gx0, gy0, gx, gy):
    t_lane, i_lane = carried(y()), carried(a())
    iid, tid = column(lane_ids(i_own())), column(lane_ids(t_own()))
    text = y()[pl.ds(0, ROWS), :]
    x0(), y0(), gx0(), gy0()
    for k, r in enumerate(HALVES):
        ids = slice(k * STEP, k * STEP + STEP)
        gx.buf[r, :] = gx0()[r, :] + nn(coef_of(par, x0()[r, :], iid[ids], text, t_lane), text)
        gy.buf[r, :] = gy0()[r, :] + nn(coef_of(par, y0()[r, :], tid[ids], x[...], i_lane), x[...])
        gx.send(k)
        gy.send(k)


def third(pars, loads, stores, scratch):
    par, starts = pars
    a2, head, y2, x1, i_near, near, u1, at1, away0, mine0 = loads
    half, low, high, mine = stores
    u2, at2, g1, g2 = scratch
    unit_images(a2(), head(), half.buf, u2)
    half.send()
    t_lane = carried(y2())
    ids1 = column(lane_ids(i_near()))
    ids2 = column(carried(a2()))
    text = y2()[pl.ds(0, ROWS), :]
    x1(), u1(), near()
    for k, r in enumerate(HALVES):
        ids = slice(k * STEP, k * STEP + STEP)
        grad = nn(coef_of(par, x1()[r, :], ids1[ids], text, t_lane), text)
        g1[r, :] = project_u(grad + near()[r, :], u1()[r, :])
        grad = nn(coef_of(par, half.buf[r, :], ids2[ids], text, t_lane), text)
        g2[r, :] = project_u(grad, u2[r, :])
    turn(a2(), at2)
    at1(), away0(), mine0()

    def summed(start, before, r):
        cols = pl.ds(pl.multiple_of(start, 128), WIDE)
        total = before()[r, :] + nn(at1()[r, :], g1[:, cols])
        return total + nn(at2[r, :], g2[:, cols])

    for i, store in enumerate((low, high)):

        @pl.loop(0, 2)
        def _(k):
            at = pl.multiple_of(k * 288, 288)
            rows = summed(starts[0], away0, pl.ds(at + 576 * i, 288))
            store.buf[pl.ds(at, 288), :] = rows.astype(BF16)

        store.send()
    for k in range(2):

        @pl.loop(2 * k, 2 * k + 2)
        def _(j):
            r = pl.ds(pl.multiple_of(j * 288, 288), 288)
            mine.buf[r, :] = summed(starts[1], mine0, r).astype(BF16)

        mine.send(k)


def to_pieces(direct, _, stores, __):
    mine, low, high = direct
    out = stores[0].buf
    for k in range(8):
        other = (low, high)[k // 4]
        s = pl.ds(144 * (k % 4), 144)
        total = mine[pl.ds(144 * k, 144), :].astype(F32) + other[s, :].astype(F32)
        total = total.astype(BF16)
        out[2 * k] = total[:, :PART]
        out[2 * k + 1] = total[:, 256 : 256 + PART]
        if k % 4 == 3:
            stores[0].send(k // 4)


def add_pieces(direct, _, stores, __):
    got, out = direct[0], stores[0].buf
    total = got[0].astype(F32)
    for k in range(1, 16):
        total = total + got[k].astype(F32)
    for k in range(8):
        out[k] = total[18 * k : 18 * k + 18].astype(BF16)
    stores[0].send()


def add_last(direct, _, stores, __):
    got = direct[0]
    total = got[0].astype(F32)
    for k in range(1, 8):
        total = total + got[k].astype(F32)
    stores[0].buf[...] = total * (1.0 / 256.0)
    stores[0].send()


def split(rows, tail, low, high):
    low.buf[pl.ds(0, LOW), :] = rows[pl.ds(0, LOW), :]
    low.buf[pl.ds(LOW, 16), :] = tail[pl.ds(ROWS, 16), :]
    low.send()
    high.buf[...] = rows[pl.ds(LOW, ROWS - LOW), :]
    high.send()


def fourth(pars, loads, stores, scratch):
    (par,) = pars
    a3, head, y0, t_own, x2, i_far, gy0, y2, x0, i_own, gx0, y3 = loads
    x_low, x_high, y_low, y_high, gy, gx = stores
    (x3,) = scratch
    unit_images(a3(), head(), x3)
    split(x3, a3(), x_low, x_high)
    i_lane, far, tid = carried(a3()), lane_ids(i_far()), column(lane_ids(t_own()))
    y0(), x2(), gy0()
    near = x3[...]
    for k, r in enumerate(HALVES):
        ids = slice(k * STEP, k * STEP + STEP)
        total = gy0()[r, :] + nn(coef_of(par, y0()[r, :], tid[ids], x2()[...], far), x2()[...])
        total = total + nn(coef_of(par, y0()[r, :], tid[ids], near, i_lane), near)
        gy.buf[r, :] = total
        gy.send(k)
    split(y3(), y3(), y_low, y_high)
    texts = [(y()[pl.ds(0, ROWS), :], carried(y())) for y in (y2, y3)]
    iid = column(lane_ids(i_own()))
    x0(), gx0()
    for k, r in enumerate(HALVES):
        ids = slice(k * STEP, k * STEP + STEP)
        total = gx0()[r, :]
        for text, lane in texts:
            total = total + nn(coef_of(par, x0()[r, :], iid[ids], text, lane), text)
        gx.buf[r, :] = total
        gx.send(k)


def last(pars, loads, stores, scratch):
    par, y_high, x_high = pars
    y_low, x0, i_own, gx0, u0, head, x_low, y0, t_own, gy0, text_in = loads
    g_image, g_text = stores

    def joined(low, high, out):
        out[pl.ds(0, LOW), :] = low()[pl.ds(0, LOW), :]
        out[pl.ds(LOW, ROWS - LOW), :] = high[...]
        return out[...], lane_ids(low().at[pl.ds(LOW, 16)])

    x0()
    (text, t_lane), iid = joined(y_low, y_high, scratch[0]), column(lane_ids(i_own()))
    for k, r in enumerate(HALVES):
        ids = slice(k * STEP, k * STEP + STEP)
        grad = gx0()[r, :] + nn(coef_of(par, x0()[r, :], iid[ids], text, t_lane), text)
        g_image.buf[r, :] = nt(project_u(grad, u0()[r, :]), head()[...]).astype(BF16)
        g_image.send(k)
    (image, i_lane), tid = joined(x_low, x_high, scratch[1]), column(lane_ids(t_own()))
    for k, r in enumerate(HALVES):
        ids = slice(k * STEP, k * STEP + STEP)
        grad = gy0()[r, :] + nn(coef_of(par, y0()[r, :], tid[ids], image, i_lane), image)
        t = text_in()[r, :].astype(F32)
        inv = inverse_norm(t)
        g_text.buf[r, :] = project(inv, grad, t * inv).astype(BF16)
        g_text.send(k)


BLOCK = ((ROWS, D), BF16)
SUMS = ((ROWS, D), F32)
TURNED = ((D, ROWS), BF16)
TRAVEL = ((SENT, D), BF16)


def per_device(image_feats, text_feats, head, image_ids, text_ids, log_scale, bias):
    core = lax.axis_index("c")
    par = jnp.stack([jnp.exp(log_scale[0]), bias[0]])
    ids_of = lambda block: (block, ROWS, 16)
    y0, a0 = run(
        prepare, [TRAVEL, TRAVEL],
        [text_feats, image_feats, text_ids.reshape(1, ROWS), image_ids.reshape(1, ROWS)],
    )
    y1, a1 = shifted(y0, 1), shifted(a0, -1)
    u0, x0, at0, gx, gy = run(first, [SUMS, BLOCK, TURNED, SUMS, SUMS], [a0, head, y0], [par], eager=2)
    y2, a2 = shifted(after(y1, gx), 1), shifted(after(a1, gx), -1)
    own_y = (y0, 0, ROWS)
    starts = jnp.stack([512 * (1 - core), 512 * core])
    piece = ((D, WIDE), F32)
    u1, x1, at1, gx, gy, near, away, mine = run(
        second, [SUMS, BLOCK, TURNED, SUMS, SUMS, SUMS, piece, piece],
        [a1, head, y1, x0, own_y, ids_of(a0), ids_of(y0), gx, gy, u0, at0],
        [par, starts], [BLOCK], eager=2,
    )
    y3, a3 = shifted(after(y2, gx), 1), shifted(after(a2, gx), -1)
    part = ((D // 2, WIDE), BF16)
    x2, low, high, mine = run(
        third, [BLOCK, part, part, ((D, WIDE), BF16)],
        [a2, head, y2, x1, ids_of(a1), near, u1, at1, away, mine],
        [par, starts], [SUMS, TURNED, BLOCK, BLOCK], eager=2,
    )
    got = [lax.ppermute(half, "c", [(0, 1), (1, 0)]) for half in (low, high)]
    (pieces,) = run(
        to_pieces, [((16, 144, PART), BF16)], [], direct=[mine, *got], vmem=16, kept=(0,)
    )
    spread = lax.all_to_all(pieces, ("y", "xl", "xh"), 0, 0)
    low, high = ((LOW + 16, D), BF16), ((ROWS - LOW, D), BF16)
    x_low, x_high, y_low, y_high, gy, gx = run(
        fourth, [low, high, low, high, SUMS, SUMS],
        [a3, head, own_y, ids_of(y0), x2, ids_of(a2), gy, y2, x0, ids_of(a0),
         after(gx, pieces), y3],
        [par], [BLOCK], flops=10**11, eager=2,
    )
    y_low, x_low = shifted(after(y_low, spread), 1), shifted(after(x_low, spread), -1)
    (total,) = run(add_pieces, [((8, 18, PART), BF16)], [], direct=[after(spread, gx)], vmem=16)
    spread = lax.all_to_all(total, "z", 0, 0)
    y_high, x_high = shifted(after(y_high, total), 1), shifted(after(x_high, total), -1)
    (total,) = run(
        add_last, [((18, PART), F32)], [], direct=[after(spread, y_low, x_low)], flops=10**11,
        vmem=16,
    )
    swap = [(0, 1), (1, 0)]
    other = lax.ppermute(total, "xh", swap)
    grad_image, grad_text = run(
        last, [BLOCK, BLOCK],
        [y_low, x0, ids_of(a0), gx, u0, head, x_low, own_y, ids_of(y0), after(gy, total),
         text_feats],
        [par], [BLOCK, BLOCK], flops=10**11, eager=4, direct=[y_high, x_high], vmem=36,
    )
    other = after(other, grad_text)
    even = lax.axis_index("xh") == 0
    left, right = jnp.where(even, total, other), jnp.where(even, other, total)
    wide = jnp.concatenate([left, right[:, 128:]], axis=1)
    other = lax.ppermute(wide, "c", swap)
    left, right = jnp.where(core == 0, wide, other), jnp.where(core == 0, other, wide)
    grad_head = jnp.concatenate([left, right[:, 128:]], axis=1)
    return grad_image, grad_text, grad_head


def solution(mesh):
    fine = Mesh(mesh.devices.reshape(4, 2, 8, 2, 2), AXES)
    placed = (P(AXES, None), P(AXES, None), P(), P(AXES), P(AXES), P(), P())
    return jax.shard_map(
        per_device,
        mesh=fine,
        in_specs=placed,
        out_specs=(P(AXES, None), P(AXES, None), P(CYCLE, None)),
        check_vma=False,
    )
```
